256 devices in a mesh: seq: 32 (over y, x, core), tp: 8 (over z).
Axes of the slice: x: 4, y: 4, z: 8, core: 2. Of those that a mesh axis runs over, the one named last changes fastest.
Arguments:
- patches: bfloat16 [1024, 16, 1280], P('seq'), may hold values from -6 to 6
- vit_qkv: bfloat16 [3, 1280, 1280], P(None, 'seq', 'tp'), may hold values from -0.15625 to 0.15625
- vit_out: bfloat16 [1280, 1280], P('tp', 'seq'), may hold values from -0.15625 to 0.15625
- merge_weight: bfloat16 [5120, 8192], P(None, 'tp'), may hold values from -0.078125 to 0.078125
- query_key_value_weight: bfloat16 [8192, 8, 10, 128], P('seq', 'tp'), may hold values from -0.0625 to 0.0625
- adapter_down: bfloat16 [8192, 128], P('tp'), may hold values from -0.0625 to 0.0625
- adapter_up_weight: bfloat16 [128, 8, 10, 128], P(None, 'tp'), may hold values from -1.5 to 1.5
- text_embed: bfloat16 [8192, 8192], P('seq', 'tp'), may hold values from -6 to 6
- vis_count: int32 [1024], replicated, may hold values from 1 to 4, as said below
- image_session: int32 [1024], replicated, may hold values from 0 to 63, as said below
- session_slot: int32 [64], replicated, may hold values from 0 to 63, as said below
- session_tenant: int32 [64], replicated, may hold values from 0 to 7
- session_len: int32 [64], replicated, may hold values from 1 to 128, as said below
Outputs:
- attended: float32 [8192, 8192], P('seq', 'tp')
The draws below stay inside these ranges and needn't reach their ends.
Inputs may be any that keep to these rules, and one draw needn't show every extreme that they name: `vis_count`: some image has exactly 4 merged rows. `image_session`: every session owns exactly 16 images; of the 32 images encoded by one index of seq, exactly 1 belong to the sessions of each shard. A permutation: session s lies in slot session_slot[s], on shard session_slot[s] // 2. `session_len`: each session has more rows than visual rows; some session fills its slot.
All inputs are finite; a program needn't handle non-finite values.
Results may differ from the reference program's by a relative error of at most 0.024.
Values may be sent and summed in bfloat16 or wider, within the bound.
A program may use at most 128 MiB of HBM per device.

```python
import math
import jax
import jax.numpy as jnp
from jax import lax

DV = 1280
HV = 16
DECODER_WIDTH = 8192
HQ = 64
KEY_VALUE_HEADS = 8
DECODER_HEAD_DIM = 128
ADAPTER_RANK = 16
TENANT_COUNT = 8
IMG_DEV = 32
VMAX = 4
SESS_DEV = 2
TOK_DEV = 256
VMIN = 1
DM = 5120
QUERY_PER_KEY = 8
PATCH = 16
SLOT = 128
IMG_SESS = 16
PER_DEST = 1
IMAGES = 1024
SESSIONS = 64
TOKENS = 8192
N_SEQ = 32


def session_layout(key):
    sub_keys = jax.random.split(key, 7)
    image_idx = jnp.arange(IMAGES, dtype=jnp.int32)
    counts = jax.random.randint(sub_keys[0], (IMAGES,), VMIN, VMAX + 1)
    counts = jnp.where(image_idx == 0, VMAX, counts).astype(jnp.int32)
    relabel = jax.random.permutation(sub_keys[2], N_SEQ)
    spread = jax.random.permutation(sub_keys[3], N_SEQ)
    encoder = image_idx // IMG_DEV
    local_idx = image_idx % IMG_DEV
    dest_shard = relabel[(spread[encoder] + local_idx) % N_SEQ]
    arrival = encoder * PER_DEST + local_idx // N_SEQ
    orders = jax.vmap(lambda sub_key: jax.random.permutation(sub_key, IMG_DEV))(jax.random.split(sub_keys[4], N_SEQ))
    place_idx = orders[dest_shard, arrival]
    dest_slot = dest_shard * SESS_DEV + place_idx // IMG_SESS
    session_slot = jax.random.permutation(sub_keys[5], SESSIONS).astype(jnp.int32)
    slot_owner = jnp.argsort(session_slot).astype(jnp.int32)
    image_session = slot_owner[dest_slot].astype(jnp.int32)
    owner_match = image_session[None, :] == jnp.arange(SESSIONS, dtype=jnp.int32)[:, None]
    vis_total = jnp.sum(jnp.where(owner_match, counts[None, :], 0), axis=1)
    extra_len = jax.random.randint(sub_keys[6], (SESSIONS,), 0, SLOT - vis_total)
    lengths = jnp.where(session_slot == 0, SLOT, vis_total + 1 + extra_len).astype(jnp.int32)
    return (counts, image_session, session_slot, lengths)


def draw_vis_count(key, part):
    return session_layout(key)[0]


def draw_image_session(key, part):
    return session_layout(key)[1]


def draw_session_slot(key, part):
    return session_layout(key)[2]


def draw_session_len(key, part):
    return session_layout(key)[3]


def touch_ends(array, own_key, least, high):
    index_at = [jax.random.randint(jax.random.fold_in(own_key, axis), (), 0, length) for axis, length in enumerate(array.shape)]
    widest = array.shape.index(max(array.shape))
    beside = index_at[:widest] + [(index_at[widest] + 1) % array.shape[widest]] + index_at[widest + 1:]
    return array.at[tuple(index_at)].set(least).at[tuple(beside)].set(high)


def block_scale(key, dims, shards, least, high):
    def one(dim, blocks):
        heights = jax.random.uniform(jax.random.fold_in(jax.random.fold_in(key, 6), dim), (blocks,), jnp.float32, least / len(shards), high / len(shards))
        return jnp.repeat(jnp.exp(heights), dims[dim] // blocks).reshape((-1,) + (1,) * (len(dims) - dim - 1))

    factor_of = one(*shards[0])
    for cut in shards[1:]:
        factor_of = factor_of * one(*cut)
    return factor_of


def normal_values(key, dims, deviation, reach, cuts=(), kind=jnp.bfloat16):
    values = jax.random.normal(key, dims, jnp.float32) * deviation
    if len(cuts) > 0:
        values = block_scale(key, dims, cuts, -0.22, 0.18) * values
    return jnp.clip(values, min=-reach, max=reach).astype(kind)


def setup_inputs(seed: int = 0) -> dict:
    splits = jax.random.split(jax.random.key(seed), 14)
    return {
        "patches": normal_values(splits[0], (IMAGES, PATCH, DV), 1.0, 6.0, ((0, 32),)),
        "vit_qkv": normal_values(splits[1], (3, DV, DV), DV ** -0.5, 0.15625, ((1, 32), (2, 8))),
        "vit_out": normal_values(splits[2], (DV, DV), DV ** -0.5, 0.15625, ((0, 8), (1, 32))),
        "merge_weight": normal_values(splits[3], (DM, DECODER_WIDTH), DM ** -0.5, 0.078125, ((1, 8),)),
        "query_key_value_weight": normal_values(splits[4], (DECODER_WIDTH, KEY_VALUE_HEADS, QUERY_PER_KEY + 2, DECODER_HEAD_DIM), DECODER_WIDTH ** -0.5, 0.0625, ((0, 32), (1, 8))),
        "adapter_down": normal_values(splits[5], (DECODER_WIDTH, TENANT_COUNT * ADAPTER_RANK), DECODER_WIDTH ** -0.5, 0.0625, ((0, 8),)),
        "adapter_up_weight": normal_values(splits[6], (TENANT_COUNT * ADAPTER_RANK, KEY_VALUE_HEADS, QUERY_PER_KEY + 2, DECODER_HEAD_DIM), ADAPTER_RANK ** -0.5, 1.5, ((1, 8),)),
        "text_embed": normal_values(splits[7], (TOKENS, DECODER_WIDTH), 1.0, 6.0, ((0, 32), (1, 8))),
        "vis_count": draw_vis_count(jax.random.fold_in(splits[13], 71), 0),
        "image_session": draw_image_session(jax.random.fold_in(splits[13], 71), 0),
        "session_slot": draw_session_slot(jax.random.fold_in(splits[13], 71), 0),
        "session_tenant": touch_ends(jax.random.randint(splits[11], (SESSIONS,), 0, TENANT_COUNT), jax.random.fold_in(splits[11], 1), 0, TENANT_COUNT - 1).astype(jnp.int32),
        "session_len": draw_session_len(jax.random.fold_in(splits[13], 71), 0),
    }


EPSILON = 1e-06
ROPE_BASE = 1000000.0

def layer_norm(values):
    mean_val = lax.optimization_barrier(jnp.mean(values, axis=-1, keepdims=True))
    centered = values - mean_val
    variance = lax.optimization_barrier(jnp.mean(centered * centered, axis=-1, keepdims=True))
    return centered * lax.rsqrt(variance + EPSILON)

def softmax_rows(scores):
    largest = lax.optimization_barrier(jnp.max(scores, axis=-1, keepdims=True))
    exponent = jnp.exp(scores - largest)
    return exponent / lax.optimization_barrier(jnp.sum(exponent, axis=-1, keepdims=True))

def rotate(values, pos_float):
    half_dim = values.shape[-1] // 2
    inverse_freq = ROPE_BASE ** (-(jnp.arange(half_dim, dtype=jnp.float32) * 2.0 / values.shape[-1]))
    angles = pos_float[:, None] * inverse_freq[None, :]
    new_shape = (values.shape[0],) + (1,) * (values.ndim - 2) + (half_dim,)
    cosine = jnp.cos(angles).reshape(new_shape)
    sine_part = jnp.sin(angles).reshape(new_shape)
    first_half = values[..., :half_dim]
    second = values[..., half_dim:]
    return jnp.concatenate([first_half * cosine - second * sine_part, second * cosine + first_half * sine_part], axis=-1)

def encode_block(block_args, vit_qkv, vit_out, merge_weight):
    images, counts = block_args
    num_img = images.shape[0]
    num_patch = images.shape[1]
    head_dim = DV // HV
    raw_vals = images.astype(jnp.float32)
    normalized_rows = layer_norm(raw_vals).astype(jnp.bfloat16)
    projected_rows = jnp.einsum('ipd,jdc->jipc', normalized_rows.astype(jnp.float32), vit_qkv.astype(jnp.float32)).astype(jnp.bfloat16)
    queries = projected_rows[0].reshape(num_img, num_patch, HV, head_dim).astype(jnp.float32)
    key_rows = projected_rows[1].reshape(num_img, num_patch, HV, head_dim).astype(jnp.float32)
    value_rows = projected_rows[2].reshape(num_img, num_patch, HV, head_dim).astype(jnp.float32)
    scores = jnp.einsum('iphd,ikhd->ihpk', queries, key_rows) / math.sqrt(head_dim)
    valid = jnp.arange(num_patch, dtype=jnp.int32)[None, :] < 4 * counts[:, None]
    scores = jnp.where(valid[:, None, None, :], scores, -1e+30)
    attn_probs = softmax_rows(scores).astype(jnp.bfloat16)
    context = jnp.einsum('ihpk,ikhd->iphd', attn_probs.astype(jnp.float32), value_rows).astype(jnp.bfloat16)
    context = context.reshape(num_img * num_patch, DV)
    encoded = raw_vals + jnp.dot(context, vit_out, preferred_element_type=jnp.float32).reshape(num_img, num_patch, DV)
    merged_in = layer_norm(encoded).reshape(num_img * (num_patch // 4), 4 * DV).astype(jnp.bfloat16)
    merged = jnp.dot(merged_in, merge_weight, preferred_element_type=jnp.float32).astype(jnp.bfloat16)
    return merged.reshape(num_img, num_patch // 4, merge_weight.shape[1])

def row_layout(shard_id, vis_count, image_session, session_slot, session_len, session_tenant, image_base):
    num_images = vis_count.shape[0]
    num_sessions = session_slot.shape[0]
    image_idx = jnp.arange(num_images, dtype=jnp.int32)
    session_idx = jnp.arange(num_sessions, dtype=jnp.int32)
    same_session = image_session[:, None] == image_session[None, :]
    earlier = image_idx[None, :] < image_idx[:, None]
    offset = lax.optimization_barrier(jnp.sum(jnp.where(same_session & earlier, vis_count[None, :], 0), axis=1))
    owner_match = image_session[None, :] == session_idx[:, None]
    image_slot = lax.optimization_barrier(jnp.sum(jnp.where(owner_match, session_slot[:, None], 0), axis=0))
    row_ids = jnp.arange(TOK_DEV, dtype=jnp.int32)
    position = row_ids % SLOT
    row_slot = shard_id * SESS_DEV + row_ids // SLOT
    slot_match = session_slot[None, :] == row_slot[:, None]
    row_len = lax.optimization_barrier(jnp.sum(jnp.where(slot_match, session_len[None, :], 0), axis=1))
    tenant_of_row = lax.optimization_barrier(jnp.sum(jnp.where(slot_match, session_tenant[None, :], 0), axis=1))
    member = (image_slot[None, :] == row_slot[:, None]) & (offset[None, :] <= position[:, None]) & (position[:, None] < offset[None, :] + vis_count[None, :])
    source = lax.optimization_barrier(jnp.sum(jnp.where(member, image_base[None, :] + position[:, None] - offset[None, :], 0), axis=1)).astype(jnp.int32)
    is_visual = jnp.any(member, axis=1)
    return (position, row_len, tenant_of_row, is_visual, source)

def decode_rows(tokens, sum_squares, down_projection_sums, flattened_qkv_weight, flattened_up_weight, position, row_len, tenant_of_row):
    num_rows = tokens.shape[0]
    root_mean_square = jnp.sqrt(sum_squares / DECODER_WIDTH + EPSILON)
    normalized_rows = (tokens.astype(jnp.float32) / root_mean_square[:, None]).astype(jnp.bfloat16)
    adapter_column_view = jnp.arange(down_projection_sums.shape[1], dtype=jnp.int32) // ADAPTER_RANK
    adapter_input_rows = jnp.where(adapter_column_view[None, :] == tenant_of_row[:, None], down_projection_sums / root_mean_square[:, None], 0.0).astype(jnp.bfloat16)
    projected_rows = jnp.dot(normalized_rows, flattened_qkv_weight, preferred_element_type=jnp.float32) + jnp.dot(adapter_input_rows, flattened_up_weight, preferred_element_type=jnp.float32)
    groups = projected_rows.shape[1] // ((QUERY_PER_KEY + 2) * DECODER_HEAD_DIM)
    projected_rows = projected_rows.reshape(num_rows, groups, QUERY_PER_KEY + 2, DECODER_HEAD_DIM)
    pos_float = position.astype(jnp.float32)
    queries = rotate(projected_rows[:, :, :QUERY_PER_KEY], pos_float).astype(jnp.bfloat16)
    key_rows = rotate(projected_rows[:, :, QUERY_PER_KEY], pos_float).astype(jnp.bfloat16)
    value_rows = projected_rows[:, :, QUERY_PER_KEY + 1].astype(jnp.bfloat16)
    queries = queries.reshape(SESS_DEV, SLOT, groups, QUERY_PER_KEY, DECODER_HEAD_DIM).astype(jnp.float32)
    key_rows = key_rows.reshape(SESS_DEV, SLOT, groups, DECODER_HEAD_DIM).astype(jnp.float32)
    value_rows = value_rows.reshape(SESS_DEV, SLOT, groups, DECODER_HEAD_DIM).astype(jnp.float32)
    scores = jnp.einsum('sqgjd,skgd->sgjqk', queries, key_rows) / math.sqrt(DECODER_HEAD_DIM)
    slot_pos = jnp.arange(SLOT, dtype=jnp.int32)
    causal = slot_pos[None, :] <= slot_pos[:, None]
    scores = jnp.where(causal, scores, -1e+30)
    attn_probs = softmax_rows(scores).astype(jnp.bfloat16)
    result = jnp.einsum('sgjqk,skgd->sqgjd', attn_probs.astype(jnp.float32), value_rows)
    result = result.reshape(num_rows, groups * QUERY_PER_KEY * DECODER_HEAD_DIM)
    return jnp.where((position < row_len)[:, None], result, 0.0).astype(jnp.float32)

def reference(patches, vit_qkv, vit_out, merge_weight, query_key_value_weight, adapter_down, adapter_up_weight, text_embed, vis_count, image_session, session_slot, session_tenant, session_len):
    visual = lax.map(lambda block_args: encode_block(block_args, vit_qkv, vit_out, merge_weight), (patches.reshape(N_SEQ, IMG_DEV, PATCH, DV), vis_count.reshape(N_SEQ, IMG_DEV)))
    flat_rows = visual.reshape(IMAGES * VMAX, DECODER_WIDTH)
    flattened_qkv_weight = query_key_value_weight.reshape(DECODER_WIDTH, KEY_VALUE_HEADS * (QUERY_PER_KEY + 2) * DECODER_HEAD_DIM)
    flattened_up_weight = adapter_up_weight.reshape(TENANT_COUNT * ADAPTER_RANK, KEY_VALUE_HEADS * (QUERY_PER_KEY + 2) * DECODER_HEAD_DIM)
    image_base = jnp.arange(IMAGES, dtype=jnp.int32) * VMAX

    def per_shard(shard_id):
        position, row_len, tenant_of_row, is_visual, source = row_layout(shard_id, vis_count, image_session, session_slot, session_len, session_tenant, image_base)
        text_rows = lax.dynamic_slice_in_dim(text_embed, (shard_id * TOK_DEV).astype(jnp.int32), TOK_DEV, 0)
        visual_rows = jnp.take(flat_rows, source, axis=0)
        tokens = jnp.where(is_visual[:, None], visual_rows, jnp.where((position < row_len)[:, None], text_rows, jnp.zeros_like(text_rows)))
        raw_vals = tokens.astype(jnp.float32)
        sum_squares = lax.optimization_barrier(jnp.sum(raw_vals * raw_vals, axis=1))
        down_projection_sums = jnp.dot(tokens, adapter_down, preferred_element_type=jnp.float32)
        return decode_rows(tokens, sum_squares, down_projection_sums, flattened_qkv_weight, flattened_up_weight, position, row_len, tenant_of_row)
    result = lax.map(per_shard, jnp.arange(N_SEQ, dtype=jnp.int32))
    return result.reshape(TOKENS, HQ * DECODER_HEAD_DIM)
```

```python
import functools
import math

import jax
import jax.numpy as jnp
import numpy as np
from jax import lax
from jax.experimental import pallas as pl
from jax.experimental.pallas import tpu as pltpu
from jax.sharding import PartitionSpec as P

DV = 1280
HV = 16
HEAD = 80
DECODER_WIDTH = 8192
DECODER_HEAD_DIM = 128
ADAPTER_RANK = 16
IMG_DEV = 32
VMAX = 4
SLOT = 128
QUERY_PER_KEY = 8
N_SEQ = 32
N_TP = 8
COLS = 1280
EPSILON = 1e-06
ROPE_BASE = 1000000.0
MESH = pl.DeviceIdType.MESH
F32 = jnp.float32
BF16 = jnp.bfloat16


def tables():
    perm = np.zeros((512, 512), np.float32)
    for j in range(4):
        for i in range(32):
            for m in range(4):
                perm[j * 128 + i * 4 + m, i * 16 + m * 4 + j] = 1
    select = np.zeros((640, 768), np.float32)
    for group in range(6):
        for lane in range(HEAD):
            select[group * HEAD + lane, group * 128 + lane] = 1
    select_out = np.zeros((160, 640), np.float32)
    for row in range(160):
        select_out[row, 480 + row] = 1
    half = DECODER_HEAD_DIM // 2
    inverse_freq = np.power(
        np.float32(ROPE_BASE), -(np.arange(half, dtype=np.float32) * 2.0 / DECODER_HEAD_DIM)
    ).astype(np.float32)
    angles = np.arange(SLOT, dtype=np.float32)[:, None] * inverse_freq[None, :]
    cosine = np.cos(angles).astype(np.float32)
    sine = np.sin(angles).astype(np.float32)
    return (
        jnp.asarray(perm, BF16),
        jnp.asarray(select, BF16),
        jnp.asarray(select_out, BF16),
        jnp.asarray(np.concatenate([cosine, cosine], 1)),
        jnp.asarray(np.concatenate([-sine, sine], 1)),
    )


def weight_copies():
    whole, first, second = (0, 256), (0, 128), (128, 128)

    def sib(blocks):
        return [(by, bx, 0, 256, 0, 0, True) for by, bx in blocks]

    def go(by, bx, part, ty, tx):
        return (by, bx, part[0], part[1], ty, tx, False)

    stage0 = [go(0, 0, whole, 0, 1), go(0, 0, whole, 0, -1), go(0, 0, whole, 1, 0), go(0, 0, whole, -1, 0)]
    stage0 += sib([(0, 0)])
    stage1 = [
        go(0, -1, first, 0, 1), go(0, 1, second, 0, -1), go(-1, 0, first, 1, 0), go(1, 0, second, -1, 0),
    ]
    for side in (-1, 1):
        for to in (-1, 1):
            stage1 += [go(0, side, first, to, 0), go(side, 0, second, 0, to)]
    stage1 += sib([(0, -1), (0, 1), (-1, 0), (1, 0)])
    stage2 = [
        go(0, 2, first, 1, 0), go(0, 2, first, -1, 0), go(2, 0, second, 0, 1), go(2, 0, second, 0, -1),
        go(-1, 1, first, 1, 0), go(1, -1, first, -1, 0), go(1, -1, second, 0, 1), go(-1, 1, second, 0, -1),
    ]
    stage2 += sib([(0, 2), (2, 0), (-1, -1), (-1, 1), (1, -1), (1, 1)])
    stage3 = [
        go(-1, 2, (0, 64), 1, 0), go(1, 2, (64, 64), -1, 0), go(2, -1, (128, 64), 0, 1), go(2, 1, (192, 64), 0, -1),
    ]
    stage3 += sib([(-1, 2), (1, 2), (2, -1), (2, 1)])
    stage4 = sib([(2, 2)])
    stages, count = [], 0
    for stage in (stage0, stage1, stage2, stage3, stage4):
        stages.append([(count + i,) + entry for i, entry in enumerate(stage)])
        count += len(stage)
    return stages, count


STAGES, W_COPIES = weight_copies()


def bdot(a, b):
    return jnp.dot(a, b, preferred_element_type=F32)


def bdot_nt(a, b):
    return lax.dot_general(a, b, (((1,), (1,)), ((), ())), preferred_element_type=F32)


def normalize(values):
    mean_val = jnp.mean(values, axis=-1, keepdims=True)
    centered = values - mean_val
    variance = jnp.mean(centered * centered, axis=-1, keepdims=True)
    return centered * lax.rsqrt(variance + EPSILON)


def kernel(
    patches, vit, mw, w, down, up, text, tgt, key, bias, tmask, keep, tenant_mask,
    perm, select, select_out, cosine, sine,
    out,
    g, wf, wall, pp, ln, qkv, o_all, ctx_all, enc, mwb, vis, xs, ys, tok, dl, w_all, acc,
    loc_sem, mw_sem, gs_sem, gr_sem, fs_sem, fr_sem, ws_sem, wr_sem,
    os_sem, or_sem, ofs_sem, ofr_sem, cs_sem, cr_sem, es_sem, er_sem, ls_sem, lr_sem,
    as_sem, ar_sem, ds_sem, dr_sem,
):
    s = lax.axis_index("seq")
    t = lax.axis_index("tp")
    core = lax.rem(s, 2)
    chip = s // 2
    cx = lax.rem(chip, 4)
    cy = chip // 4
    sibling = s + 1 - 2 * core

    def chip_at(dy, dx):
        return lax.rem(cy + (dy + 4), 4) * 4 + lax.rem(cx + (dx + 4), 4)

    def rows(ref, start, size, step=16):
        return ref.at[pl.ds(pl.multiple_of(start, step), size)]

    def arrived(ref, sem):
        pltpu.make_async_copy(ref, ref, sem).wait()

    barrier = pltpu.get_barrier_semaphore()

    def greet_seq(i, carry):
        pl.semaphore_signal(barrier, inc=1, device_id=(lax.rem(s + i, N_SEQ), t), device_id_type=MESH)
        return carry

    def greet_tp(i, carry):
        pl.semaphore_signal(barrier, inc=1, device_id=(s, lax.rem(t + i, N_TP)), device_id_type=MESH)
        return carry

    lax.fori_loop(1, N_SEQ, greet_seq, 0)
    lax.fori_loop(1, N_TP, greet_tp, 0)
    pl.semaphore_wait(barrier, N_SEQ + N_TP - 2)

    def g_row(c, chip_id):
        return (c * 16 + chip_id) * 48

    own_g = pltpu.make_async_copy(vit, rows(g, g_row(core, chip), 48), loc_sem.at[0])
    own_g.start()
    for dy in range(4):
        for dx in range(4):
            if dy == 0 and dx == 0:
                continue
            pltpu.make_async_remote_copy(
                src_ref=vit,
                dst_ref=rows(g, g_row(core, chip), 48),
                send_sem=gs_sem.at[0],
                recv_sem=gr_sem.at[(4 - dy) % 4],
                device_id=(chip_at(dy, dx) * 2 + core, t),
                device_id_type=MESH,
            ).start()

    own_w = pltpu.make_async_copy(w, rows(w_all, s * 256, 256), loc_sem.at[1])
    own_w.start()
    mw_loads = [
        pltpu.make_async_copy(mw.at[pl.ds(1280 * j, 1280)], mwb.at[j % 2], mw_sem.at[j]) for j in range(4)
    ]
    mw_loads[0].start()
    mw_loads[1].start()

    def w_ref(by, bx, first, size):
        return rows(w_all, (chip_at(by, bx) * 2 + core) * 256 + first, size)

    def w_start(stage):
        for index, by, bx, first, size, ty, tx, sib in STAGES[stage]:
            source = w if stage == 0 else w_ref(by, bx, first, size)
            pltpu.make_async_remote_copy(
                src_ref=source,
                dst_ref=w_ref(by, bx, first, size),
                send_sem=ws_sem.at[index],
                recv_sem=wr_sem.at[index],
                device_id=(sibling if sib else chip_at(ty, tx) * 2 + core, t),
                device_id_type=MESH,
            ).start()

    def w_arrived(stage):
        for index, by, bx, first, size, ty, tx, sib in STAGES[stage]:
            if not sib:
                arrived(w_ref(by - ty, bx - tx, first, size), wr_sem.at[index])

    def w_rest():
        for stage in STAGES:
            for index, by, bx, first, size, ty, tx, sib in stage:
                if sib:
                    arrived(rows(w_all, (chip_at(by, bx) * 2 + 1 - core) * 256, 256), wr_sem.at[index])

    def w_sent():
        for stage in STAGES:
            for index, by, bx, first, size, ty, tx, sib in stage:
                arrived(w_ref(by, bx, first, size), ws_sem.at[index])

    right = (s, lax.rem(t + 1, N_TP))
    left = (s, lax.rem(t + N_TP - 1, N_TP))

    def ring(buf, base, size, cut, send, recv):
        def part(way, origin, k):
            first = base(lax.rem(origin + 2 * N_TP, N_TP))
            if k < 3:
                return rows(buf, first, size)
            if way == 0:
                return rows(buf, first, cut)
            return rows(buf, first + cut, size - cut)

        def start(k):
            for way, to, origin in ((0, right, t - k), (1, left, t + k)):
                piece = part(way, origin, k)
                pltpu.make_async_remote_copy(
                    src_ref=piece, dst_ref=piece, send_sem=send.at[way * 4 + k], recv_sem=recv.at[way * 4 + k],
                    device_id=to, device_id_type=MESH,
                ).start()

        def wait(k):
            arrived(part(0, t - 1 - k, k), recv.at[k])
            arrived(part(1, t + 1 + k, k), recv.at[4 + k])

        def sent():
            for k in range(4):
                arrived(part(0, t - k, k), send.at[k])
                arrived(part(1, t + k, k), send.at[4 + k])

        return start, wait, sent

    e_start, e_wait, e_sent = ring(tok, lambda z: z * 256 + 128, 128, 64, es_sem, er_sem)
    l_start, l_wait, l_sent = ring(tok, lambda z: z * 256, 128, 64, ls_sem, lr_sem)
    o_start, o_wait, o_sent = ring(o_all, lambda z: z * 160 + 80 * core, 80, 48, os_sem, or_sem)
    c_start, c_wait, c_sent = ring(ctx_all, lambda z: z * 160, 160, 80, cs_sem, cr_sem)

    def o_share(k):
        origins = [(0, t - 1 - k), (1, t + 1 + k)] if k < 3 else [(0, t + 4)]
        for way, origin in origins:
            first = lax.rem(origin + 2 * N_TP, N_TP) * 160 + 80 * core
            piece = rows(o_all, first, 80)
            pltpu.make_async_remote_copy(
                src_ref=piece, dst_ref=piece, send_sem=ofs_sem.at[way * 4 + k], recv_sem=ofr_sem.at[way * 4 + k],
                device_id=(sibling, t), device_id_type=MESH,
            ).start()

    def o_shared(sems, c):
        for k in range(4):
            origins = [(0, t - 1 - k), (1, t + 1 + k)] if k < 3 else [(0, t + 4)]
            for way, origin in origins:
                first = lax.rem(origin + 2 * N_TP, N_TP) * 160 + 80 * c
                arrived(rows(o_all, first, 80), sems.at[way * 4 + k])

    own_tok = pl.multiple_of(t * 256, 256)
    for l in range(2):
        tok[pl.ds(own_tok + 128 + 64 * l, 64), :] = jnp.where(
            tmask[128 + 64 * l:192 + 64 * l, :] > 0, text[128 * l + 64:128 * l + 128, :], jnp.zeros((64, 1024), BF16)
        )
    e_start(0)

    for n in range(5):
        lanes = slice(256 * n, 256 * n + 256)
        pp[:, lanes] = bdot(perm[...], patches[:, lanes]).astype(BF16)
    for r in range(4):
        part = slice(128 * r, 128 * r + 128)
        ln[part, :] = normalize(pp[part, :].astype(F32)).astype(BF16)

    own_g.wait()
    arrived(g.at[pl.ds(0, 144)], gr_sem.at[0])
    for d in range(4):
        group = rows(g, g_row(core, lax.rem(cy + d, 4) * 4), 192)
        if d > 0:
            arrived(group, gr_sem.at[d])
        pltpu.make_async_remote_copy(
            src_ref=group, dst_ref=group, send_sem=fs_sem.at[d], recv_sem=fr_sem.at[d],
            device_id=(sibling, t), device_id_type=MESH,
        ).start()
    own_w.wait()
    w_start(0)
    for d in range(4):
        arrived(rows(g, g_row(1 - core, lax.rem(cy + d, 4) * 4), 192), fr_sem.at[d])
    e_wait(0)
    e_start(1)

    for b in range(32):
        first = g_row(b % 2, b // 2)
        wf[40 * b:40 * b + 40, :] = g[first:first + 48, :].astype(F32)[:40, :]
    for r in range(5):
        part = slice(256 * r, 256 * r + 256)
        wall[part, :] = wf[part, :].astype(BF16)
    own_o = pl.multiple_of(t * 160, 32)
    for r in range(5):
        part = slice(256 * r, 256 * r + 256)
        o_all[pl.ds(own_o, 160), part] = bdot_nt(select_out[...], wall[part, :]).astype(BF16)
    o_start(0)

    for n in range(5):
        lanes = slice(128 * n, 128 * n + 128)
        qkv[:, lanes] = bdot(ln[...], wall[:, lanes]).astype(BF16)
    scale = 1.0 / math.sqrt(HEAD)
    for h in range(2):
        q_h = bdot(qkv[...], select[:, 128 * h:128 * h + 128]).astype(BF16)
        k_h = bdot(qkv[...], select[:, 256 + 128 * h:384 + 128 * h]).astype(BF16)
        v_h = bdot(qkv[...], select[:, 512 + 128 * h:640 + 128 * h])
        v_t = jnp.transpose(v_h).astype(BF16)
        for q in range(4):
            scores = bdot_nt(k_h, q_h[128 * q:128 * q + 128, :]) * scale
            scores = scores.reshape(4, 128, 128) + bias[...][None]
            largest = jnp.max(jnp.max(scores, axis=0), axis=0, keepdims=True)
            exponent = jnp.exp(scores - largest[None])
            total = jnp.sum(jnp.sum(exponent, axis=0), axis=0, keepdims=True)
            probs = (exponent / total[None]).astype(BF16).reshape(512, 128)
            ctx_t = bdot(v_t, probs).astype(BF16)
            ctx_all[pl.ds(own_o + 80 * h, 80), 128 * q:128 * q + 128] = ctx_t[:80, :]
    c_start(0)

    o_wait(0)
    o_start(1)
    o_share(0)
    c_wait(0)
    c_start(1)
    w_arrived(0)
    w_start(1)
    o_wait(1)
    o_start(2)
    o_share(1)
    c_wait(1)
    c_start(2)
    o_wait(2)
    o_start(3)
    o_share(2)
    c_wait(2)
    c_start(3)
    e_wait(1)
    e_start(2)
    o_wait(3)
    o_share(3)
    c_wait(3)
    o_shared(ofr_sem, 1 - core)

    for r in range(4):
        part = slice(128 * r, 128 * r + 128)
        ln[part, :] = jnp.transpose(ctx_all[:, part].astype(F32)).astype(BF16)
    for n in range(5):
        lanes = slice(256 * n, 256 * n + 256)
        enc[:, lanes] = pp[:, lanes].astype(F32) + bdot(ln[...], o_all[:, lanes])
    for j in range(4):
        part = slice(128 * j, 128 * j + 128)
        merged_in = normalize(enc[part, :]).astype(BF16)
        mw_loads[j].wait()
        if j == 0:
            vis[...] = bdot(merged_in, mwb[j % 2])
        else:
            vis[...] += bdot(merged_in, mwb[j % 2])
        if j < 2:
            mw_loads[j + 2].start()

    row_512 = lax.broadcasted_iota(jnp.int32, (512, 128), 0)
    outgoing = jnp.zeros((512, 256), F32)
    for q in range(4):
        place = (row_512 == tgt[q:q + 1, :]).astype(F32).astype(BF16)
        outgoing += bdot(place, vis[:, 256 * q:256 * q + 256].astype(BF16))
    xs[...] = outgoing.astype(BF16)

    def send_rows(i, carry):
        to = lax.rem(s + i, N_SEQ)
        pltpu.make_async_remote_copy(
            src_ref=rows(xs, to * 16, 16), dst_ref=rows(ys, s * 16, 16),
            send_sem=as_sem.at[0], recv_sem=ar_sem.at[0], device_id=(to, t), device_id_type=MESH,
        ).start()
        return carry

    lax.fori_loop(1, N_SEQ, send_rows, 0)
    own_y = pl.ds(pl.multiple_of(s * 16, 16), 16)
    ys[own_y, :] = xs[own_y, :]
    w_arrived(1)
    w_start(2)
    e_wait(2)
    e_start(3)
    arrived(ys.at[pl.ds(0, 496)], ar_sem.at[0])

    row_128 = lax.broadcasted_iota(jnp.int32, (128, 512), 0)
    for q in range(4):
        lanes = slice(256 * q, 256 * q + 256)
        place = (row_128 == key[q:q + 1, :]).astype(F32).astype(BF16)
        picked = bdot(place, ys[...]).astype(BF16)
        for l in range(2):
            half = slice(64 * l, 64 * l + 64)
            tok[pl.ds(own_tok + 64 * l, 64), lanes] = jnp.where(
                tmask[half, :] > 0, text[128 * l:128 * l + 64, lanes], picked[half, :]
            )
    l_start(0)

    down_sums = jnp.transpose(bdot(tok[pl.ds(own_tok, 256), :], down[...])) * tenant_mask[...]
    dl[pl.ds(pl.multiple_of(t * 16, 16), 16), :] = jnp.sum(down_sums.reshape(8, 16, 256), axis=0)

    def send_down(i, carry):
        piece = rows(dl, t * 16, 16)
        pltpu.make_async_remote_copy(
            src_ref=piece, dst_ref=piece, send_sem=ds_sem.at[0], recv_sem=dr_sem.at[0],
            device_id=(s, lax.rem(t + i, N_TP)), device_id_type=MESH,
        ).start()
        return carry

    lax.fori_loop(1, N_TP, send_down, 0)

    w_arrived(2)
    w_start(3)
    l_wait(0)
    l_start(1)
    e_wait(3)
    w_arrived(3)
    w_start(4)
    l_wait(1)
    l_start(2)
    w_rest()

    def project(z):
        x = tok[pl.ds(pl.multiple_of(z * 256, 256), 256), :]
        first = pl.multiple_of(z * 1024, 1024)
        for n in range(5):
            lanes = slice(256 * n, 256 * n + 256)
            acc[:, lanes] += bdot(x, w_all[pl.ds(first, 1024), lanes])
        x_wide = x.astype(F32)
        return jnp.sum(x_wide * x_wide, axis=1, keepdims=True)

    acc[...] = jnp.zeros_like(acc)
    squares = project(t)
    squares += project(lax.rem(t + 1, N_TP))
    squares += project(lax.rem(t + 7, N_TP))
    l_wait(2)
    l_start(3)
    for k in (2, 6, 3, 5):
        squares += project(lax.rem(t + k, N_TP))
    arrived(dl.at[pl.ds(0, 112)], dr_sem.at[0])
    down_t = jnp.sum(dl[...].reshape(8, 16, 256), axis=0)
    lora = jnp.transpose(jnp.concatenate([down_t] * 8, axis=0) * tenant_mask[...]).astype(BF16)
    acc[...] += bdot(lora, up[...])
    l_wait(3)
    squares += project(lax.rem(t + 4, N_TP))
    inverse = lax.rsqrt(squares * (1.0 / DECODER_WIDTH) + EPSILON)

    causal = lax.broadcasted_iota(jnp.int32, (128, 128), 0) >= lax.broadcasted_iota(jnp.int32, (128, 128), 1)
    for l in range(2):
        low, high = slice(64 * l, 64 * l + 64), slice(128 + 64 * l, 192 + 64 * l)
        factor = jnp.concatenate([inverse[low, :], inverse[high, :]], axis=0)

        def column(index):
            lanes = slice(128 * index, 128 * index + 128)
            return jnp.concatenate([acc[low, lanes], acc[high, lanes]], axis=0) * factor

        def rotate(values):
            return values * cosine[...] + pltpu.roll(values, 64, 1) * sine[...]

        key_rows = rotate(column(8)).astype(BF16)
        value_rows = column(9).astype(BF16)
        kept = keep[128 * l:128 * l + 128, :] > 0
        for j in range(QUERY_PER_KEY):
            query = rotate(column(j)).astype(BF16)
            scores = bdot_nt(query, key_rows) * (1.0 / math.sqrt(DECODER_HEAD_DIM))
            scores = jnp.where(causal, scores, -1e30)
            exponent = jnp.exp(scores - jnp.max(scores, axis=1, keepdims=True))
            probs = (exponent / jnp.sum(exponent, axis=1, keepdims=True)).astype(BF16)
            out[128 * l:128 * l + 128, 128 * j:128 * j + 128] = jnp.where(kept, bdot(probs, value_rows), 0.0)

    arrived(g.at[pl.ds(0, 720)], gs_sem.at[0])
    for d in range(4):
        arrived(rows(g, g_row(core, lax.rem(cy + d, 4) * 4), 192), fs_sem.at[d])
    w_sent()
    e_sent()
    l_sent()
    o_sent()
    c_sent()
    o_shared(ofs_sem, core)
    arrived(xs.at[pl.ds(0, 496)], as_sem.at[0])
    arrived(dl.at[pl.ds(0, 112)], ds_sem.at[0])


def layout(shard_id, vis_count, image_session, session_slot, session_len, session_tenant):
    owner = image_session[None, :] == jnp.arange(session_slot.shape[0], dtype=jnp.int32)[:, None]
    image_slot = jnp.sum(jnp.where(owner, session_slot[:, None], 0), axis=0).reshape(N_SEQ, IMG_DEV)
    counts = vis_count.reshape(N_SEQ, IMG_DEV)
    here_dest = lax.dynamic_slice_in_dim(image_slot, shard_id, 1, 0)[0] // 2
    here_count = lax.dynamic_slice_in_dim(counts, shard_id, 1, 0)[0]
    quarter = jnp.arange(8, dtype=jnp.int32)
    merged = jnp.arange(128, dtype=jnp.int32)
    tgt = jnp.repeat(here_dest, VMAX)[None, :] * 16 + quarter[:, None] * 4 + (merged % 4)[None, :]
    same_image = (merged[:, None] // 4 == merged[None, :] // 4) & (
        (merged % 4) < jnp.repeat(here_count, VMAX)
    )[:, None]
    bias = jnp.where(same_image, 0.0, -1e30).astype(F32)
    mine = image_slot // 2 == shard_id
    count = jnp.sum(jnp.where(mine, counts, 0), axis=1)
    place = jnp.sum(jnp.where(mine, image_slot % 2, 0), axis=1)
    encoder = jnp.arange(N_SEQ, dtype=jnp.int32)
    before = (place[:, None] == place[None, :]) & (encoder[None, :] < encoder[:, None])
    offset = jnp.sum(jnp.where(before, count[None, :], 0), axis=1)
    column = jnp.arange(512, dtype=jnp.int32)
    valid = ((column // 4) % 4)[None, :] == quarter[:, None]
    valid = valid & (column % 4 < jnp.repeat(count, 16))[None, :]
    key = jnp.where(valid, (jnp.repeat(place * 64 + offset, 16) + column % 4)[None, :], -1)
    two = jnp.arange(2, dtype=jnp.int32)
    total = jnp.sum(jnp.where(place[None, :] == two[:, None], count[None, :], 0), axis=1)
    match = session_slot[None, :] == (shard_id * 2 + two)[:, None]
    length = jnp.sum(jnp.where(match, session_len[None, :], 0), axis=1)
    tenant = jnp.sum(jnp.where(match, session_tenant[None, :], 0), axis=1)
    row = jnp.arange(256, dtype=jnp.int32)
    row_place = (row // 64) % 2
    row_pos = row % 64 + 64 * (row // 128)

    def of(pair, index):
        return jnp.where(index == 0, pair[0], pair[1])

    tmask = (row_pos >= of(total, row_place)) & (row_pos < of(length, row_place))
    keep = (row % 128) < of(length, row // 128)
    tenant_mask = (jnp.arange(128, dtype=jnp.int32) // ADAPTER_RANK)[:, None] == of(tenant, row_place)[None, :]
    return (
        tgt, key, bias, tmask.astype(F32)[:, None], keep.astype(F32)[:, None], tenant_mask.astype(F32)
    )


def on_device(
    patches, vit_qkv, vit_out, merge_weight, query_key_value_weight, adapter_down, adapter_up_weight,
    text_embed, vis_count, image_session, session_slot, session_tenant, session_len,
):
    shard_id = lax.axis_index("seq")
    vit = jnp.concatenate([vit_qkv[0], vit_qkv[1], vit_qkv[2], vit_out.T], axis=1)
    vit = jnp.pad(vit, ((0, 8), (0, 0)))
    maps = layout(shard_id, vis_count, image_session, session_slot, session_len, session_tenant)
    operands = (
        patches.reshape(512, DV), vit, merge_weight, query_key_value_weight.reshape(256, COLS),
        adapter_down, adapter_up_weight.reshape(128, COLS), text_embed,
    ) + maps + tables()
    vmem = pl.BlockSpec(memory_space=pltpu.VMEM)
    hbm = pl.BlockSpec(memory_space=pl.ANY)
    dma = pltpu.SemaphoreType.DMA
    return pl.pallas_call(
        kernel,
        out_shape=jax.ShapeDtypeStruct((256, 1024), F32),
        in_specs=[hbm if i in (2, 3) else vmem for i in range(len(operands))],
        out_specs=vmem,
        scratch_shapes=[
            pltpu.VMEM((1536, 640), BF16),
            pltpu.VMEM((1280, 640), F32),
            pltpu.VMEM((1280, 640), BF16),
            pltpu.VMEM((512, 1280), BF16),
            pltpu.VMEM((512, 1280), BF16),
            pltpu.VMEM((512, 640), BF16),
            pltpu.VMEM((1280, 1280), BF16),
            pltpu.VMEM((1280, 512), BF16),
            pltpu.VMEM((512, 1280), F32),
            pltpu.VMEM((2, 1280, 1024), BF16),
            pltpu.VMEM((128, 1024), F32),
            pltpu.VMEM((512, 256), BF16),
            pltpu.VMEM((512, 256), BF16),
            pltpu.VMEM((2048, 1024), BF16),
            pltpu.VMEM((128, 256), F32),
            pltpu.VMEM((8192, 1280), BF16),
            pltpu.VMEM((256, 1280), F32),
            dma((2,)), dma((4,)), dma((1,)), dma((4,)), dma((4,)), dma((4,)), dma((W_COPIES,)), dma((W_COPIES,)),
            dma((8,)), dma((8,)), dma((8,)), dma((8,)), dma((8,)), dma((8,)), dma((8,)), dma((8,)), dma((8,)), dma((8,)),
            dma((1,)), dma((1,)), dma((1,)), dma((1,)),
        ],
        compiler_params=pltpu.CompilerParams(
            collective_id=0, has_side_effects=True, vmem_limit_bytes=63 * 1024 * 1024
        ),
    )(*operands)


def solution(mesh):
    placed = (
        P("seq", None, None),
        P(None, "seq", "tp"),
        P("tp", "seq"),
        P(None, "tp"),
        P("seq", "tp", None, None),
        P("tp", None),
        P(None, "tp", None, None),
        P("seq", "tp"),
        P(),
        P(),
        P(),
        P(),
        P(),
    )
    return jax.shard_map(
        on_device, mesh=mesh, in_specs=placed, out_specs=P("seq", "tp"), check_vma=False
    )
```

```python
import functools
import math

import jax
import jax.numpy as jnp
import numpy as np
from jax import lax
from jax.experimental import pallas as pl
from jax.experimental.pallas import tpu as pltpu
from jax.sharding import PartitionSpec as P

DV = 1280
HV = 16
HEAD = 80
DECODER_WIDTH = 8192
DECODER_HEAD_DIM = 128
ADAPTER_RANK = 16
IMG_DEV = 32
VMAX = 4
SLOT = 128
QUERY_PER_KEY = 8
N_SEQ = 32
N_TP = 8
COLS = 1280
EPSILON = 1e-06
ROPE_BASE = 1000000.0
MESH = pl.DeviceIdType.MESH
F32 = jnp.float32
BF16 = jnp.bfloat16


def tables():
    perm = np.zeros((512, 512), np.float32)
    for j in range(4):
        for i in range(32):
            for m in range(4):
                perm[j * 128 + i * 4 + m, i * 16 + m * 4 + j] = 1
    select = np.zeros((512, 768), np.float32)
    for group in range(6):
        for lane in range(HEAD):
            select[group * HEAD + lane, group * 128 + lane] = 1
    select_out = np.zeros((160, 640), np.float32)
    for row in range(160):
        select_out[row, 480 + row] = 1
    half = DECODER_HEAD_DIM // 2
    inverse_freq = np.power(
        np.float32(ROPE_BASE), -(np.arange(half, dtype=np.float32) * 2.0 / DECODER_HEAD_DIM)
    ).astype(np.float32)
    angles = np.arange(SLOT, dtype=np.float32)[:, None] * inverse_freq[None, :]
    cosine = np.cos(angles).astype(np.float32)
    sine = np.sin(angles).astype(np.float32)
    return (
        jnp.asarray(perm, BF16),
        jnp.asarray(select, BF16),
        jnp.asarray(select_out, BF16),
        jnp.asarray(np.concatenate([cosine, cosine], 1)),
        jnp.asarray(np.concatenate([-sine, sine], 1)),
    )


def plane_copies(size, cut, opposite):
    whole, first, second = (0, size), (0, cut), (cut, size - cut)

    def sib(blocks):
        return [(by, bx, 0, size, 0, 0, True) for by, bx in blocks]

    def go(by, bx, part, ty, tx):
        return (by, bx, part[0], part[1], ty, tx, False)

    stage0 = [go(0, 0, whole, 0, 1), go(0, 0, whole, 0, -1), go(0, 0, whole, 1, 0), go(0, 0, whole, -1, 0)]
    stage0 += sib([(0, 0)])
    stage1 = [
        go(0, -1, first, 0, 1), go(0, 1, second, 0, -1), go(-1, 0, first, 1, 0), go(1, 0, second, -1, 0),
    ]
    for side in (-1, 1):
        for to in (-1, 1):
            stage1 += [go(0, side, first, to, 0), go(side, 0, second, 0, to)]
    stage1 += sib([(0, -1), (0, 1), (-1, 0), (1, 0)])
    stage2 = [
        go(0, 2, first, 1, 0), go(0, 2, first, -1, 0), go(2, 0, second, 0, 1), go(2, 0, second, 0, -1),
        go(-1, 1, first, 1, 0), go(1, -1, first, -1, 0), go(1, -1, second, 0, 1), go(-1, 1, second, 0, -1),
    ]
    stage2 += sib([(0, 2), (2, 0), (-1, -1), (-1, 1), (1, -1), (1, 1)])
    ways = ((-1, 2, 1, 0), (1, 2, -1, 0), (2, -1, 0, 1), (2, 1, 0, -1))
    stage3 = [go(by, bx, part, ty, tx) for (by, bx, ty, tx), part in zip(ways, opposite) if part is not None]
    stage3 += sib([(-1, 2), (1, 2), (2, -1), (2, 1)])
    stage4 = sib([(2, 2)])
    stages, count = [], 0
    for stage in (stage0, stage1, stage2, stage3, stage4):
        stages.append([(count + i,) + entry for i, entry in enumerate(stage)])
        count += len(stage)
    return stages, count


W_STAGES, W_COPIES = plane_copies(256, 128, ((0, 64), (64, 64), (128, 64), (192, 64)))
G_STAGES, G_COPIES = plane_copies(48, 32, ((0, 16), (16, 16), (32, 16), None))


def bdot(a, b):
    return jnp.dot(a, b, preferred_element_type=F32)


def bdot_nt(a, b):
    return lax.dot_general(a, b, (((1,), (1,)), ((), ())), preferred_element_type=F32)


def normalize(values):
    mean_val = jnp.mean(values, axis=-1, keepdims=True)
    centered = values - mean_val
    variance = jnp.mean(centered * centered, axis=-1, keepdims=True)
    return centered * lax.rsqrt(variance + EPSILON)


def iota(shape, axis):
    return lax.broadcasted_iota(jnp.int32, shape, axis)


def one_hot(mask):
    return mask.astype(F32).astype(BF16)


def kernel(
    slot_ref, tenant_ref, len_ref, counts, sessions,
    patches, vit_qkv, vit_out, mw, w, down, up, text, perm, select, select_out, cosine, sine,
    out,
    g, wf, wall, pp, ln, qkv, o_all, ctx_all, enc, mwb, vis, xs, ys, tok, dl, w_all, up_all, acc,
    mw_sem, gs_sem, gr_sem, ws_sem, wr_sem,
    os_sem, or_sem, ofs_sem, ofr_sem, cs_sem, cr_sem, es_sem, er_sem, ls_sem, lr_sem,
    as_sem, ar_sem, ds_sem, dr_sem,
):
    s = lax.axis_index("seq")
    t = lax.axis_index("tp")
    core = lax.rem(s, 2)
    chip = s // 2
    cx = lax.rem(chip, 4)
    cy = chip // 4
    sibling = s + 1 - 2 * core

    def chip_at(dy, dx):
        return lax.rem(cy + (dy + 4), 4) * 4 + lax.rem(cx + (dx + 4), 4)

    def rows(ref, start, size, step=16):
        return ref.at[pl.ds(pl.multiple_of(start, step), size)]

    def arrived(ref, sem):
        pltpu.make_async_copy(ref, ref, sem).wait()

    barrier = pltpu.get_barrier_semaphore()

    def greet_seq(i, carry):
        pl.semaphore_signal(barrier, inc=1, device_id=(lax.rem(s + i, N_SEQ), t), device_id_type=MESH)
        return carry

    def greet_tp(i, carry):
        pl.semaphore_signal(barrier, inc=1, device_id=(s, lax.rem(t + i, N_TP)), device_id_type=MESH)
        return carry

    lax.fori_loop(1, N_SEQ, greet_seq, 0)
    lax.fori_loop(1, N_TP, greet_tp, 0)

    mw_load = pltpu.make_async_copy(mw, mwb, mw_sem.at[0])
    mw_load.start()

    def plane(stages, ref, send, recv):
        def start(stage):
            for index, by, bx, first, size, ty, tx, sib in stages[stage]:
                piece = ref(core, chip_at(by, bx), first, size)
                pltpu.make_async_remote_copy(
                    src_ref=piece, dst_ref=piece, send_sem=send.at[index], recv_sem=recv.at[index],
                    device_id=(sibling if sib else chip_at(ty, tx) * 2 + core, t), device_id_type=MESH,
                ).start()

        def wait(stage):
            for index, by, bx, first, size, ty, tx, sib in stages[stage]:
                if not sib:
                    arrived(ref(core, chip_at(by - ty, bx - tx), first, size), recv.at[index])

        def rest():
            for stage in stages:
                for index, by, bx, first, size, ty, tx, sib in stage:
                    if sib:
                        arrived(ref(1 - core, chip_at(by, bx), first, size), recv.at[index])

        def sent():
            for stage in stages:
                for index, by, bx, first, size, ty, tx, sib in stage:
                    arrived(ref(core, chip_at(by, bx), first, size), send.at[index])

        return start, wait, rest, sent

    g_start, g_wait, g_rest, g_sent = plane(
        G_STAGES, lambda c, at, first, size: rows(g, (c * 16 + at) * 48 + first, size), gs_sem, gr_sem
    )
    w_start, w_wait, w_rest, w_sent = plane(
        W_STAGES, lambda c, at, first, size: rows(w_all, (at * 2 + c) * 256 + first, size), ws_sem, wr_sem
    )

    right = (s, lax.rem(t + 1, N_TP))
    left = (s, lax.rem(t + N_TP - 1, N_TP))

    def ring(buf, base, size, cut, send, recv):
        def part(way, origin, k):
            first = base(lax.rem(origin + 2 * N_TP, N_TP))
            if k < 3:
                return rows(buf, first, size)
            if way == 0:
                return rows(buf, first, cut)
            return rows(buf, first + cut, size - cut)

        def start(k):
            for way, to, origin in ((0, right, t - k), (1, left, t + k)):
                piece = part(way, origin, k)
                pltpu.make_async_remote_copy(
                    src_ref=piece, dst_ref=piece, send_sem=send.at[way * 4 + k], recv_sem=recv.at[way * 4 + k],
                    device_id=to, device_id_type=MESH,
                ).start()

        def wait(k):
            arrived(part(0, t - 1 - k, k), recv.at[k])
            arrived(part(1, t + 1 + k, k), recv.at[4 + k])

        def sent():
            for k in range(4):
                arrived(part(0, t - k, k), send.at[k])
                arrived(part(1, t + k, k), send.at[4 + k])

        return start, wait, sent

    e_start, e_wait, e_sent = ring(tok, lambda z: z * 256 + 128, 128, 64, es_sem, er_sem)
    l_start, l_wait, l_sent = ring(tok, lambda z: z * 256, 128, 64, ls_sem, lr_sem)
    o_start, o_wait, o_sent = ring(o_all, lambda z: z * 160 + 80 * core, 80, 48, os_sem, or_sem)
    c_start, c_wait, c_sent = ring(ctx_all, lambda z: z * 160, 160, 80, cs_sem, cr_sem)

    def o_pieces(k, c):
        origins = [(0, t - 1 - k), (1, t + 1 + k)] if k < 3 else [(0, t + 4)]
        for way, origin in origins:
            yield way * 4 + k, rows(o_all, lax.rem(origin + 2 * N_TP, N_TP) * 160 + 80 * c, 80)

    def o_share(k):
        for index, piece in o_pieces(k, core):
            pltpu.make_async_remote_copy(
                src_ref=piece, dst_ref=piece, send_sem=ofs_sem.at[index], recv_sem=ofr_sem.at[index],
                device_id=(sibling, t), device_id_type=MESH,
            ).start()

    def o_shared(k, sems, c):
        for index, piece in o_pieces(k, c):
            arrived(piece, sems.at[index])

    r_640, c_640 = iota((160, 640), 0), iota((160, 640), 1)
    mine = jnp.zeros((40, 640), F32)
    for j in range(3):
        mine += bdot(vit_qkv[j], one_hot(c_640 == r_640 + 160 * j))
    mine += lax.dot_general(
        vit_out[...], one_hot(c_640 == r_640 + 480), (((0,), (0,)), ((), ())), preferred_element_type=F32
    )
    own_g = pl.ds(pl.multiple_of((core * 16 + chip) * 48, 16), 48)
    g[own_g, :] = jnp.concatenate([mine, jnp.zeros((8, 640), F32)], axis=0).astype(BF16)

    def look_up(k, carry):
        slots, len0, len1, tenant0, tenant1 = carry
        slot = slot_ref[k]
        slots = jnp.where(sessions[...] == k, slot, slots)
        at0, at1 = slot == 2 * s, slot == 2 * s + 1
        return (
            slots, jnp.where(at0, len_ref[k], len0), jnp.where(at1, len_ref[k], len1),
            jnp.where(at0, tenant_ref[k], tenant0), jnp.where(at1, tenant_ref[k], tenant1),
        )

    zero = jnp.int32(0)
    slots, len0, len1, tenant0, tenant1 = lax.fori_loop(
        0, 64, look_up, (jnp.zeros((8, 128), jnp.int32), zero, zero, zero, zero)
    )
    length = (len0, len1)

    pl.semaphore_wait(barrier, N_SEQ + N_TP - 2)
    g_start(0)

    own_tok = pl.multiple_of(t * 256, 256)
    for l in range(2):
        tok[pl.ds(own_tok + 128 + 64 * l, 64), :] = jnp.where(
            iota((64, 1024), 0) + 64 < length[l], text[128 * l + 64:128 * l + 128, :], jnp.zeros((64, 1024), BF16)
        )
    e_start(0)

    for n in range(5):
        lanes = slice(256 * n, 256 * n + 256)
        pp[:, lanes] = bdot(perm[...], patches[:, lanes]).astype(BF16)

    g_wait(0)
    g_start(1)
    for r in range(4):
        part = slice(128 * r, 128 * r + 128)
        ln[part, :] = normalize(pp[part, :].astype(F32)).astype(BF16)

    here = (slots >> 1) == s
    folded = jnp.concatenate(
        [jnp.where(here, counts[...], 0).astype(F32), jnp.where(here, slots & 1, 0).astype(F32)], axis=0
    ).astype(BF16)
    spread = bdot(folded, one_hot((iota((128, 512), 0) >> 5) == ((iota((128, 512), 1) >> 4) & 3)))
    n_8 = iota((8, 512), 1)
    own_row = iota((8, 512), 0) == (n_8 >> 6)
    count_n = jnp.sum(jnp.where(own_row, spread[:8, :], 0.0), axis=0, keepdims=True)
    place_n = jnp.sum(jnp.where(own_row, spread[8:, :], 0.0), axis=0, keepdims=True)
    by_place = jnp.where(iota((8, 512), 0) == place_n.astype(jnp.int32), count_n, 0.0)
    n_from, n_to = iota((512, 512), 0), iota((512, 512), 1)
    before = bdot(by_place.astype(BF16), one_hot(((n_from & 15) == 0) & ((n_from >> 4) < (n_to >> 4))))
    offset_n = jnp.where(place_n > 0.5, before[1:2, :], before[0:1, :])
    visual_rows = jnp.sum(by_place, axis=1, keepdims=True) * (1.0 / 16.0)
    n_1 = n_8[0:1, :]
    row_n = jnp.where(
        (n_1 & 3).astype(F32) < count_n, place_n * 64.0 + offset_n + (n_1 & 3).astype(F32), -1.0
    ).astype(jnp.int32)

    lane_8 = iota((128, 128), 1)
    encoded_here = bdot(
        jnp.concatenate([slots.astype(F32), counts[...].astype(F32)], axis=0).astype(BF16),
        one_hot(iota((128, 128), 0) == lax.rem(s, 4) * 32 + (lane_8 >> 2)),
    )
    own_row = iota((8, 128), 0) == s // 4
    slot_c = jnp.sum(jnp.where(own_row, encoded_here[:8, :], 0.0), axis=0, keepdims=True).astype(jnp.int32)
    count_c = jnp.sum(jnp.where(own_row, encoded_here[8:, :], 0.0), axis=0, keepdims=True).astype(jnp.int32)
    target_c = (slot_c >> 1) * 16 + (lane_8[0:1, :] & 3)
    key_8 = iota((128, 128), 0)
    bias = jnp.where(((key_8 >> 2) == (lane_8 >> 2)) & ((key_8 & 3) < count_c), 0.0, -1e30)
    tenant_mask = (
        (iota((128, 256), 0) >> 4) == jnp.where((iota((128, 256), 1) & 64) == 0, tenant0, tenant1)
    ).astype(F32)

    g_wait(1)
    g_start(2)
    own_w = pl.ds(pl.multiple_of(s * 256, 256), 256)
    for j in range(10):
        w_all[own_w, 128 * j:128 * j + 128] = w[:, j, :]
    e_wait(0)
    e_start(1)
    g_wait(2)
    g_start(3)
    w_start(0)
    for j in range(10):
        up_all[:, 128 * j:128 * j + 128] = up[:, j, :]
    g_wait(3)
    g_start(4)
    g_rest()

    for c in range(4):
        for b in range(8):
            first = ((b % 2) * 16 + 4 * c + b // 2) * 48
            wf[40 * b:40 * b + 40, :] = g[first:first + 48, :].astype(F32)[:40, :]
        wall[320 * c:320 * c + 320, :] = wf[...].astype(BF16)
    own_o = pl.multiple_of(t * 160, 32)
    for r in range(5):
        part = slice(256 * r, 256 * r + 256)
        o_all[pl.ds(own_o, 160), part] = bdot_nt(select_out[...], wall[part, :]).astype(BF16)
    o_start(0)

    for n in range(2):
        lanes = slice(256 * n, 256 * n + 256)
        qkv[:, lanes] = bdot(ln[...], wall[:, lanes]).astype(BF16)
    scale = 1.0 / math.sqrt(HEAD)
    for h in range(2):
        q_h = bdot(qkv[...], select[:, 128 * h:128 * h + 128]).astype(BF16)
        k_h = bdot(qkv[...], select[:, 256 + 128 * h:384 + 128 * h]).astype(BF16)
        v_h = bdot(qkv[...], select[:, 512 + 128 * h:640 + 128 * h])
        v_t = jnp.transpose(v_h).astype(BF16)
        for q in range(4):
            scores = bdot_nt(k_h, q_h[128 * q:128 * q + 128, :]) * scale
            scores = scores.reshape(4, 128, 128) + bias[None]
            largest = jnp.max(jnp.max(scores, axis=0), axis=0, keepdims=True)
            exponent = jnp.exp(scores - largest[None])
            total = jnp.sum(jnp.sum(exponent, axis=0), axis=0, keepdims=True)
            probs = (exponent / total[None]).astype(BF16).reshape(512, 128)
            ctx_t = bdot(v_t, probs).astype(BF16)
            ctx_all[pl.ds(own_o + 80 * h, 80), 128 * q:128 * q + 128] = ctx_t[:80, :]
    c_start(0)

    def project_out(z, first=False):
        at = pl.ds(pl.multiple_of(lax.rem(z + 2 * N_TP, N_TP) * 160, 32), 160)
        for n in range(5):
            lanes = slice(256 * n, 256 * n + 256)
            term = lax.dot_general(
                ctx_all[at, :], o_all[at, lanes], (((0,), (0,)), ((), ())), preferred_element_type=F32
            )
            enc[:, lanes] = (pp[:, lanes].astype(F32) if first else enc[:, lanes]) + term

    o_wait(0)
    o_start(1)
    o_share(0)
    project_out(t, True)
    c_wait(0)
    c_start(1)
    o_wait(1)
    o_start(2)
    o_share(1)
    w_wait(0)
    w_start(1)
    o_shared(0, ofr_sem, 1 - core)
    project_out(t - 1)
    project_out(t + 1)
    c_wait(1)
    c_start(2)
    o_wait(2)
    o_start(3)
    o_share(2)
    o_shared(1, ofr_sem, 1 - core)
    project_out(t - 2)
    project_out(t + 2)
    c_wait(2)
    c_start(3)
    o_wait(3)
    o_share(3)
    o_shared(2, ofr_sem, 1 - core)
    e_wait(1)
    e_start(2)
    project_out(t - 3)
    project_out(t + 3)
    o_shared(3, ofr_sem, 1 - core)
    mw_load.wait()
    c_wait(3)
    project_out(t + 4)

    merged = jnp.zeros((128, 1024), F32)
    for j in range(4):
        merged_in = normalize(enc[128 * j:128 * j + 128, :]).astype(BF16)
        merged += bdot(merged_in, mwb[1280 * j:1280 * j + 1280, :])
    vis[...] = merged.astype(BF16)

    row_512 = iota((512, 128), 0)
    outgoing = jnp.zeros((512, 256), F32)
    for q in range(4):
        outgoing += bdot(one_hot(row_512 == target_c + 4 * q), vis[:, 256 * q:256 * q + 256])
    xs[...] = outgoing.astype(BF16)

    def send_rows(i, carry):
        to = lax.rem(s + i, N_SEQ)
        pltpu.make_async_remote_copy(
            src_ref=rows(xs, to * 16, 16), dst_ref=rows(ys, s * 16, 16),
            send_sem=as_sem.at[0], recv_sem=ar_sem.at[0], device_id=(to, t), device_id_type=MESH,
        ).start()
        return carry

    lax.fori_loop(1, N_SEQ, send_rows, 0)
    own_y = pl.ds(pl.multiple_of(s * 16, 16), 16)
    ys[own_y, :] = xs[own_y, :]
    w_wait(1)
    w_start(2)
    e_wait(2)
    e_start(3)
    arrived(ys.at[pl.ds(0, 496)], ar_sem.at[0])

    row_128 = iota((128, 512), 0)
    position = iota((64, 256), 0)
    for q in range(4):
        lanes = slice(256 * q, 256 * q + 256)
        picked = bdot(one_hot((row_128 == row_n) & (((n_1 >> 2) & 3) == q)), ys[...]).astype(BF16)
        for l in range(2):
            is_text = (position.astype(F32) >= visual_rows[l:l + 1, :]) & (position < length[l])
            tok[pl.ds(own_tok + 64 * l, 64), lanes] = jnp.where(
                is_text, text[128 * l:128 * l + 64, lanes], picked[64 * l:64 * l + 64, :]
            )
    l_start(0)

    down_sums = jnp.transpose(bdot(tok[pl.ds(own_tok, 256), :], down[...])) * tenant_mask
    dl[pl.ds(pl.multiple_of(t * 16, 16), 16), :] = jnp.sum(down_sums.reshape(8, 16, 256), axis=0)

    def send_down(i, carry):
        piece = rows(dl, t * 16, 16)
        pltpu.make_async_remote_copy(
            src_ref=piece, dst_ref=piece, send_sem=ds_sem.at[0], recv_sem=dr_sem.at[0],
            device_id=(s, lax.rem(t + i, N_TP)), device_id_type=MESH,
        ).start()
        return carry

    lax.fori_loop(1, N_TP, send_down, 0)

    l_wait(0)
    l_start(1)
    w_wait(2)
    w_start(3)
    l_wait(1)
    l_start(2)
    e_wait(3)
    w_wait(3)
    w_start(4)
    w_rest()

    def project(z):
        x = tok[pl.ds(pl.multiple_of(z * 256, 256), 256), :]
        first = pl.multiple_of(z * 1024, 1024)
        for n in range(5):
            lanes = slice(256 * n, 256 * n + 256)
            acc[:, lanes] += bdot(x, w_all[pl.ds(first, 1024), lanes])
        x_wide = x.astype(F32)
        return jnp.sum(x_wide * x_wide, axis=1, keepdims=True)

    acc[...] = jnp.zeros_like(acc)
    squares = project(t)
    squares += project(lax.rem(t + 1, N_TP))
    squares += project(lax.rem(t + 7, N_TP))
    l_wait(2)
    l_start(3)
    for k in (2, 6, 3, 5):
        squares += project(lax.rem(t + k, N_TP))
    arrived(dl.at[pl.ds(0, 112)], dr_sem.at[0])
    down_t = jnp.sum(dl[...].reshape(8, 16, 256), axis=0)
    lora = jnp.transpose(jnp.concatenate([down_t] * 8, axis=0) * tenant_mask).astype(BF16)
    acc[...] += bdot(lora, up_all[...])
    l_wait(3)
    squares += project(lax.rem(t + 4, N_TP))
    inverse = lax.rsqrt(squares * (1.0 / DECODER_WIDTH) + EPSILON)

    causal = iota((128, 128), 0) >= iota((128, 128), 1)
    ones = jnp.ones((128, 128), BF16)
    for l in range(2):
        low, high = slice(64 * l, 64 * l + 64), slice(128 + 64 * l, 192 + 64 * l)
        factor = jnp.concatenate([inverse[low, :], inverse[high, :]], axis=0)

        def column(index):
            lanes = slice(128 * index, 128 * index + 128)
            return jnp.concatenate([acc[low, lanes], acc[high, lanes]], axis=0) * factor

        def rotate(values):
            return values * cosine[...] + pltpu.roll(values, 64, 1) * sine[...]

        key_rows = rotate(column(8)).astype(BF16)
        value_rows = jnp.concatenate([column(9).astype(BF16), ones], axis=1)
        kept = iota((128, 128), 0) < length[l]
        for j in range(QUERY_PER_KEY):
            query = rotate(column(j)).astype(BF16)
            scores = bdot_nt(query, key_rows) * (1.0 / math.sqrt(DECODER_HEAD_DIM))
            scores = jnp.where(causal, scores, -1e30)
            exponent = jnp.exp(scores - jnp.max(scores, axis=1, keepdims=True)).astype(BF16)
            summed = bdot(exponent, value_rows)
            out[128 * l:128 * l + 128, 128 * j:128 * j + 128] = jnp.where(
                kept, summed[:, :128] / summed[:, 128:], 0.0
            )

    g_sent()
    w_sent()
    e_sent()
    l_sent()
    o_sent()
    c_sent()
    for k in range(4):
        o_shared(k, ofs_sem, core)
    arrived(xs.at[pl.ds(0, 496)], as_sem.at[0])
    arrived(dl.at[pl.ds(0, 112)], ds_sem.at[0])


def on_device(
    patches, vit_qkv, vit_out, merge_weight, query_key_value_weight, adapter_down, adapter_up_weight,
    text_embed, vis_count, image_session, session_slot, session_tenant, session_len,
):
    operands = (
        session_slot, session_tenant, session_len, vis_count.reshape(8, 128), image_session.reshape(8, 128),
        patches.reshape(512, DV), vit_qkv, vit_out, merge_weight,
        query_key_value_weight.reshape(256, 10, 128), adapter_down, adapter_up_weight.reshape(128, 10, 128), text_embed,
    ) + tables()
    vmem = pl.BlockSpec(memory_space=pltpu.VMEM)
    smem = pl.BlockSpec(memory_space=pltpu.SMEM)
    hbm = pl.BlockSpec(memory_space=pl.ANY)
    dma = pltpu.SemaphoreType.DMA
    return pl.pallas_call(
        kernel,
        out_shape=jax.ShapeDtypeStruct((256, 1024), F32),
        in_specs=[smem if i < 3 else hbm if i == 8 else vmem for i in range(len(operands))],
        out_specs=vmem,
        scratch_shapes=[
            pltpu.VMEM((1536, 640), BF16),
            pltpu.VMEM((320, 640), F32),
            pltpu.VMEM((1280, 640), BF16),
            pltpu.VMEM((512, 1280), BF16),
            pltpu.VMEM((512, 1280), BF16),
            pltpu.VMEM((512, 512), BF16),
            pltpu.VMEM((1280, 1280), BF16),
            pltpu.VMEM((1280, 512), BF16),
            pltpu.VMEM((512, 1280), F32),
            pltpu.VMEM((5120, 1024), BF16),
            pltpu.VMEM((128, 1024), BF16),
            pltpu.VMEM((512, 256), BF16),
            pltpu.VMEM((512, 256), BF16),
            pltpu.VMEM((2048, 1024), BF16),
            pltpu.VMEM((128, 256), F32),
            pltpu.VMEM((8192, 1280), BF16),
            pltpu.VMEM((128, 1280), BF16),
            pltpu.VMEM((256, 1280), F32),
            dma((1,)), dma((G_COPIES,)), dma((G_COPIES,)), dma((W_COPIES,)), dma((W_COPIES,)),
            dma((8,)), dma((8,)), dma((8,)), dma((8,)), dma((8,)), dma((8,)), dma((8,)), dma((8,)), dma((8,)), dma((8,)),
            dma((1,)), dma((1,)), dma((1,)), dma((1,)),
        ],
        compiler_params=pltpu.CompilerParams(
            collective_id=0, has_side_effects=True, vmem_limit_bytes=64 * 1024 * 1024
        ),
    )(*operands)


def solution(mesh):
    placed = (
        P("seq", None, None),
        P(None, "seq", "tp"),
        P("tp", "seq"),
        P(None, "tp"),
        P("seq", "tp", None, None),
        P("tp", None),
        P(None, "tp", None, None),
        P("seq", "tp"),
        P(),
        P(),
        P(),
        P(),
        P(),
    )
    return jax.shard_map(
        on_device, mesh=mesh, in_specs=placed, out_specs=P("seq", "tp"), check_vma=False
    )
```

```python
import functools
import math

import jax
import jax.numpy as jnp
import numpy as np
from jax import lax
from jax.experimental import pallas as pl
from jax.experimental.pallas import tpu as pltpu
from jax.sharding import PartitionSpec as P

DV = 1280
HV = 16
HEAD = 80
DECODER_WIDTH = 8192
DECODER_HEAD_DIM = 128
ADAPTER_RANK = 16
IMG_DEV = 32
VMAX = 4
SLOT = 128
QUERY_PER_KEY = 8
N_SEQ = 32
N_TP = 8
COLS = 1280
EPSILON = 1e-06
ROPE_BASE = 1000000.0
MESH = pl.DeviceIdType.MESH
F32 = jnp.float32
BF16 = jnp.bfloat16


def tables():
    perm = np.zeros((512, 512), np.float32)
    for j in range(4):
        for i in range(32):
            for m in range(4):
                perm[j * 128 + i * 4 + m, i * 16 + m * 4 + j] = 1
    select = np.zeros((512, 768), np.float32)
    for group in range(6):
        for lane in range(HEAD):
            select[32 + group * HEAD + lane, group * 128 + lane] = 1
    half = DECODER_HEAD_DIM // 2
    inverse_freq = np.power(
        np.float32(ROPE_BASE), -(np.arange(half, dtype=np.float32) * 2.0 / DECODER_HEAD_DIM)
    ).astype(np.float32)
    angles = np.arange(SLOT, dtype=np.float32)[:, None] * inverse_freq[None, :]
    cosine = np.cos(angles).astype(np.float32)
    sine = np.sin(angles).astype(np.float32)
    return (
        jnp.asarray(perm, BF16),
        jnp.asarray(select, BF16),
        jnp.asarray(np.concatenate([cosine, cosine], 1)),
        jnp.asarray(np.concatenate([-sine, sine], 1)),
    )


def plane_copies():
    part_a, part_b = (0, 128), (128, 128)

    def sib(blocks):
        return [(by, bx, 0, 256, 0, 0, True) for by, bx in blocks]

    def go(by, bx, part, ty, tx):
        return (by, bx, part[0], part[1], ty, tx, False)

    sides = (-1, 1)
    near = [(0, -1), (0, 1), (-1, 0), (1, 0)]
    lists = {
        "0a": [go(0, 0, part_a, ty, tx) for ty, tx in near],
        "0b": [go(0, 0, part_b, ty, tx) for ty, tx in near],
        "0s": sib([(0, 0)]),
        "1a": [go(0, -1, part_a, 0, 1), go(-1, 0, part_a, 1, 0)]
        + [go(0, side, part_a, to, 0) for side in sides for to in sides],
        "1b": [go(0, 1, part_b, 0, -1), go(1, 0, part_b, -1, 0)]
        + [go(side, 0, part_b, 0, to) for side in sides for to in sides],
        "1s": sib(near),
        "2a": [go(0, 2, part_a, 1, 0), go(0, 2, part_a, -1, 0), go(-1, 1, part_a, 1, 0), go(1, -1, part_a, -1, 0)],
        "2b": [go(2, 0, part_b, 0, 1), go(2, 0, part_b, 0, -1), go(1, -1, part_b, 0, 1), go(-1, 1, part_b, 0, -1)],
        "2s": sib([(0, 2), (2, 0), (-1, -1), (-1, 1), (1, -1), (1, 1)]),
        "3a": [go(-1, 2, (0, 64), 1, 0), go(1, 2, (64, 64), -1, 0)],
        "3b": [go(2, -1, (128, 64), 0, 1), go(2, 1, (192, 64), 0, -1)],
        "3s": sib([(-1, 2), (1, 2), (2, -1), (2, 1)]),
        "4s": sib([(2, 2)]),
    }
    return {
        name: (i, sum(entry[3] for entry in entries), entries) for i, (name, entries) in enumerate(lists.items())
    }


W_GROUPS = plane_copies()
LANES = (256, 384)


def bdot(a, b):
    return jnp.dot(a, b, preferred_element_type=F32)


def bdot_nt(a, b):
    return lax.dot_general(a, b, (((1,), (1,)), ((), ())), preferred_element_type=F32)


def normalize(values):
    mean_val = jnp.mean(values, axis=-1, keepdims=True)
    centered = values - mean_val
    variance = jnp.mean(centered * centered, axis=-1, keepdims=True)
    return centered * lax.rsqrt(variance + EPSILON)


def iota(shape, axis):
    return lax.broadcasted_iota(jnp.int32, shape, axis)


def one_hot(mask):
    return mask.astype(F32).astype(BF16)


def kernel(
    slot_ref, tenant_ref, len_ref, counts, sessions, vit_qkv, vit_out,
    patches_hbm, mw, w, down_hbm, up, text_hbm, perm_hbm, select_hbm, cosine_hbm, sine_hbm,
    out,
    patches, down, text, perm, select, cosine, sine, w_in, up_in,
    g0, g1, wf, wall, pp, ln, qkv, o_all, ctx_all, enc, mwb, vis, xs, ys, tok, dl, w_all, up_all, acc, squares, res,
    load_sem, gs_sem, gr_sem, fs_sem, fr_sem, ws_sem, wr_sem,
    os_sem, or_sem, ofs_sem, ofr_sem, cs_sem, cr_sem, es_sem, er_sem, ls_sem, lr_sem,
    as_sem, ar_sem, ds_sem, dr_sem,
):
    s = lax.axis_index("seq")
    t = lax.axis_index("tp")
    core = lax.rem(s, 2)
    chip = s // 2
    cx = lax.rem(chip, 4)
    cy = chip // 4
    sibling = s + 1 - 2 * core

    def chip_at(dy, dx):
        return lax.rem(cy + (dy + 4), 4) * 4 + lax.rem(cx + (dx + 4), 4)

    def rows(ref, start, size, step=16):
        return ref.at[pl.ds(pl.multiple_of(start, step), size)]

    def arrived(ref, sem):
        pltpu.make_async_copy(ref, ref, sem).wait()

    barrier = pltpu.get_barrier_semaphore()

    def greet_seq(i, carry):
        pl.semaphore_signal(barrier, inc=1, device_id=(lax.rem(s + i, N_SEQ), t), device_id_type=MESH)
        return carry

    def greet_tp(i, carry):
        pl.semaphore_signal(barrier, inc=1, device_id=(s, lax.rem(t + i, N_TP)), device_id_type=MESH)
        return carry

    lax.fori_loop(1, N_SEQ, greet_seq, 0)
    lax.fori_loop(1, N_TP, greet_tp, 0)

    loads = [
        pltpu.make_async_copy(source, to, load_sem.at[i])
        for i, (source, to) in enumerate(
            (
                (perm_hbm, perm), (patches_hbm, patches), (text_hbm, text), (select_hbm, select), (down_hbm, down),
                (cosine_hbm, cosine), (sine_hbm, sine), (w, w_in), (up, up_in), (mw, mwb),
            )
        )
    ]
    for load in loads:
        load.start()
    g_of = (g0, g1)

    def g_ref(c, at, blocks, phase):
        return rows(g_of[phase], (c * 16 + at) * 48, 48 * blocks)

    def g_start(phase):
        for dx, dy in ((2, 2), (1, 2), (2, 1), (3, 2), (2, 3), (1, 1), (3, 3), (1, 3), (3, 1), (2, 0), (0, 2), (1, 0), (0, 1), (3, 0), (0, 3)):
            piece = g_ref(core, chip, 1, phase)
            pltpu.make_async_remote_copy(
                src_ref=piece, dst_ref=piece, send_sem=gs_sem.at[phase], recv_sem=gr_sem.at[4 * phase + (4 - dy) % 4],
                device_id=(chip_at(dy, dx) * 2 + core, t), device_id_type=MESH,
            ).start()

    def g_row_of_chips(c, d, phase):
        return g_ref(c, lax.rem(cy + d, 4) * 4, 4, phase)

    def g_share(phase, groups):
        for d in groups:
            group = g_row_of_chips(core, d, phase)
            arrived(g_of[phase].at[pl.ds(0, 192 if d > 0 else 144)], gr_sem.at[4 * phase + d])
            pltpu.make_async_remote_copy(
                src_ref=group, dst_ref=group, send_sem=fs_sem.at[phase], recv_sem=fr_sem.at[phase],
                device_id=(sibling, t), device_id_type=MESH,
            ).start()

    def g_shared(phase, sems):
        arrived(g_of[phase].at[pl.ds(0, 768)], sems.at[phase])

    def g_sent():
        for phase in range(2):
            arrived(g_of[phase].at[pl.ds(0, 720)], gs_sem.at[phase])
            g_shared(phase, fs_sem)

    def w_start(name):
        group, total, entries = W_GROUPS[name]
        for by, bx, first, size, ty, tx, sib in entries:
            piece = rows(w_all, (chip_at(by, bx) * 2 + core) * 256 + first, size)
            pltpu.make_async_remote_copy(
                src_ref=piece, dst_ref=piece, send_sem=ws_sem.at[group], recv_sem=wr_sem.at[group],
                device_id=(sibling if sib else chip_at(ty, tx) * 2 + core, t), device_id_type=MESH,
            ).start()

    def w_wait(name):
        group, total, entries = W_GROUPS[name]
        arrived(w_all.at[pl.ds(0, total)], wr_sem.at[group])

    def w_sent():
        for group, total, entries in W_GROUPS.values():
            arrived(w_all.at[pl.ds(0, total)], ws_sem.at[group])

    right = (s, lax.rem(t + 1, N_TP))
    left = (s, lax.rem(t + N_TP - 1, N_TP))

    def ring(buf, base, size, cut, send, recv):
        def piece(origin, j):
            first = base(lax.rem(origin + 2 * N_TP, N_TP))
            return rows(buf, first + cut * j, cut if j == 0 else size - cut)

        def ways(k, j):
            return [way for way in range(2) if k < 3 or way == j]

        def start(k, j):
            for way in ways(k, j):
                part = piece(t - k if way == 0 else t + k, j)
                pltpu.make_async_remote_copy(
                    src_ref=part, dst_ref=part, send_sem=send.at[0], recv_sem=recv.at[k * 2 + j],
                    device_id=(right, left)[way], device_id_type=MESH,
                ).start()

        def wait(k, j):
            arrived(buf.at[pl.ds(0, (cut if j == 0 else size - cut) * len(ways(k, j)))], recv.at[k * 2 + j])

        def on(k, j):
            wait(k - 1, j)
            start(k, j)

        def sent():
            arrived(buf.at[pl.ds(0, 7 * size)], send.at[0])

        return start, wait, on, sent

    e_start, e_wait, e_on, e_sent = ring(tok, lambda z: z * 256 + 128, 128, 64, es_sem, er_sem)
    l_start, l_wait, l_on, l_sent = ring(tok, lambda z: z * 256, 128, 64, ls_sem, lr_sem)
    o_start, o_wait, o_on, o_sent = ring(o_all, lambda z: z * 160 + 80 * core, 80, 48, os_sem, or_sem)
    c_start, c_wait, c_on, c_sent = ring(ctx_all, lambda z: z * 160, 160, 80, cs_sem, cr_sem)

    def o_share(k):
        for origin in (t - 1 - k, t + 1 + k) if k < 3 else (t + 4,):
            piece = rows(o_all, lax.rem(origin + 2 * N_TP, N_TP) * 160 + 80 * core, 80)
            pltpu.make_async_remote_copy(
                src_ref=piece, dst_ref=piece, send_sem=ofs_sem.at[0], recv_sem=ofr_sem.at[k],
                device_id=(sibling, t), device_id_type=MESH,
            ).start()

    def o_shared(k):
        arrived(o_all.at[pl.ds(0, 160 if k < 3 else 80)], ofr_sem.at[k])

    r_640, c_640 = iota((160, 640), 0), iota((160, 640), 1)
    mine = bdot(vit_out[...], one_hot(c_640 == r_640))
    for j in range(3):
        mine += bdot(vit_qkv[j], one_hot(c_640 == r_640 + 160 * (j + 1)))
    own_g = pl.ds(pl.multiple_of((core * 16 + chip) * 48, 16), 48)
    mine = jnp.concatenate([mine, jnp.zeros((8, 640), F32)], axis=0).astype(BF16)
    g0[own_g, :] = mine[:, :256]
    g1[own_g, :] = mine[:, 256:]

    def look_up(k, carry):
        slots, len0, len1, tenant0, tenant1 = carry
        slot = slot_ref[k]
        slots = jnp.where(sessions[...] == k, slot, slots)
        at0, at1 = slot == 2 * s, slot == 2 * s + 1
        return (
            slots, jnp.where(at0, len_ref[k], len0), jnp.where(at1, len_ref[k], len1),
            jnp.where(at0, tenant_ref[k], tenant0), jnp.where(at1, tenant_ref[k], tenant1),
        )

    zero = jnp.int32(0)
    slots, len0, len1, tenant0, tenant1 = lax.fori_loop(
        0, 64, look_up, (jnp.zeros((8, 128), jnp.int32), zero, zero, zero, zero)
    )
    length = (len0, len1)

    loads[7].wait()
    own_w = pl.ds(pl.multiple_of(s * 256, 256), 256)
    for j in range(10):
        w_all[own_w, 128 * j:128 * j + 128] = w_in[j]
    loads[8].wait()
    for j in range(10):
        up_all[:, 128 * j:128 * j + 128] = up_in[j]

    pl.semaphore_wait(barrier, N_SEQ + N_TP - 2)
    g_start(0)

    own_tok = pl.multiple_of(t * 256, 256)
    loads[2].wait()
    for l in range(2):
        tok[pl.ds(own_tok + 128 + 64 * l, 64), :] = jnp.where(
            iota((64, 1024), 0) + 64 < length[l], text[128 * l + 64:128 * l + 128, :], jnp.zeros((64, 1024), BF16)
        )
    e_start(0, 0)
    e_start(0, 1)

    loads[0].wait()
    loads[1].wait()
    for n in range(5):
        lanes = slice(256 * n, 256 * n + 256)
        pp[:, lanes] = bdot(perm[...], patches[:, lanes]).astype(BF16)
    for r in range(4):
        part = slice(128 * r, 128 * r + 128)
        ln[part, :] = normalize(pp[part, :].astype(F32)).astype(BF16)

    here = (slots >> 1) == s
    folded = jnp.concatenate(
        [jnp.where(here, counts[...], 0).astype(F32), jnp.where(here, slots & 1, 0).astype(F32)], axis=0
    ).astype(BF16)
    spread = bdot(folded, one_hot((iota((128, 512), 0) >> 5) == ((iota((128, 512), 1) >> 4) & 3)))
    n_8 = iota((8, 512), 1)
    own_row = iota((8, 512), 0) == (n_8 >> 6)
    count_n = jnp.sum(jnp.where(own_row, spread[:8, :], 0.0), axis=0, keepdims=True)
    place_n = jnp.sum(jnp.where(own_row, spread[8:, :], 0.0), axis=0, keepdims=True)
    by_place = jnp.where(iota((8, 512), 0) == place_n.astype(jnp.int32), count_n, 0.0)
    n_from, n_to = iota((512, 512), 0), iota((512, 512), 1)
    before = bdot(by_place.astype(BF16), one_hot(((n_from & 15) == 0) & ((n_from >> 4) < (n_to >> 4))))
    offset_n = jnp.where(place_n > 0.5, before[1:2, :], before[0:1, :])
    visual_rows = jnp.sum(by_place, axis=1, keepdims=True) * (1.0 / 16.0)
    n_1 = n_8[0:1, :]
    row_n = jnp.where(
        (n_1 & 3).astype(F32) < count_n, place_n * 64.0 + offset_n + (n_1 & 3).astype(F32), -1.0
    ).astype(jnp.int32)

    lane_8 = iota((128, 128), 1)
    encoded_here = bdot(
        jnp.concatenate([slots.astype(F32), counts[...].astype(F32)], axis=0).astype(BF16),
        one_hot(iota((128, 128), 0) == lax.rem(s, 4) * 32 + (lane_8 >> 2)),
    )
    own_row = iota((8, 128), 0) == s // 4
    slot_c = jnp.sum(jnp.where(own_row, encoded_here[:8, :], 0.0), axis=0, keepdims=True).astype(jnp.int32)
    count_c = jnp.sum(jnp.where(own_row, encoded_here[8:, :], 0.0), axis=0, keepdims=True).astype(jnp.int32)
    target_c = (slot_c >> 1) * 16 + (lane_8[0:1, :] & 3)
    key_8 = iota((128, 128), 0)
    bias = jnp.where(((key_8 >> 2) == (lane_8 >> 2)) & ((key_8 & 3) < count_c), 0.0, -1e30)
    tenant_mask = (
        (iota((128, 256), 0) >> 4) == jnp.where((iota((128, 256), 1) & 64) == 0, tenant0, tenant1)
    ).astype(F32)

    g_share(0, (0, 1, 2, 3))
    g_start(1)
    g_shared(0, fr_sem)

    def unpack(phase):
        lanes = slice(256 * phase, 256 * phase + LANES[phase])
        for c in range(4):
            for b in range(8):
                first = ((b % 2) * 16 + 4 * c + b // 2) * 48
                wf[40 * b:40 * b + 40, lanes] = g_of[phase][first:first + 48, :].astype(F32)[:40, :]
            wall[320 * c:320 * c + 320, lanes] = wf[:, lanes].astype(BF16)

    unpack(0)
    own_o = pl.multiple_of(t * 160, 32)
    pick = one_hot(iota((160, 256), 0) == iota((160, 256), 1))
    for r in range(5):
        part = slice(256 * r, 256 * r + 256)
        o_all[pl.ds(own_o, 160), part] = bdot_nt(pick, wall[part, 0:256]).astype(BF16)
    o_start(0, 0)
    o_start(0, 1)
    e_on(1, 0)

    g_share(1, (2, 1))
    w_start("0a")
    w_start("0b")
    w_start("0s")
    g_share(1, (3, 0))
    o_on(1, 0)
    g_shared(1, fr_sem)
    unpack(1)
    o_on(1, 1)
    o_share(0)
    for n in range(2):
        lanes = slice(256 * n, 256 * n + 256)
        qkv[:, lanes] = bdot(ln[...], wall[:, 128 + 256 * n:384 + 256 * n]).astype(BF16)
    loads[3].wait()
    scale = 1.0 / math.sqrt(HEAD)
    for h in range(2):
        q_h = bdot(qkv[...], select[:, 128 * h:128 * h + 128]).astype(BF16)
        k_h = bdot(qkv[...], select[:, 256 + 128 * h:384 + 128 * h]).astype(BF16)
        v_h = bdot(qkv[...], select[:, 512 + 128 * h:640 + 128 * h])
        v_t = jnp.transpose(v_h).astype(BF16)
        for q in range(4):
            scores = bdot_nt(k_h, q_h[128 * q:128 * q + 128, :]) * scale
            scores = scores.reshape(4, 128, 128) + bias[None]
            largest = jnp.max(jnp.max(scores, axis=0), axis=0, keepdims=True)
            exponent = jnp.exp(scores - largest[None])
            total = jnp.sum(jnp.sum(exponent, axis=0), axis=0, keepdims=True)
            probs = (exponent / total[None]).astype(BF16).reshape(512, 128)
            ctx_t = bdot(v_t, probs).astype(BF16)
            ctx_all[pl.ds(own_o + 80 * h, 80), 128 * q:128 * q + 128] = ctx_t[:80, :]
        c_start(0, h)

    def project_out(z, first=False):
        at = pl.ds(pl.multiple_of(lax.rem(z + 2 * N_TP, N_TP) * 160, 32), 160)
        for n in range(5):
            lanes = slice(256 * n, 256 * n + 256)
            term = lax.dot_general(
                ctx_all[at, :], o_all[at, lanes], (((0,), (0,)), ((), ())), preferred_element_type=F32
            )
            enc[:, lanes] = (pp[:, lanes].astype(F32) if first else enc[:, lanes]) + term

    w_wait("0a")
    w_start("1a")
    o_on(2, 0)
    o_on(2, 1)
    o_share(1)
    project_out(t, True)
    c_on(1, 0)
    c_on(1, 1)
    w_wait("0b")
    w_start("1b")
    w_start("1s")
    o_shared(0)
    project_out(t - 1)
    project_out(t + 1)
    o_on(3, 0)
    o_on(3, 1)
    o_share(2)
    c_on(2, 0)
    c_on(2, 1)
    o_shared(1)
    project_out(t - 2)
    project_out(t + 2)
    o_wait(3, 0)
    o_wait(3, 1)
    o_share(3)
    c_on(3, 0)
    c_on(3, 1)
    o_shared(2)
    e_on(1, 1)
    e_on(2, 0)
    project_out(t - 3)
    project_out(t + 3)
    o_shared(3)
    loads[9].wait()
    c_wait(3, 0)
    c_wait(3, 1)
    project_out(t + 4)

    merged = jnp.zeros((128, 1024), F32)
    for j in range(4):
        merged_in = normalize(enc[128 * j:128 * j + 128, :]).astype(BF16)
        merged += bdot(merged_in, mwb[1280 * j:1280 * j + 1280, :])
    vis[...] = merged.astype(BF16)
    e_on(2, 1)

    row_512 = iota((512, 128), 0)
    outgoing = jnp.zeros((512, 256), F32)
    for q in range(4):
        outgoing += bdot(one_hot(row_512 == target_c + 4 * q), vis[:, 256 * q:256 * q + 256])
    xs[...] = outgoing.astype(BF16)

    def send_rows(i, carry):
        to = lax.rem(s + i, N_SEQ)
        pltpu.make_async_remote_copy(
            src_ref=rows(xs, to * 16, 16), dst_ref=rows(ys, s * 16, 16),
            send_sem=as_sem.at[0], recv_sem=ar_sem.at[0], device_id=(to, t), device_id_type=MESH,
        ).start()
        return carry

    lax.fori_loop(1, N_SEQ, send_rows, 0)
    own_y = pl.ds(pl.multiple_of(s * 16, 16), 16)
    ys[own_y, :] = xs[own_y, :]
    e_on(3, 0)
    e_on(3, 1)
    arrived(ys.at[pl.ds(0, 496)], ar_sem.at[0])
    w_wait("1a")
    w_start("2a")
    w_wait("1b")
    w_start("2b")
    w_start("2s")

    row_128 = iota((128, 512), 0)
    position = iota((64, 256), 0)
    for q in range(4):
        lanes = slice(256 * q, 256 * q + 256)
        picked = bdot(one_hot((row_128 == row_n) & (((n_1 >> 2) & 3) == q)), ys[...]).astype(BF16)
        for l in range(2):
            is_text = (position.astype(F32) >= visual_rows[l:l + 1, :]) & (position < length[l])
            tok[pl.ds(own_tok + 64 * l, 64), lanes] = jnp.where(
                is_text, text[128 * l:128 * l + 64, lanes], picked[64 * l:64 * l + 64, :]
            )
    l_start(0, 0)
    l_start(0, 1)

    loads[4].wait()
    down_sums = jnp.transpose(bdot(tok[pl.ds(own_tok, 256), :], down[...])) * tenant_mask
    dl[pl.ds(pl.multiple_of(t * 16, 16), 16), :] = jnp.sum(down_sums.reshape(8, 16, 256), axis=0)

    def send_down(i, carry):
        piece = rows(dl, t * 16, 16)
        pltpu.make_async_remote_copy(
            src_ref=piece, dst_ref=piece, send_sem=ds_sem.at[0], recv_sem=dr_sem.at[0],
            device_id=(s, lax.rem(t + i, N_TP)), device_id_type=MESH,
        ).start()
        return carry

    lax.fori_loop(1, N_TP, send_down, 0)

    def project(far, nearest, farthest):
        for z in range(8):
            distance = min(z, N_TP - z)
            if not nearest <= distance <= farthest:
                continue
            z = lax.rem(t + z, N_TP)
            x = tok[pl.ds(pl.multiple_of(z * 256, 256), 256), :]
            first = pl.multiple_of(z * 1024, 1024)
            for n in range(5):
                lanes = slice(256 * n, 256 * n + 256)
                acc[:, lanes] += bdot(x, w_all[pl.ds(first, 1024), lanes])
            x_wide = x.astype(F32)
            x_wide = x_wide * x_wide
            for n in range(8):
                squares[...] += x_wide[:, 128 * n:128 * n + 128]

    acc[...] = jnp.zeros_like(acc)
    squares[...] = jnp.zeros_like(squares)
    l_on(1, 0)
    l_on(1, 1)
    for name in ("0s", "1s", "2s"):
        w_wait(name)
    l_on(2, 0)
    w_wait("2a")
    w_start("3a")
    w_wait("2b")
    w_start("3b")
    w_start("3s")
    l_on(2, 1)
    e_wait(3, 0)
    e_wait(3, 1)
    w_wait("3a")
    w_wait("3b")
    w_start("4s")
    l_on(3, 0)
    l_on(3, 1)
    w_wait("3s")
    w_wait("4s")
    project(True, 0, 3)
    arrived(dl.at[pl.ds(0, 112)], dr_sem.at[0])
    down_t = jnp.sum(dl[...].reshape(8, 16, 256), axis=0)
    lora = jnp.transpose(jnp.concatenate([down_t] * 8, axis=0) * tenant_mask).astype(BF16)
    acc[...] += bdot(lora, up_all[...])
    l_wait(3, 0)
    l_wait(3, 1)
    project(None, 4, 4)
    inverse = lax.rsqrt(jnp.sum(squares[...], axis=1, keepdims=True) * (1.0 / DECODER_WIDTH) + EPSILON)

    loads[5].wait()
    loads[6].wait()

    causal = iota((128, 128), 0) >= iota((128, 128), 1)
    ones = jnp.ones((128, 128), BF16)
    stores = []
    for l in range(2):
        low, high = slice(64 * l, 64 * l + 64), slice(128 + 64 * l, 192 + 64 * l)
        factor = jnp.concatenate([inverse[low, :], inverse[high, :]], axis=0)

        def column(index):
            lanes = slice(128 * index, 128 * index + 128)
            return jnp.concatenate([acc[low, lanes], acc[high, lanes]], axis=0) * factor

        def rotate(values):
            return values * cosine[...] + pltpu.roll(values, 64, 1) * sine[...]

        key_rows = rotate(column(8)).astype(BF16)
        value_rows = jnp.concatenate([column(9).astype(BF16), ones], axis=1)
        kept = iota((128, 128), 0) < length[l]
        for j in range(QUERY_PER_KEY):
            query = rotate(column(j)).astype(BF16)
            scores = bdot_nt(query, key_rows) * (1.0 / math.sqrt(DECODER_HEAD_DIM))
            scores = jnp.where(causal, scores, -1e30)
            exponent = jnp.exp(scores - jnp.max(scores, axis=1, keepdims=True)).astype(BF16)
            summed = bdot(exponent, value_rows)
            res[128 * l:128 * l + 128, 128 * j:128 * j + 128] = jnp.where(
                kept, summed[:, :128] / summed[:, 128:], 0.0
            ).astype(BF16)
        stores.append(pltpu.make_async_copy(
            res.at[pl.ds(128 * l, 128)], out.at[pl.ds(128 * l, 128)], load_sem.at[10 + l]
        ))
        stores[l].start()

    for store in stores:
        store.wait()
    g_sent()
    w_sent()
    e_sent()
    l_sent()
    o_sent()
    c_sent()
    arrived(o_all.at[pl.ds(0, 560)], ofs_sem.at[0])
    arrived(xs.at[pl.ds(0, 496)], as_sem.at[0])
    arrived(dl.at[pl.ds(0, 112)], ds_sem.at[0])


def on_device(
    patches, vit_qkv, vit_out, merge_weight, query_key_value_weight, adapter_down, adapter_up_weight,
    text_embed, vis_count, image_session, session_slot, session_tenant, session_len,
):
    operands = (
        session_slot, session_tenant, session_len, vis_count.reshape(8, 128), image_session.reshape(8, 128),
        vit_qkv, vit_out.T, patches.reshape(512, DV), merge_weight,
        jnp.transpose(query_key_value_weight.reshape(256, 10, 128), (1, 0, 2)), adapter_down,
        jnp.transpose(adapter_up_weight.reshape(128, 10, 128), (1, 0, 2)), text_embed,
    ) + tables()
    vmem = pl.BlockSpec(memory_space=pltpu.VMEM)
    smem = pl.BlockSpec(memory_space=pltpu.SMEM)
    hbm = pl.BlockSpec(memory_space=pl.ANY)
    dma = pltpu.SemaphoreType.DMA
    return pl.pallas_call(
        kernel,
        out_shape=jax.ShapeDtypeStruct((256, 1024), BF16),
        in_specs=[smem if i < 3 else vmem if i < 7 else hbm for i in range(len(operands))],
        out_specs=hbm,
        scratch_shapes=[
            pltpu.VMEM((512, 1280), BF16),
            pltpu.VMEM((1024, 128), BF16),
            pltpu.VMEM((256, 1024), BF16),
            pltpu.VMEM((512, 512), BF16),
            pltpu.VMEM((512, 768), BF16),
            pltpu.VMEM((128, 128), F32),
            pltpu.VMEM((128, 128), F32),
            pltpu.VMEM((10, 256, 128), BF16),
            pltpu.VMEM((10, 128, 128), BF16),
            pltpu.VMEM((1536, LANES[0]), BF16),
            pltpu.VMEM((1536, LANES[1]), BF16),
            pltpu.VMEM((320, 640), F32),
            pltpu.VMEM((1280, 640), BF16),
            pltpu.VMEM((512, 1280), BF16),
            pltpu.VMEM((512, 1280), BF16),
            pltpu.VMEM((512, 512), BF16),
            pltpu.VMEM((1280, 1280), BF16),
            pltpu.VMEM((1280, 512), BF16),
            pltpu.VMEM((512, 1280), F32),
            pltpu.VMEM((5120, 1024), BF16),
            pltpu.VMEM((128, 1024), BF16),
            pltpu.VMEM((512, 256), BF16),
            pltpu.VMEM((512, 256), BF16),
            pltpu.VMEM((2048, 1024), BF16),
            pltpu.VMEM((128, 256), F32),
            pltpu.VMEM((8192, 1280), BF16),
            pltpu.VMEM((128, 1280), BF16),
            pltpu.VMEM((256, 1280), F32),
            pltpu.VMEM((256, 128), F32),
            pltpu.VMEM((256, 1024), BF16),
            dma((12,)), dma((2,)), dma((8,)), dma((2,)), dma((2,)), dma((len(W_GROUPS),)), dma((len(W_GROUPS),)),
            dma((1,)), dma((8,)), dma((1,)), dma((4,)),
            dma((1,)), dma((8,)), dma((1,)), dma((8,)), dma((1,)), dma((8,)),
            dma((1,)), dma((1,)), dma((1,)), dma((1,)),
        ],
        compiler_params=pltpu.CompilerParams(
            collective_id=0, has_side_effects=True, vmem_limit_bytes=64 * 1024 * 1024
        ),
    )(*operands).astype(F32)


def solution(mesh):
    placed = (
        P("seq", None, None),
        P(None, "seq", "tp"),
        P("tp", "seq"),
        P(None, "tp"),
        P("seq", "tp", None, None),
        P("tp", None),
        P(None, "tp", None, None),
        P("seq", "tp"),
        P(),
        P(),
        P(),
        P(),
        P(),
    )
    return jax.shard_map(
        on_device, mesh=mesh, in_specs=placed, out_specs=P("seq", "tp"), check_vma=False
    )
```

```python
import functools
import math

import jax
import jax.numpy as jnp
import numpy as np
from jax import lax
from jax.experimental import pallas as pl
from jax.experimental.pallas import tpu as pltpu
from jax.sharding import PartitionSpec as P

DV = 1280
HV = 16
HEAD = 80
DECODER_WIDTH = 8192
DECODER_HEAD_DIM = 128
ADAPTER_RANK = 16
IMG_DEV = 32
VMAX = 4
SLOT = 128
QUERY_PER_KEY = 8
N_SEQ = 32
N_TP = 8
COLS = 1280
EPSILON = 1e-06
ROPE_BASE = 1000000.0
MESH = pl.DeviceIdType.MESH
F32 = jnp.float32
BF16 = jnp.bfloat16


def tables():
    perm = np.zeros((512, 512), np.float32)
    for j in range(4):
        for i in range(32):
            for m in range(4):
                perm[j * 128 + i * 4 + m, i * 16 + m * 4 + j] = 1
    select = np.zeros((512, 768), np.float32)
    for group in range(6):
        for lane in range(HEAD):
            select[32 + group * HEAD + lane, group * 128 + lane] = 1
    half = DECODER_HEAD_DIM // 2
    inverse_freq = np.power(
        np.float32(ROPE_BASE), -(np.arange(half, dtype=np.float32) * 2.0 / DECODER_HEAD_DIM)
    ).astype(np.float32)
    angles = np.arange(SLOT, dtype=np.float32)[:, None] * inverse_freq[None, :]
    cosine = np.cos(angles).astype(np.float32)
    sine = np.sin(angles).astype(np.float32)
    return (
        jnp.asarray(perm, BF16),
        jnp.asarray(select, BF16),
        jnp.asarray(np.concatenate([cosine, cosine], 1)),
        jnp.asarray(np.concatenate([-sine, sine], 1)),
    )


def plane_copies():
    part_a, part_b = (0, 128), (128, 128)

    def sib(blocks):
        return [(by, bx, 0, 256, 0, 0, True) for by, bx in blocks]

    def go(by, bx, part, ty, tx):
        return (by, bx, part[0], part[1], ty, tx, False)

    sides = (-1, 1)
    near = [(0, -1), (0, 1), (-1, 0), (1, 0)]
    lists = {
        "0a": [go(0, 0, part_a, ty, tx) for ty, tx in near],
        "0b": [go(0, 0, part_b, ty, tx) for ty, tx in near],
        "0s": sib([(0, 0)]),
        "1a": [go(0, -1, part_a, 0, 1), go(-1, 0, part_a, 1, 0)]
        + [go(0, side, part_a, to, 0) for side in sides for to in sides],
        "1b": [go(1, 0, part_b, -1, 0)]
        + [go(side, 0, part_b, 0, to) for side in sides for to in sides],
        "1c": [go(0, 1, (128, 64), 0, -1), go(0, -1, (192, 64), 0, 1)],
        "1s": sib(near),
        "2a": [go(0, 2, part_a, 1, 0), go(0, 2, part_a, -1, 0), go(-1, 1, part_a, 1, 0), go(1, -1, part_a, -1, 0)],
        "2b": [go(2, 0, part_b, 0, 1), go(2, 0, part_b, 0, -1), go(1, -1, part_b, 0, 1), go(-1, 1, part_b, 0, -1)],
        "2s": sib([(2, 0), (-1, -1), (-1, 1), (1, -1), (1, 1)]),
        "3a": [go(-1, 2, (0, 64), 1, 0), go(1, 2, (64, 64), -1, 0)],
        "3b": [go(2, -1, (128, 64), 0, 1), go(2, 1, (192, 64), 0, -1)],
        "3s": sib([(-1, 2), (1, 2), (2, -1), (2, 1)]),
        "4s": sib([(0, 2), (2, 2)]),
    }
    return {
        name: (i, sum(entry[3] for entry in entries), entries) for i, (name, entries) in enumerate(lists.items())
    }


W_GROUPS = plane_copies()
LANES = (256, 384)


def bdot(a, b):
    return jnp.dot(a, b, preferred_element_type=F32)


def bdot_nt(a, b):
    return lax.dot_general(a, b, (((1,), (1,)), ((), ())), preferred_element_type=F32)


def normalize(values):
    mean_val = jnp.mean(values, axis=-1, keepdims=True)
    centered = values - mean_val
    variance = jnp.mean(centered * centered, axis=-1, keepdims=True)
    return centered * lax.rsqrt(variance + EPSILON)


def iota(shape, axis):
    return lax.broadcasted_iota(jnp.int32, shape, axis)


def one_hot(mask):
    return mask.astype(F32).astype(BF16)


def kernel(
    slot_ref, tenant_ref, len_ref, counts, sessions, vit_qkv, vit_out,
    patches_hbm, mw, w, down_hbm, up, text_hbm, perm_hbm, select_hbm, cosine_hbm, sine_hbm,
    out,
    patches, down, text, perm, select, cosine, sine, w_in, up_in,
    g0, g1, wf, wall, pp, ln, qkv, o_all, ctx_all, enc, mwb, vis, xs, ys, tok, dl, w_all, up_all, acc, squares, res,
    load_sem, gs_sem, gr_sem, fs_sem, fr_sem, ws_sem, wr_sem,
    os_sem, or_sem, ofs_sem, ofr_sem, cs_sem, cr_sem, es_sem, er_sem, ls_sem, lr_sem,
    as_sem, ar_sem, ds_sem, dr_sem,
):
    s = lax.axis_index("seq")
    t = lax.axis_index("tp")
    core = lax.rem(s, 2)
    chip = s // 2
    cx = lax.rem(chip, 4)
    cy = chip // 4
    sibling = s + 1 - 2 * core

    def chip_at(dy, dx):
        return lax.rem(cy + (dy + 4), 4) * 4 + lax.rem(cx + (dx + 4), 4)

    def rows(ref, start, size, step=16):
        return ref.at[pl.ds(pl.multiple_of(start, step), size)]

    def arrived(ref, sem):
        pltpu.make_async_copy(ref, ref, sem).wait()

    barrier = pltpu.get_barrier_semaphore()

    def greet_seq(i, carry):
        pl.semaphore_signal(barrier, inc=1, device_id=(lax.rem(s + i, N_SEQ), t), device_id_type=MESH)
        return carry

    def greet_tp(i, carry):
        pl.semaphore_signal(barrier, inc=1, device_id=(s, lax.rem(t + i, N_TP)), device_id_type=MESH)
        return carry

    lax.fori_loop(1, N_SEQ, greet_seq, 0)
    lax.fori_loop(1, N_TP, greet_tp, 0)

    loads = [
        pltpu.make_async_copy(source, to, load_sem.at[i])
        for i, (source, to) in enumerate(
            (
                (perm_hbm, perm), (patches_hbm, patches), (text_hbm, text), (select_hbm, select), (down_hbm, down),
                (cosine_hbm, cosine), (sine_hbm, sine), (w, w_in), (up, up_in), (mw, mwb),
            )
        )
    ]
    for load in loads:
        load.start()
    g_of = (g0, g1)

    def g_ref(c, at, blocks, phase):
        return rows(g_of[phase], (c * 16 + at) * 48, 48 * blocks)

    def g_start(phase):
        for dx, dy in ((2, 2), (1, 2), (2, 1), (3, 2), (2, 3), (1, 1), (3, 3), (1, 3), (3, 1), (2, 0), (0, 2), (1, 0), (0, 1), (3, 0), (0, 3)):
            piece = g_ref(core, chip, 1, phase)
            pltpu.make_async_remote_copy(
                src_ref=piece, dst_ref=piece, send_sem=gs_sem.at[phase], recv_sem=gr_sem.at[4 * phase + (4 - dy) % 4],
                device_id=(chip_at(dy, dx) * 2 + core, t), device_id_type=MESH,
            ).start()

    def g_row_of_chips(c, d, phase):
        return g_ref(c, lax.rem(cy + d, 4) * 4, 4, phase)

    def g_share(phase, groups):
        for d in groups:
            group = g_row_of_chips(core, d, phase)
            arrived(g_of[phase].at[pl.ds(0, 192 if d > 0 else 144)], gr_sem.at[4 * phase + d])
            pltpu.make_async_remote_copy(
                src_ref=group, dst_ref=group, send_sem=fs_sem.at[phase], recv_sem=fr_sem.at[phase],
                device_id=(sibling, t), device_id_type=MESH,
            ).start()

    def g_shared(phase, sems):
        arrived(g_of[phase].at[pl.ds(0, 768)], sems.at[phase])

    def g_sent():
        for phase in range(2):
            arrived(g_of[phase].at[pl.ds(0, 720)], gs_sem.at[phase])
            g_shared(phase, fs_sem)

    def w_start(name):
        group, total, entries = W_GROUPS[name]
        for by, bx, first, size, ty, tx, sib in entries:
            piece = rows(w_all, (chip_at(by, bx) * 2 + core) * 256 + first, size)
            pltpu.make_async_remote_copy(
                src_ref=piece, dst_ref=piece, send_sem=ws_sem.at[group], recv_sem=wr_sem.at[group],
                device_id=(sibling if sib else chip_at(ty, tx) * 2 + core, t), device_id_type=MESH,
            ).start()

    def w_wait(name):
        group, total, entries = W_GROUPS[name]
        arrived(w_all.at[pl.ds(0, total)], wr_sem.at[group])

    def w_sent():
        for group, total, entries in W_GROUPS.values():
            arrived(w_all.at[pl.ds(0, total)], ws_sem.at[group])

    right = (s, lax.rem(t + 1, N_TP))
    left = (s, lax.rem(t + N_TP - 1, N_TP))

    def ring(buf, base, size, cut, send, recv, crossed):
        def piece(origin, j):
            first = base(lax.rem(origin + 2 * N_TP, N_TP))
            return rows(buf, first + cut * j, cut if j == 0 else size - cut)

        def ways(k, j):
            both = [(0, j), (1, 1 - j if crossed else j)]
            return both if k < 3 else [(way, part) for way, part in both if part == way]

        def start(k, j):
            for way, part in ways(k, j):
                block = piece(t - k if way == 0 else t + k, part)
                pltpu.make_async_remote_copy(
                    src_ref=block, dst_ref=block, send_sem=send.at[0], recv_sem=recv.at[k * 2 + j],
                    device_id=(right, left)[way], device_id_type=MESH,
                ).start()

        def wait(k, j):
            total = sum((cut, size - cut)[part] for way, part in ways(k, j))
            if total > 0:
                arrived(buf.at[pl.ds(0, total)], recv.at[k * 2 + j])

        def on(k, j):
            wait(k - 1, j)
            start(k, j)

        def sent():
            arrived(buf.at[pl.ds(0, 7 * size)], send.at[0])

        return start, wait, on, sent

    e_start, e_wait, e_on, e_sent = ring(tok, lambda z: z * 256 + 128, 128, 64, es_sem, er_sem, True)
    l_start, l_wait, l_on, l_sent = ring(tok, lambda z: z * 256, 128, 64, ls_sem, lr_sem, True)
    o_start, o_wait, o_on, o_sent = ring(o_all, lambda z: z * 160 + 80 * core, 80, 48, os_sem, or_sem, True)
    c_start, c_wait, c_on, c_sent = ring(ctx_all, lambda z: z * 160, 160, 80, cs_sem, cr_sem, True)

    def o_share(k):
        for origin in (t - 1 - k, t + 1 + k) if k < 3 else (t + 4,):
            piece = rows(o_all, lax.rem(origin + 2 * N_TP, N_TP) * 160 + 80 * core, 80)
            pltpu.make_async_remote_copy(
                src_ref=piece, dst_ref=piece, send_sem=ofs_sem.at[0], recv_sem=ofr_sem.at[k],
                device_id=(sibling, t), device_id_type=MESH,
            ).start()

    def o_shared(k):
        arrived(o_all.at[pl.ds(0, 160 if k < 3 else 80)], ofr_sem.at[k])

    r_640, c_640 = iota((160, 640), 0), iota((160, 640), 1)
    mine = bdot(vit_out[...], one_hot(c_640 == r_640))
    for j in range(3):
        mine += bdot(vit_qkv[j], one_hot(c_640 == r_640 + 160 * (j + 1)))
    own_g = pl.ds(pl.multiple_of((core * 16 + chip) * 48, 16), 48)
    mine = jnp.concatenate([mine, jnp.zeros((8, 640), F32)], axis=0).astype(BF16)
    g0[own_g, :] = mine[:, :256]
    g1[own_g, :] = mine[:, 256:]

    def look_up(k, carry):
        slots, len0, len1, tenant0, tenant1 = carry
        slot = slot_ref[k]
        slots = jnp.where(sessions[...] == k, slot, slots)
        at0, at1 = slot == 2 * s, slot == 2 * s + 1
        return (
            slots, jnp.where(at0, len_ref[k], len0), jnp.where(at1, len_ref[k], len1),
            jnp.where(at0, tenant_ref[k], tenant0), jnp.where(at1, tenant_ref[k], tenant1),
        )

    zero = jnp.int32(0)
    slots, len0, len1, tenant0, tenant1 = lax.fori_loop(
        0, 64, look_up, (jnp.zeros((8, 128), jnp.int32), zero, zero, zero, zero)
    )
    length = (len0, len1)

    loads[7].wait()
    own_w = pl.ds(pl.multiple_of(s * 256, 256), 256)
    for j in range(10):
        w_all[own_w, 128 * j:128 * j + 128] = w_in[j]
    loads[8].wait()
    for j in range(10):
        up_all[:, 128 * j:128 * j + 128] = up_in[j]

    pl.semaphore_wait(barrier, N_SEQ + N_TP - 2)
    g_start(0)

    own_tok = pl.multiple_of(t * 256, 256)
    loads[2].wait()
    for l in range(2):
        tok[pl.ds(own_tok + 128 + 64 * l, 64), :] = jnp.where(
            iota((64, 1024), 0) + 64 < length[l], text[128 * l + 64:128 * l + 128, :], jnp.zeros((64, 1024), BF16)
        )
    e_start(0, 0)
    e_start(0, 1)

    loads[0].wait()
    loads[1].wait()
    for n in range(5):
        lanes = slice(256 * n, 256 * n + 256)
        pp[:, lanes] = bdot(perm[...], patches[:, lanes]).astype(BF16)
    for r in range(4):
        part = slice(128 * r, 128 * r + 128)
        ln[part, :] = normalize(pp[part, :].astype(F32)).astype(BF16)

    here = (slots >> 1) == s
    folded = jnp.concatenate(
        [jnp.where(here, counts[...], 0).astype(F32), jnp.where(here, slots & 1, 0).astype(F32)], axis=0
    ).astype(BF16)
    spread = bdot(folded, one_hot((iota((128, 512), 0) >> 5) == ((iota((128, 512), 1) >> 4) & 3)))
    n_8 = iota((8, 512), 1)
    own_row = iota((8, 512), 0) == (n_8 >> 6)
    count_n = jnp.sum(jnp.where(own_row, spread[:8, :], 0.0), axis=0, keepdims=True)
    place_n = jnp.sum(jnp.where(own_row, spread[8:, :], 0.0), axis=0, keepdims=True)
    by_place = jnp.where(iota((8, 512), 0) == place_n.astype(jnp.int32), count_n, 0.0)
    n_from, n_to = iota((512, 512), 0), iota((512, 512), 1)
    before = bdot(by_place.astype(BF16), one_hot(((n_from & 15) == 0) & ((n_from >> 4) < (n_to >> 4))))
    offset_n = jnp.where(place_n > 0.5, before[1:2, :], before[0:1, :])
    visual_rows = jnp.sum(by_place, axis=1, keepdims=True) * (1.0 / 16.0)
    n_1 = n_8[0:1, :]
    row_n = jnp.where(
        (n_1 & 3).astype(F32) < count_n, place_n * 64.0 + offset_n + (n_1 & 3).astype(F32), -1.0
    ).astype(jnp.int32)

    lane_8 = iota((128, 128), 1)
    encoded_here = bdot(
        jnp.concatenate([slots.astype(F32), counts[...].astype(F32)], axis=0).astype(BF16),
        one_hot(iota((128, 128), 0) == lax.rem(s, 4) * 32 + (lane_8 >> 2)),
    )
    own_row = iota((8, 128), 0) == s // 4
    slot_c = jnp.sum(jnp.where(own_row, encoded_here[:8, :], 0.0), axis=0, keepdims=True).astype(jnp.int32)
    count_c = jnp.sum(jnp.where(own_row, encoded_here[8:, :], 0.0), axis=0, keepdims=True).astype(jnp.int32)
    target_c = (slot_c >> 1) * 16 + (lane_8[0:1, :] & 3)
    key_8 = iota((128, 128), 0)
    bias = jnp.where(((key_8 >> 2) == (lane_8 >> 2)) & ((key_8 & 3) < count_c), 0.0, -1e30)
    tenant_mask = (
        (iota((128, 256), 0) >> 4) == jnp.where((iota((128, 256), 1) & 64) == 0, tenant0, tenant1)
    ).astype(F32)

    g_share(0, (2, 3, 1, 0))
    g_start(1)
    g_shared(0, fr_sem)

    def unpack(phase):
        lanes = slice(256 * phase, 256 * phase + LANES[phase])
        for c in range(4):
            for b in range(8):
                first = ((b % 2) * 16 + 4 * c + b // 2) * 48
                wf[40 * b:40 * b + 40, lanes] = g_of[phase][first:first + 48, :].astype(F32)[:40, :]
            wall[320 * c:320 * c + 320, lanes] = wf[:, lanes].astype(BF16)

    unpack(0)
    own_o = pl.multiple_of(t * 160, 32)
    pick = one_hot(iota((160, 256), 0) == iota((160, 256), 1))
    for r in range(5):
        part = slice(256 * r, 256 * r + 256)
        o_all[pl.ds(own_o, 160), part] = bdot_nt(pick, wall[part, 0:256]).astype(BF16)
    o_start(0, 0)
    o_start(0, 1)

    g_share(1, (2, 3))
    w_start("0a")
    w_start("0b")
    w_start("0s")
    g_share(1, (1, 0))
    o_on(1, 0)
    g_shared(1, fr_sem)
    unpack(1)
    o_on(1, 1)
    o_share(0)
    for n in range(2):
        lanes = slice(256 * n, 256 * n + 256)
        qkv[:, lanes] = bdot(ln[...], wall[:, 128 + 256 * n:384 + 256 * n]).astype(BF16)
    loads[3].wait()
    scale = 1.0 / math.sqrt(HEAD)
    for h in range(2):
        q_h = bdot(qkv[...], select[:, 128 * h:128 * h + 128]).astype(BF16)
        k_h = bdot(qkv[...], select[:, 256 + 128 * h:384 + 128 * h]).astype(BF16)
        v_h = bdot(qkv[...], select[:, 512 + 128 * h:640 + 128 * h])
        v_t = jnp.transpose(v_h).astype(BF16)
        for q in range(4):
            scores = bdot_nt(k_h, q_h[128 * q:128 * q + 128, :]) * scale
            scores = scores.reshape(4, 128, 128) + bias[None]
            largest = jnp.max(jnp.max(scores, axis=0), axis=0, keepdims=True)
            exponent = jnp.exp(scores - largest[None])
            total = jnp.sum(jnp.sum(exponent, axis=0), axis=0, keepdims=True)
            probs = (exponent / total[None]).astype(BF16).reshape(512, 128)
            ctx_t = bdot(v_t, probs).astype(BF16)
            ctx_all[pl.ds(own_o + 80 * h, 80), 128 * q:128 * q + 128] = ctx_t[:80, :]

    c_start(0, 0)
    c_start(0, 1)

    def project_out(z, first=False):
        at = pl.ds(pl.multiple_of(lax.rem(z + 2 * N_TP, N_TP) * 160, 32), 160)
        for n in range(5):
            lanes = slice(256 * n, 256 * n + 256)
            term = lax.dot_general(
                ctx_all[at, :], o_all[at, lanes], (((0,), (0,)), ((), ())), preferred_element_type=F32
            )
            enc[:, lanes] = (pp[:, lanes].astype(F32) if first else enc[:, lanes]) + term

    o_on(2, 0)
    o_on(2, 1)
    o_share(1)
    project_out(t, True)
    c_on(1, 0)
    c_on(1, 1)
    w_wait("0a")
    w_start("1a")
    o_shared(0)
    project_out(t - 1)
    project_out(t + 1)
    o_on(3, 0)
    o_on(3, 1)
    o_share(2)
    c_on(2, 0)
    c_on(2, 1)
    w_wait("0b")
    w_start("1b")
    w_start("1s")
    o_shared(1)
    project_out(t - 2)
    project_out(t + 2)
    o_wait(3, 0)
    o_share(3)
    c_on(3, 0)
    c_on(3, 1)
    o_shared(2)
    e_on(1, 0)
    e_on(1, 1)
    project_out(t - 3)
    project_out(t + 3)
    o_shared(3)
    loads[9].wait()
    c_wait(3, 0)
    project_out(t + 4)

    merged = jnp.zeros((128, 1024), F32)
    for j in range(4):
        merged_in = normalize(enc[128 * j:128 * j + 128, :]).astype(BF16)
        merged += bdot(merged_in, mwb[1280 * j:1280 * j + 1280, :])
    vis[...] = merged.astype(BF16)
    e_on(2, 0)

    row_512 = iota((512, 128), 0)
    outgoing = jnp.zeros((512, 256), F32)
    for q in range(4):
        outgoing += bdot(one_hot(row_512 == target_c + 4 * q), vis[:, 256 * q:256 * q + 256])
    xs[...] = outgoing.astype(BF16)

    def send_rows(i, carry):
        to = lax.rem(s + i, N_SEQ)
        pltpu.make_async_remote_copy(
            src_ref=rows(xs, to * 16, 16), dst_ref=rows(ys, s * 16, 16),
            send_sem=as_sem.at[0], recv_sem=ar_sem.at[0], device_id=(to, t), device_id_type=MESH,
        ).start()
        return carry

    lax.fori_loop(1, N_SEQ, send_rows, 0)
    own_y = pl.ds(pl.multiple_of(s * 16, 16), 16)
    ys[own_y, :] = xs[own_y, :]
    e_on(2, 1)
    w_wait("1a")
    w_start("2a")
    e_on(3, 0)
    arrived(ys.at[pl.ds(0, 496)], ar_sem.at[0])

    row_128 = iota((128, 512), 0)
    position = iota((64, 256), 0)
    for q in range(4):
        lanes = slice(256 * q, 256 * q + 256)
        picked = bdot(one_hot((row_128 == row_n) & (((n_1 >> 2) & 3) == q)), ys[...]).astype(BF16)
        for l in range(2):
            is_text = (position.astype(F32) >= visual_rows[l:l + 1, :]) & (position < length[l])
            tok[pl.ds(own_tok + 64 * l, 64), lanes] = jnp.where(
                is_text, text[128 * l:128 * l + 64, lanes], picked[64 * l:64 * l + 64, :]
            )
    l_start(0, 0)
    l_start(0, 1)
    w_wait("1b")
    w_start("2b")
    w_start("1c")
    w_start("2s")

    loads[4].wait()
    down_sums = jnp.transpose(bdot(tok[pl.ds(own_tok, 256), :], down[...])) * tenant_mask
    dl[pl.ds(pl.multiple_of(t * 16, 16), 16), :] = jnp.sum(down_sums.reshape(8, 16, 256), axis=0)

    def send_down(i, carry):
        piece = rows(dl, t * 16, 16)
        pltpu.make_async_remote_copy(
            src_ref=piece, dst_ref=piece, send_sem=ds_sem.at[0], recv_sem=dr_sem.at[0],
            device_id=(s, lax.rem(t + i, N_TP)), device_id_type=MESH,
        ).start()
        return carry

    lax.fori_loop(1, N_TP, send_down, 0)

    near = [(0, 0), (0, -1), (0, 1), (-1, 0), (1, 0), (2, 0), (-1, -1), (-1, 1), (1, -1), (1, 1)]
    far = [(-1, 2), (1, 2), (2, -1), (2, 1), (0, 2), (2, 2)]

    def project(chips, top, size):
        for by, bx in chips:
            at = chip_at(by, bx)
            odd = lax.rem(at, 2)
            even = (1 - odd).astype(F32).astype(BF16)
            odd = odd.astype(F32).astype(BF16)
            of_z = pl.ds(pl.multiple_of(at // 2 * 256 + top, 128), size)
            x = tok[of_z, 0:512] * even + tok[of_z, 512:1024] * odd
            first = pl.multiple_of(at * 512, 512)
            for n in range(5):
                lanes = slice(256 * n, 256 * n + 256)
                acc[top:top + size, lanes] += bdot(x, w_all[pl.ds(first, 512), lanes])

    def add_squares(aheads, top):
        for ahead in aheads:
            of_z = pl.ds(pl.multiple_of(lax.rem(t + ahead + N_TP, N_TP) * 256 + top, 128), 128)
            total = squares[top:top + 128, :]
            for n in range(8):
                part = tok[of_z, 128 * n:128 * n + 128].astype(F32)
                total += part * part
            squares[top:top + 128, :] = total

    acc[...] = jnp.zeros_like(acc)
    squares[...] = jnp.zeros_like(squares)
    l_on(1, 0)
    e_wait(2, 1)
    e_wait(3, 0)
    add_squares(range(8), 128)
    l_on(1, 1)
    add_squares((0, 1, -1), 0)
    for name in ("0s", "1s"):
        w_wait(name)
    l_on(2, 0)
    w_wait("2s")
    l_on(2, 1)
    w_wait("2a")
    w_start("3a")
    add_squares((2, -2), 0)
    l_on(3, 0)
    w_wait("2b")
    w_start("3b")
    w_start("3s")
    l_on(3, 1)
    add_squares((3, -3), 0)
    for name in ("1c", "3a", "3b"):
        w_wait(name)
    w_start("4s")
    arrived(dl.at[pl.ds(0, 112)], dr_sem.at[0])
    down_t = jnp.sum(dl[...].reshape(8, 16, 256), axis=0)
    lora = jnp.transpose(jnp.concatenate([down_t] * 8, axis=0) * tenant_mask).astype(BF16)
    acc[...] += bdot(lora, up_all[...])
    l_wait(3, 0)
    add_squares((4,), 0)
    w_wait("3s")
    w_wait("4s")
    project(near, 0, 256)
    project(far, 0, 256)
    inverse = lax.rsqrt(jnp.sum(squares[...], axis=1, keepdims=True) * (1.0 / DECODER_WIDTH) + EPSILON)

    loads[5].wait()
    loads[6].wait()

    causal = iota((128, 128), 0) >= iota((128, 128), 1)
    ones = jnp.ones((128, 128), BF16)
    stores = []
    for l in range(2):
        low, high = slice(64 * l, 64 * l + 64), slice(128 + 64 * l, 192 + 64 * l)
        factor = jnp.concatenate([inverse[low, :], inverse[high, :]], axis=0)

        def column(index):
            lanes = slice(128 * index, 128 * index + 128)
            return jnp.concatenate([acc[low, lanes], acc[high, lanes]], axis=0) * factor

        def rotate(values):
            return values * cosine[...] + pltpu.roll(values, 64, 1) * sine[...]

        key_rows = rotate(column(8)).astype(BF16)
        value_rows = jnp.concatenate([column(9).astype(BF16), ones], axis=1)
        kept = iota((128, 128), 0) < length[l]
        for j in range(QUERY_PER_KEY):
            query = rotate(column(j)).astype(BF16)
            scores = bdot_nt(query, key_rows) * (1.0 / math.sqrt(DECODER_HEAD_DIM))
            scores = jnp.where(causal, scores, -1e30)
            exponent = jnp.exp(scores - jnp.max(scores, axis=1, keepdims=True)).astype(BF16)
            summed = bdot(exponent, value_rows)
            res[128 * l:128 * l + 128, 128 * j:128 * j + 128] = jnp.where(
                kept, summed[:, :128] / summed[:, 128:], 0.0
            ).astype(BF16)
        stores.append(pltpu.make_async_copy(
            res.at[pl.ds(128 * l, 128)], out.at[pl.ds(128 * l, 128)], load_sem.at[10 + l]
        ))
        stores[l].start()

    for store in stores:
        store.wait()
    g_sent()
    w_sent()
    e_sent()
    l_sent()
    o_sent()
    c_sent()
    arrived(o_all.at[pl.ds(0, 560)], ofs_sem.at[0])
    arrived(xs.at[pl.ds(0, 496)], as_sem.at[0])
    arrived(dl.at[pl.ds(0, 112)], ds_sem.at[0])


def on_device(
    patches, vit_qkv, vit_out, merge_weight, query_key_value_weight, adapter_down, adapter_up_weight,
    text_embed, vis_count, image_session, session_slot, session_tenant, session_len,
):
    operands = (
        session_slot, session_tenant, session_len, vis_count.reshape(8, 128), image_session.reshape(8, 128),
        vit_qkv, vit_out.T, patches.reshape(512, DV), merge_weight,
        jnp.transpose(query_key_value_weight.reshape(256, 10, 128), (1, 0, 2)), adapter_down,
        jnp.transpose(adapter_up_weight.reshape(128, 10, 128), (1, 0, 2)), text_embed,
    ) + tables()
    vmem = pl.BlockSpec(memory_space=pltpu.VMEM)
    smem = pl.BlockSpec(memory_space=pltpu.SMEM)
    hbm = pl.BlockSpec(memory_space=pl.ANY)
    dma = pltpu.SemaphoreType.DMA
    return pl.pallas_call(
        kernel,
        out_shape=jax.ShapeDtypeStruct((256, 1024), BF16),
        in_specs=[smem if i < 3 else vmem if i < 7 else hbm for i in range(len(operands))],
        out_specs=hbm,
        scratch_shapes=[
            pltpu.VMEM((512, 1280), BF16),
            pltpu.VMEM((1024, 128), BF16),
            pltpu.VMEM((256, 1024), BF16),
            pltpu.VMEM((512, 512), BF16),
            pltpu.VMEM((512, 768), BF16),
            pltpu.VMEM((128, 128), F32),
            pltpu.VMEM((128, 128), F32),
            pltpu.VMEM((10, 256, 128), BF16),
            pltpu.VMEM((10, 128, 128), BF16),
            pltpu.VMEM((1536, LANES[0]), BF16),
            pltpu.VMEM((1536, LANES[1]), BF16),
            pltpu.VMEM((320, 640), F32),
            pltpu.VMEM((1280, 640), BF16),
            pltpu.VMEM((512, 1280), BF16),
            pltpu.VMEM((512, 1280), BF16),
            pltpu.VMEM((512, 512), BF16),
            pltpu.VMEM((1280, 1280), BF16),
            pltpu.VMEM((1280, 512), BF16),
            pltpu.VMEM((512, 1280), F32),
            pltpu.VMEM((5120, 1024), BF16),
            pltpu.VMEM((128, 1024), BF16),
            pltpu.VMEM((512, 256), BF16),
            pltpu.VMEM((512, 256), BF16),
            pltpu.VMEM((2048, 1024), BF16),
            pltpu.VMEM((128, 256), F32),
            pltpu.VMEM((8192, 1280), BF16),
            pltpu.VMEM((128, 1280), BF16),
            pltpu.VMEM((256, 1280), F32),
            pltpu.VMEM((256, 128), F32),
            pltpu.VMEM((256, 1024), BF16),
            dma((12,)), dma((2,)), dma((8,)), dma((2,)), dma((2,)), dma((len(W_GROUPS),)), dma((len(W_GROUPS),)),
            dma((1,)), dma((8,)), dma((1,)), dma((4,)),
            dma((1,)), dma((8,)), dma((1,)), dma((8,)), dma((1,)), dma((8,)),
            dma((1,)), dma((1,)), dma((1,)), dma((1,)),
        ],
        compiler_params=pltpu.CompilerParams(
            collective_id=0, has_side_effects=True, vmem_limit_bytes=64 * 1024 * 1024
        ),
    )(*operands).astype(F32)


def solution(mesh):
    placed = (
        P("seq", None, None),
        P(None, "seq", "tp"),
        P("tp", "seq"),
        P(None, "tp"),
        P("seq", "tp", None, None),
        P("tp", None),
        P(None, "tp", None, None),
        P("seq", "tp"),
        P(),
        P(),
        P(),
        P(),
        P(),
    )
    return jax.shard_map(
        on_device, mesh=mesh, in_specs=placed, out_specs=P("seq", "tp"), check_vma=False
    )
```

```python
import functools
import math

import jax
import jax.numpy as jnp
import numpy as np
from jax import lax
from jax.experimental import pallas as pl
from jax.experimental.pallas import tpu as pltpu
from jax.sharding import PartitionSpec as P

DV = 1280
HV = 16
HEAD = 80
DECODER_WIDTH = 8192
DECODER_HEAD_DIM = 128
ADAPTER_RANK = 16
IMG_DEV = 32
VMAX = 4
SLOT = 128
QUERY_PER_KEY = 8
N_SEQ = 32
N_TP = 8
COLS = 1280
EPSILON = 1e-06
ROPE_BASE = 1000000.0
MESH = pl.DeviceIdType.MESH
F32 = jnp.float32
BF16 = jnp.bfloat16


def tables():
    perm = np.zeros((512, 512), np.float32)
    for j in range(4):
        for i in range(32):
            for m in range(4):
                perm[j * 128 + i * 4 + m, i * 16 + m * 4 + j] = 1
    select = np.zeros((512, 768), np.float32)
    for group in range(6):
        for lane in range(HEAD):
            select[32 + group * HEAD + lane, group * 128 + lane] = 1
    half = DECODER_HEAD_DIM // 2
    inverse_freq = np.power(
        np.float32(ROPE_BASE), -(np.arange(half, dtype=np.float32) * 2.0 / DECODER_HEAD_DIM)
    ).astype(np.float32)
    angles = np.arange(SLOT, dtype=np.float32)[:, None] * inverse_freq[None, :]
    cosine = np.cos(angles).astype(np.float32)
    sine = np.sin(angles).astype(np.float32)
    return (
        jnp.asarray(perm, BF16),
        jnp.asarray(select, BF16),
        jnp.asarray(np.concatenate([cosine, cosine], 1)),
        jnp.asarray(np.concatenate([-sine, sine], 1)),
    )


def plane_copies():
    part_a, part_b = (0, 128), (128, 128)

    def sib(blocks):
        return [(by, bx, 0, 256, 0, 0, True) for by, bx in blocks]

    def go(by, bx, part, ty, tx):
        return (by, bx, part[0], part[1], ty, tx, False)

    sides = (-1, 1)
    near = [(0, -1), (0, 1), (-1, 0), (1, 0)]
    lists = {
        "0a": [go(0, 0, part_a, ty, tx) for ty, tx in near],
        "0b": [go(0, 0, part_b, ty, tx) for ty, tx in near],
        "0s": sib([(0, 0)]),
        "1a": [go(0, -1, part_a, 0, 1), go(-1, 0, part_a, 1, 0)]
        + [go(0, side, part_a, to, 0) for side in sides for to in sides],
        "1b": [go(1, 0, part_b, -1, 0)]
        + [go(side, 0, part_b, 0, to) for side in sides for to in sides],
        "1c": [go(0, 1, (128, 64), 0, -1), go(0, -1, (192, 64), 0, 1)],
        "1s": sib(near),
        "2a": [go(0, 2, part_a, 1, 0), go(0, 2, part_a, -1, 0), go(-1, 1, part_a, 1, 0), go(1, -1, part_a, -1, 0)],
        "2b": [go(2, 0, part_b, 0, 1), go(2, 0, part_b, 0, -1), go(1, -1, part_b, 0, 1), go(-1, 1, part_b, 0, -1)],
        "2s": sib([(2, 0), (-1, -1), (-1, 1), (1, -1), (1, 1)]),
        "3a": [go(-1, 2, (0, 64), 1, 0), go(1, 2, (64, 64), -1, 0)],
        "3b": [go(2, -1, (128, 64), 0, 1), go(2, 1, (192, 64), 0, -1)],
        "3s": sib([(-1, 2), (1, 2), (2, -1), (2, 1)]),
        "4s": sib([(0, 2), (2, 2)]),
    }
    return {
        name: (i, sum(entry[3] for entry in entries), entries) for i, (name, entries) in enumerate(lists.items())
    }


W_GROUPS = plane_copies()
NEAR = [(0, 0), (0, 3), (0, 1), (3, 0), (1, 0), (2, 0), (3, 3), (3, 1), (1, 3), (1, 1)]
FAR = [(3, 2), (1, 2), (2, 3), (2, 1), (0, 2), (2, 2)]
LANES = (256, 384)


def bdot(a, b):
    return jnp.dot(a, b, preferred_element_type=F32)


def bdot_nt(a, b):
    return lax.dot_general(a, b, (((1,), (1,)), ((), ())), preferred_element_type=F32)


def normalize(values):
    mean_val = jnp.mean(values, axis=-1, keepdims=True)
    centered = values - mean_val
    variance = jnp.mean(centered * centered, axis=-1, keepdims=True)
    return centered * lax.rsqrt(variance + EPSILON)


def iota(shape, axis):
    return lax.broadcasted_iota(jnp.int32, shape, axis)


def one_hot(mask):
    return mask.astype(F32).astype(BF16)


def kernel(
    slot_ref, tenant_ref, len_ref, counts, sessions, vit_qkv, vit_out,
    patches_hbm, mw, w, down_hbm, up, text_hbm, perm_hbm, select_hbm, cosine_hbm, sine_hbm,
    out,
    patches, down, text, perm, select, cosine, sine, w_in, up_in,
    g0, g1, wf, wall, pp, ln, qkv, o_all, ctx_all, enc, mwb, vis, xs, ys, tok_l, tok_e, dl, w_near, w_far, up_all, acc, squares, res,
    load_sem, gs_sem, gr_sem, fs_sem, fr_sem, ws_sem, wr_sem,
    os_sem, or_sem, ofs_sem, ofr_sem, cs_sem, cr_sem, es_sem, er_sem, ls_sem, lr_sem,
    as_sem, ar_sem, ds_sem, dr_sem,
):
    s = lax.axis_index("seq")
    t = lax.axis_index("tp")
    core = lax.rem(s, 2)
    chip = s // 2
    cx = lax.rem(chip, 4)
    cy = chip // 4
    sibling = s + 1 - 2 * core

    def chip_at(dy, dx):
        return lax.rem(cy + (dy + 4), 4) * 4 + lax.rem(cx + (dx + 4), 4)

    def rows(ref, start, size, step=16):
        return ref.at[pl.ds(pl.multiple_of(start, step), size)]

    def arrived(ref, sem):
        pltpu.make_async_copy(ref, ref, sem).wait()

    barrier = pltpu.get_barrier_semaphore()

    def greet_seq(i, carry):
        pl.semaphore_signal(barrier, inc=1, device_id=(lax.rem(s + i, N_SEQ), t), device_id_type=MESH)
        return carry

    def greet_tp(i, carry):
        pl.semaphore_signal(barrier, inc=1, device_id=(s, lax.rem(t + i, N_TP)), device_id_type=MESH)
        return carry

    lax.fori_loop(1, N_SEQ, greet_seq, 0)
    lax.fori_loop(1, N_TP, greet_tp, 0)

    loads = [
        pltpu.make_async_copy(source, to, load_sem.at[i])
        for i, (source, to) in enumerate(
            (
                (perm_hbm, perm), (patches_hbm, patches), (text_hbm, text), (select_hbm, select), (down_hbm, down),
                (cosine_hbm, cosine), (sine_hbm, sine), (w, w_in), (up, up_in), (mw, mwb),
            )
        )
    ]
    for load in loads:
        load.start()
    g_of = (g0, g1)

    def g_ref(c, at, blocks, phase):
        return rows(g_of[phase], (c * 16 + at) * 48, 48 * blocks)

    def g_start(phase):
        for dx, dy in ((2, 2), (1, 2), (2, 1), (3, 2), (2, 3), (1, 1), (3, 3), (1, 3), (3, 1), (2, 0), (0, 2), (1, 0), (0, 1), (3, 0), (0, 3)):
            piece = g_ref(core, chip, 1, phase)
            pltpu.make_async_remote_copy(
                src_ref=piece, dst_ref=piece, send_sem=gs_sem.at[phase], recv_sem=gr_sem.at[4 * phase + (4 - dy) % 4],
                device_id=(chip_at(dy, dx) * 2 + core, t), device_id_type=MESH,
            ).start()

    def g_row_of_chips(c, d, phase):
        return g_ref(c, lax.rem(cy + d, 4) * 4, 4, phase)

    def g_share(phase, groups):
        for d in groups:
            group = g_row_of_chips(core, d, phase)
            arrived(g_of[phase].at[pl.ds(0, 192 if d > 0 else 144)], gr_sem.at[4 * phase + d])
            pltpu.make_async_remote_copy(
                src_ref=group, dst_ref=group, send_sem=fs_sem.at[phase], recv_sem=fr_sem.at[phase],
                device_id=(sibling, t), device_id_type=MESH,
            ).start()

    def g_shared(phase, sems):
        arrived(g_of[phase].at[pl.ds(0, 768)], sems.at[phase])

    def g_sent():
        for phase in range(2):
            arrived(g_of[phase].at[pl.ds(0, 720)], gs_sem.at[phase])
            g_shared(phase, fs_sem)

    def w_ref(c, by, bx, first, size):
        place = (by % 4, bx % 4)
        buf, order = (w_near, NEAR) if place in NEAR else (w_far, FAR)
        return rows(buf, order.index(place) * 512 + c * 256 + first, size)

    def w_start(name):
        group, total, entries = W_GROUPS[name]
        for by, bx, first, size, ty, tx, sib in entries:
            pltpu.make_async_remote_copy(
                src_ref=w_ref(core, by, bx, first, size), dst_ref=w_ref(core, by - ty, bx - tx, first, size),
                send_sem=ws_sem.at[group], recv_sem=wr_sem.at[group],
                device_id=(sibling if sib else chip_at(ty, tx) * 2 + core, t), device_id_type=MESH,
            ).start()

    def w_wait(name):
        group, total, entries = W_GROUPS[name]
        arrived(w_near.at[pl.ds(0, total)], wr_sem.at[group])

    def w_sent():
        for group, total, entries in W_GROUPS.values():
            arrived(w_near.at[pl.ds(0, total)], ws_sem.at[group])

    right = (s, lax.rem(t + 1, N_TP))
    left = (s, lax.rem(t + N_TP - 1, N_TP))

    def ring(buf, base, size, cut, send, recv, crossed):
        def piece(origin, j):
            first = base(lax.rem(origin + 2 * N_TP, N_TP))
            return rows(buf, first + cut * j, cut if j == 0 else size - cut)

        def ways(k, j):
            both = [(0, j), (1, 1 - j if crossed else j)]
            return both if k < 3 else [(way, part) for way, part in both if part == way]

        def start(k, j):
            for way, part in ways(k, j):
                block = piece(t - k if way == 0 else t + k, part)
                pltpu.make_async_remote_copy(
                    src_ref=block, dst_ref=block, send_sem=send.at[0], recv_sem=recv.at[k * 2 + j],
                    device_id=(right, left)[way], device_id_type=MESH,
                ).start()

        def wait(k, j):
            total = sum((cut, size - cut)[part] for way, part in ways(k, j))
            if total > 0:
                arrived(buf.at[pl.ds(0, total)], recv.at[k * 2 + j])

        def on(k, j):
            wait(k - 1, j)
            start(k, j)

        def sent():
            arrived(buf.at[pl.ds(0, 7 * size)], send.at[0])

        return start, wait, on, sent

    e_start, e_wait, e_on, e_sent = ring(tok_e, lambda z: z * 128, 128, 64, es_sem, er_sem, True)
    l_start, l_wait, l_on, l_sent = ring(tok_l, lambda z: z * 128, 128, 64, ls_sem, lr_sem, True)
    o_start, o_wait, o_on, o_sent = ring(o_all, lambda z: z * 160 + 80 * core, 80, 48, os_sem, or_sem, True)
    c_start, c_wait, c_on, c_sent = ring(ctx_all, lambda z: z * 160, 160, 80, cs_sem, cr_sem, True)

    def o_share(k):
        for origin in (t - 1 - k, t + 1 + k) if k < 3 else (t + 4,):
            piece = rows(o_all, lax.rem(origin + 2 * N_TP, N_TP) * 160 + 80 * core, 80)
            pltpu.make_async_remote_copy(
                src_ref=piece, dst_ref=piece, send_sem=ofs_sem.at[0], recv_sem=ofr_sem.at[k],
                device_id=(sibling, t), device_id_type=MESH,
            ).start()

    def o_shared(k):
        arrived(o_all.at[pl.ds(0, 160 if k < 3 else 80)], ofr_sem.at[k])

    r_640, c_640 = iota((160, 640), 0), iota((160, 640), 1)
    mine = bdot(vit_out[...], one_hot(c_640 == r_640))
    for j in range(3):
        mine += bdot(vit_qkv[j], one_hot(c_640 == r_640 + 160 * (j + 1)))
    own_g = pl.ds(pl.multiple_of((core * 16 + chip) * 48, 16), 48)
    mine = jnp.concatenate([mine, jnp.zeros((8, 640), F32)], axis=0).astype(BF16)
    g0[own_g, :] = mine[:, :256]
    g1[own_g, :] = mine[:, 256:]

    def look_up(k, carry):
        slots, len0, len1, tenant0, tenant1 = carry
        slot = slot_ref[k]
        slots = jnp.where(sessions[...] == k, slot, slots)
        at0, at1 = slot == 2 * s, slot == 2 * s + 1
        return (
            slots, jnp.where(at0, len_ref[k], len0), jnp.where(at1, len_ref[k], len1),
            jnp.where(at0, tenant_ref[k], tenant0), jnp.where(at1, tenant_ref[k], tenant1),
        )

    zero = jnp.int32(0)
    slots, len0, len1, tenant0, tenant1 = lax.fori_loop(
        0, 64, look_up, (jnp.zeros((8, 128), jnp.int32), zero, zero, zero, zero)
    )
    length = (len0, len1)

    loads[7].wait()
    own_w = pl.ds(pl.multiple_of(core * 256, 256), 256)
    for j in range(10):
        w_near[own_w, 128 * j:128 * j + 128] = w_in[j]
    loads[8].wait()
    for j in range(10):
        up_all[:, 128 * j:128 * j + 128] = up_in[j]

    pl.semaphore_wait(barrier, N_SEQ + N_TP - 2)
    g_start(0)

    own_tok = pl.multiple_of(t * 128, 128)
    loads[2].wait()
    for l in range(2):
        tok_e[pl.ds(own_tok + 64 * l, 64), :] = jnp.where(
            iota((64, 1024), 0) + 64 < length[l], text[128 * l + 64:128 * l + 128, :], jnp.zeros((64, 1024), BF16)
        )
    e_start(0, 0)
    e_start(0, 1)

    loads[0].wait()
    loads[1].wait()
    for n in range(5):
        lanes = slice(256 * n, 256 * n + 256)
        pp[:, lanes] = bdot(perm[...], patches[:, lanes]).astype(BF16)
    for r in range(4):
        part = slice(128 * r, 128 * r + 128)
        ln[part, :] = normalize(pp[part, :].astype(F32)).astype(BF16)

    here = (slots >> 1) == s
    folded = jnp.concatenate(
        [jnp.where(here, counts[...], 0).astype(F32), jnp.where(here, slots & 1, 0).astype(F32)], axis=0
    ).astype(BF16)
    spread = bdot(folded, one_hot((iota((128, 512), 0) >> 5) == ((iota((128, 512), 1) >> 4) & 3)))
    n_8 = iota((8, 512), 1)
    own_row = iota((8, 512), 0) == (n_8 >> 6)
    count_n = jnp.sum(jnp.where(own_row, spread[:8, :], 0.0), axis=0, keepdims=True)
    place_n = jnp.sum(jnp.where(own_row, spread[8:, :], 0.0), axis=0, keepdims=True)
    by_place = jnp.where(iota((8, 512), 0) == place_n.astype(jnp.int32), count_n, 0.0)
    n_from, n_to = iota((512, 512), 0), iota((512, 512), 1)
    before = bdot(by_place.astype(BF16), one_hot(((n_from & 15) == 0) & ((n_from >> 4) < (n_to >> 4))))
    offset_n = jnp.where(place_n > 0.5, before[1:2, :], before[0:1, :])
    visual_rows = jnp.sum(by_place, axis=1, keepdims=True) * (1.0 / 16.0)
    n_1 = n_8[0:1, :]
    row_n = jnp.where(
        (n_1 & 3).astype(F32) < count_n, place_n * 64.0 + offset_n + (n_1 & 3).astype(F32), -1.0
    ).astype(jnp.int32)

    lane_8 = iota((128, 128), 1)
    encoded_here = bdot(
        jnp.concatenate([slots.astype(F32), counts[...].astype(F32)], axis=0).astype(BF16),
        one_hot(iota((128, 128), 0) == lax.rem(s, 4) * 32 + (lane_8 >> 2)),
    )
    own_row = iota((8, 128), 0) == s // 4
    slot_c = jnp.sum(jnp.where(own_row, encoded_here[:8, :], 0.0), axis=0, keepdims=True).astype(jnp.int32)
    count_c = jnp.sum(jnp.where(own_row, encoded_here[8:, :], 0.0), axis=0, keepdims=True).astype(jnp.int32)
    target_c = (slot_c >> 1) * 16 + (lane_8[0:1, :] & 3)
    key_8 = iota((128, 128), 0)
    bias = jnp.where(((key_8 >> 2) == (lane_8 >> 2)) & ((key_8 & 3) < count_c), 0.0, -1e30)
    tenant_mask = (
        (iota((128, 256), 0) >> 4) == jnp.where((iota((128, 256), 1) & 64) == 0, tenant0, tenant1)
    ).astype(F32)

    g_share(0, (2, 3, 1, 0))
    g_start(1)
    g_shared(0, fr_sem)

    def unpack(phase):
        lanes = slice(256 * phase, 256 * phase + LANES[phase])
        for c in range(4):
            for b in range(8):
                first = ((b % 2) * 16 + 4 * c + b // 2) * 48
                wf[40 * b:40 * b + 40, lanes] = g_of[phase][first:first + 48, :].astype(F32)[:40, :]
            wall[320 * c:320 * c + 320, lanes] = wf[:, lanes].astype(BF16)

    unpack(0)
    own_o = pl.multiple_of(t * 160, 32)
    pick = one_hot(iota((160, 256), 0) == iota((160, 256), 1))
    for r in range(5):
        part = slice(256 * r, 256 * r + 256)
        o_all[pl.ds(own_o, 160), part] = bdot_nt(pick, wall[part, 0:256]).astype(BF16)
    o_start(0, 0)
    o_start(0, 1)

    g_share(1, (2, 3))
    w_start("0a")
    w_start("0b")
    w_start("0s")
    g_share(1, (1, 0))
    o_on(1, 0)
    g_shared(1, fr_sem)
    unpack(1)
    o_on(1, 1)
    o_share(0)
    for n in range(2):
        lanes = slice(256 * n, 256 * n + 256)
        qkv[:, lanes] = bdot(ln[...], wall[:, 128 + 256 * n:384 + 256 * n]).astype(BF16)
    loads[3].wait()
    scale = 1.0 / math.sqrt(HEAD)
    for h in range(2):
        q_h = bdot(qkv[...], select[:, 128 * h:128 * h + 128]).astype(BF16)
        k_h = bdot(qkv[...], select[:, 256 + 128 * h:384 + 128 * h]).astype(BF16)
        v_h = bdot(qkv[...], select[:, 512 + 128 * h:640 + 128 * h])
        v_t = jnp.transpose(v_h).astype(BF16)
        for q in range(4):
            scores = bdot_nt(k_h, q_h[128 * q:128 * q + 128, :]) * scale
            scores = scores.reshape(4, 128, 128) + bias[None]
            largest = jnp.max(jnp.max(scores, axis=0), axis=0, keepdims=True)
            exponent = jnp.exp(scores - largest[None])
            total = jnp.sum(jnp.sum(exponent, axis=0), axis=0, keepdims=True)
            probs = (exponent / total[None]).astype(BF16).reshape(512, 128)
            ctx_t = bdot(v_t, probs).astype(BF16)
            ctx_all[pl.ds(own_o + 80 * h, 80), 128 * q:128 * q + 128] = ctx_t[:80, :]

    c_start(0, 0)
    c_start(0, 1)

    def project_out(z, first=False):
        at = pl.ds(pl.multiple_of(lax.rem(z + 2 * N_TP, N_TP) * 160, 32), 160)
        for n in range(5):
            lanes = slice(256 * n, 256 * n + 256)
            term = lax.dot_general(
                ctx_all[at, :], o_all[at, lanes], (((0,), (0,)), ((), ())), preferred_element_type=F32
            )
            enc[:, lanes] = (pp[:, lanes].astype(F32) if first else enc[:, lanes]) + term

    o_on(2, 0)
    o_on(2, 1)
    o_share(1)
    project_out(t, True)
    c_on(1, 0)
    c_on(1, 1)
    w_wait("0a")
    w_start("1a")
    o_shared(0)
    project_out(t - 1)
    project_out(t + 1)
    o_on(3, 0)
    o_on(3, 1)
    o_share(2)
    c_on(2, 0)
    c_on(2, 1)
    w_wait("0b")
    w_start("1b")
    w_start("1s")
    o_shared(1)
    project_out(t - 2)
    project_out(t + 2)
    o_wait(3, 0)
    o_share(3)
    c_on(3, 0)
    c_on(3, 1)
    o_shared(2)
    e_on(1, 0)
    e_on(1, 1)
    project_out(t - 3)
    project_out(t + 3)
    o_shared(3)
    loads[9].wait()
    c_wait(3, 0)
    project_out(t + 4)

    merged = jnp.zeros((128, 1024), F32)
    for j in range(4):
        merged_in = normalize(enc[128 * j:128 * j + 128, :]).astype(BF16)
        merged += bdot(merged_in, mwb[1280 * j:1280 * j + 1280, :])
    vis[...] = merged.astype(BF16)
    e_on(2, 0)

    row_512 = iota((512, 128), 0)
    outgoing = jnp.zeros((512, 256), F32)
    for q in range(4):
        outgoing += bdot(one_hot(row_512 == target_c + 4 * q), vis[:, 256 * q:256 * q + 256])
    xs[...] = outgoing.astype(BF16)

    def send_rows(i, carry):
        to = lax.rem(s + i, N_SEQ)
        pltpu.make_async_remote_copy(
            src_ref=rows(xs, to * 16, 16), dst_ref=rows(ys, s * 16, 16),
            send_sem=as_sem.at[0], recv_sem=ar_sem.at[0], device_id=(to, t), device_id_type=MESH,
        ).start()
        return carry

    lax.fori_loop(1, N_SEQ, send_rows, 0)
    own_y = pl.ds(pl.multiple_of(s * 16, 16), 16)
    ys[own_y, :] = xs[own_y, :]
    e_on(2, 1)
    w_wait("1a")
    w_start("2a")
    e_on(3, 0)
    arrived(ys.at[pl.ds(0, 496)], ar_sem.at[0])

    row_128 = iota((128, 512), 0)
    position = iota((64, 256), 0)
    for q in range(4):
        lanes = slice(256 * q, 256 * q + 256)
        picked = bdot(one_hot((row_128 == row_n) & (((n_1 >> 2) & 3) == q)), ys[...]).astype(BF16)
        for l in range(2):
            is_text = (position.astype(F32) >= visual_rows[l:l + 1, :]) & (position < length[l])
            tok_l[pl.ds(own_tok + 64 * l, 64), lanes] = jnp.where(
                is_text, text[128 * l:128 * l + 64, lanes], picked[64 * l:64 * l + 64, :]
            )
    l_start(0, 0)
    l_start(0, 1)
    w_wait("1b")
    w_start("2b")
    w_start("1c")
    w_start("2s")

    loads[4].wait()
    own_rows = jnp.concatenate([tok_l[pl.ds(own_tok, 128), :], tok_e[pl.ds(own_tok, 128), :]], axis=0)
    down_sums = jnp.transpose(bdot(own_rows, down[...])) * tenant_mask
    dl[pl.ds(pl.multiple_of(t * 16, 16), 16), :] = jnp.sum(down_sums.reshape(8, 16, 256), axis=0)

    def send_down(i, carry):
        piece = rows(dl, t * 16, 16)
        pltpu.make_async_remote_copy(
            src_ref=piece, dst_ref=piece, send_sem=ds_sem.at[0], recv_sem=dr_sem.at[0],
            device_id=(s, lax.rem(t + i, N_TP)), device_id_type=MESH,
        ).start()
        return carry

    lax.fori_loop(1, N_TP, send_down, 0)

    def project(chips, late, early):
        tops = [top for top, due in ((0, late), (128, early)) if due]
        buf, order = (w_near, NEAR) if chips[0] in NEAR else (w_far, FAR)
        for by, bx in chips:
            at = chip_at(by, bx)
            odd = lax.rem(at, 2)
            even = (1 - odd).astype(F32).astype(BF16)
            odd = odd.astype(F32).astype(BF16)
            of_z = pl.ds(pl.multiple_of(at // 2 * 128, 128), 128)
            parts = [(tok_l, tok_e)[top // 128] for top in tops]
            parts = [part[of_z, 0:512] * even + part[of_z, 512:1024] * odd for part in parts]
            x = jnp.concatenate(parts, axis=0) if len(parts) > 1 else parts[0]
            rows_of = slice(tops[0], tops[-1] + 128)
            first = order.index((by, bx)) * 512
            for n in range(5):
                lanes = slice(256 * n, 256 * n + 256)
                acc[rows_of, lanes] += bdot(x, buf[first:first + 512, lanes])

    def add_squares(aheads, tok, top):
        for ahead in aheads:
            of_z = pl.ds(pl.multiple_of(lax.rem(t + ahead + N_TP, N_TP) * 128, 128), 128)
            total = squares[top:top + 128, :]
            for n in range(8):
                part = tok[of_z, 128 * n:128 * n + 128].astype(F32)
                total += part * part
            squares[top:top + 128, :] = total

    acc[...] = jnp.zeros_like(acc)
    squares[...] = jnp.zeros_like(squares)
    l_on(1, 0)
    e_wait(2, 1)
    e_wait(3, 0)
    add_squares(range(8), tok_e, 128)
    l_on(1, 1)
    add_squares((0, 1, -1), tok_l, 0)
    for name in ("0s", "1s"):
        w_wait(name)
    project(NEAR[:5], False, True)
    l_on(2, 0)
    w_wait("2s")
    project(NEAR[5:], False, True)
    l_on(2, 1)
    w_wait("2a")
    w_start("3a")
    add_squares((2, -2), tok_l, 0)
    l_on(3, 0)
    w_wait("2b")
    w_start("3b")
    w_start("3s")
    l_on(3, 1)
    add_squares((3, -3), tok_l, 0)
    for name in ("1c", "3a", "3b"):
        w_wait(name)
    w_start("4s")
    arrived(dl.at[pl.ds(0, 112)], dr_sem.at[0])
    down_t = jnp.sum(dl[...].reshape(8, 16, 256), axis=0)
    lora = jnp.transpose(jnp.concatenate([down_t] * 8, axis=0) * tenant_mask).astype(BF16)
    acc[...] += bdot(lora, up_all[...])
    l_wait(3, 0)
    add_squares((4,), tok_l, 0)
    project(NEAR, True, False)
    w_wait("3s")
    w_wait("4s")
    project(FAR, True, True)
    inverse = lax.rsqrt(jnp.sum(squares[...], axis=1, keepdims=True) * (1.0 / DECODER_WIDTH) + EPSILON)

    loads[5].wait()
    loads[6].wait()

    causal = iota((128, 128), 0) >= iota((128, 128), 1)
    ones = jnp.ones((128, 128), BF16)
    stores = []
    for l in range(2):
        low, high = slice(64 * l, 64 * l + 64), slice(128 + 64 * l, 192 + 64 * l)
        factor = jnp.concatenate([inverse[low, :], inverse[high, :]], axis=0)

        def column(index):
            lanes = slice(128 * index, 128 * index + 128)
            return jnp.concatenate([acc[low, lanes], acc[high, lanes]], axis=0) * factor

        def rotate(values):
            return values * cosine[...] + pltpu.roll(values, 64, 1) * sine[...]

        key_rows = rotate(column(8)).astype(BF16)
        value_rows = jnp.concatenate([column(9).astype(BF16), ones], axis=1)
        kept = iota((128, 128), 0) < length[l]
        for j in range(QUERY_PER_KEY):
            query = rotate(column(j)).astype(BF16)
            scores = bdot_nt(query, key_rows) * (1.0 / math.sqrt(DECODER_HEAD_DIM))
            scores = jnp.where(causal, scores, -1e30)
            exponent = jnp.exp(scores - jnp.max(scores, axis=1, keepdims=True)).astype(BF16)
            summed = bdot(exponent, value_rows)
            res[128 * l:128 * l + 128, 128 * j:128 * j + 128] = jnp.where(
                kept, summed[:, :128] / summed[:, 128:], 0.0
            ).astype(BF16)
        stores.append(pltpu.make_async_copy(
            res.at[pl.ds(128 * l, 128)], out.at[pl.ds(128 * l, 128)], load_sem.at[10 + l]
        ))
        stores[l].start()

    for store in stores:
        store.wait()
    g_sent()
    w_sent()
    e_sent()
    l_sent()
    o_sent()
    c_sent()
    arrived(o_all.at[pl.ds(0, 560)], ofs_sem.at[0])
    arrived(xs.at[pl.ds(0, 496)], as_sem.at[0])
    arrived(dl.at[pl.ds(0, 112)], ds_sem.at[0])


def on_device(
    patches, vit_qkv, vit_out, merge_weight, query_key_value_weight, adapter_down, adapter_up_weight,
    text_embed, vis_count, image_session, session_slot, session_tenant, session_len,
):
    operands = (
        session_slot, session_tenant, session_len, vis_count.reshape(8, 128), image_session.reshape(8, 128),
        vit_qkv, vit_out.T, patches.reshape(512, DV), merge_weight,
        jnp.transpose(query_key_value_weight.reshape(256, 10, 128), (1, 0, 2)), adapter_down,
        jnp.transpose(adapter_up_weight.reshape(128, 10, 128), (1, 0, 2)), text_embed,
    ) + tables()
    vmem = pl.BlockSpec(memory_space=pltpu.VMEM)
    smem = pl.BlockSpec(memory_space=pltpu.SMEM)
    hbm = pl.BlockSpec(memory_space=pl.ANY)
    dma = pltpu.SemaphoreType.DMA
    return pl.pallas_call(
        kernel,
        out_shape=jax.ShapeDtypeStruct((256, 1024), BF16),
        in_specs=[smem if i < 3 else vmem if i < 7 else hbm for i in range(len(operands))],
        out_specs=hbm,
        scratch_shapes=[
            pltpu.VMEM((512, 1280), BF16),
            pltpu.VMEM((1024, 128), BF16),
            pltpu.VMEM((256, 1024), BF16),
            pltpu.VMEM((512, 512), BF16),
            pltpu.VMEM((512, 768), BF16),
            pltpu.VMEM((128, 128), F32),
            pltpu.VMEM((128, 128), F32),
            pltpu.VMEM((10, 256, 128), BF16),
            pltpu.VMEM((10, 128, 128), BF16),
            pltpu.VMEM((1536, LANES[0]), BF16),
            pltpu.VMEM((1536, LANES[1]), BF16),
            pltpu.VMEM((320, 640), F32),
            pltpu.VMEM((1280, 640), BF16),
            pltpu.VMEM((512, 1280), BF16),
            pltpu.VMEM((512, 1280), BF16),
            pltpu.VMEM((512, 512), BF16),
            pltpu.VMEM((1280, 1280), BF16),
            pltpu.VMEM((1280, 512), BF16),
            pltpu.VMEM((512, 1280), F32),
            pltpu.VMEM((5120, 1024), BF16),
            pltpu.VMEM((128, 1024), BF16),
            pltpu.VMEM((512, 256), BF16),
            pltpu.VMEM((512, 256), BF16),
            pltpu.VMEM((1024, 1024), BF16),
            pltpu.VMEM((1024, 1024), BF16),
            pltpu.VMEM((128, 256), F32),
            pltpu.VMEM((5120, 1280), BF16),
            pltpu.VMEM((3072, 1280), BF16),
            pltpu.VMEM((128, 1280), BF16),
            pltpu.VMEM((256, 1280), F32),
            pltpu.VMEM((256, 128), F32),
            pltpu.VMEM((256, 1024), BF16),
            dma((12,)), dma((2,)), dma((8,)), dma((2,)), dma((2,)), dma((len(W_GROUPS),)), dma((len(W_GROUPS),)),
            dma((1,)), dma((8,)), dma((1,)), dma((4,)),
            dma((1,)), dma((8,)), dma((1,)), dma((8,)), dma((1,)), dma((8,)),
            dma((1,)), dma((1,)), dma((1,)), dma((1,)),
        ],
        compiler_params=pltpu.CompilerParams(
            collective_id=0, has_side_effects=True, vmem_limit_bytes=64 * 1024 * 1024
        ),
    )(*operands).astype(F32)


def solution(mesh):
    placed = (
        P("seq", None, None),
        P(None, "seq", "tp"),
        P("tp", "seq"),
        P(None, "tp"),
        P("seq", "tp", None, None),
        P("tp", None),
        P(None, "tp", None, None),
        P("seq", "tp"),
        P(),
        P(),
        P(),
        P(),
        P(),
    )
    return jax.shard_map(
        on_device, mesh=mesh, in_specs=placed, out_specs=P("seq", "tp"), check_vma=False
    )
```

```python
import functools
import math

import jax
import jax.numpy as jnp
import numpy as np
from jax import lax
from jax.experimental import pallas as pl
from jax.experimental.pallas import tpu as pltpu
from jax.sharding import PartitionSpec as P

DV = 1280
HV = 16
HEAD = 80
DECODER_WIDTH = 8192
DECODER_HEAD_DIM = 128
ADAPTER_RANK = 16
IMG_DEV = 32
VMAX = 4
SLOT = 128
QUERY_PER_KEY = 8
N_SEQ = 32
N_TP = 8
COLS = 1280
EPSILON = 1e-06
ROPE_BASE = 1000000.0
MESH = pl.DeviceIdType.MESH
F32 = jnp.float32
BF16 = jnp.bfloat16


def tables():
    perm = np.zeros((512, 512), np.float32)
    for j in range(4):
        for i in range(32):
            for m in range(4):
                perm[j * 128 + i * 4 + m, i * 16 + m * 4 + j] = 1
    select = np.zeros((512, 768), np.float32)
    for group in range(6):
        for lane in range(HEAD):
            select[32 + group * HEAD + lane, group * 128 + lane] = 1
    half = DECODER_HEAD_DIM // 2
    inverse_freq = np.power(
        np.float32(ROPE_BASE), -(np.arange(half, dtype=np.float32) * 2.0 / DECODER_HEAD_DIM)
    ).astype(np.float32)
    angles = np.arange(SLOT, dtype=np.float32)[:, None] * inverse_freq[None, :]
    cosine = np.cos(angles).astype(np.float32)
    sine = np.sin(angles).astype(np.float32)
    return (
        jnp.asarray(perm, BF16),
        jnp.asarray(select, BF16),
        jnp.asarray(np.concatenate([cosine, cosine], 1)),
        jnp.asarray(np.concatenate([-sine, sine], 1)),
    )


def plane_copies():
    part_a, part_b = (0, 128), (128, 128)

    def sib(blocks):
        return [(by, bx, 0, 256, 0, 0, True) for by, bx in blocks]

    def go(by, bx, part, ty, tx):
        return (by, bx, part[0], part[1], ty, tx, False)

    sides = (-1, 1)
    near = [(0, -1), (0, 1), (-1, 0), (1, 0)]
    lists = {
        "0a": [go(0, 0, part_a, ty, tx) for ty, tx in near],
        "0b": [go(0, 0, part_b, ty, tx) for ty, tx in near],
        "0s": sib([(0, 0)]),
        "1a": [go(0, -1, part_a, 0, 1), go(-1, 0, part_a, 1, 0)]
        + [go(0, side, part_a, to, 0) for side in sides for to in sides],
        "1b": [go(1, 0, part_b, -1, 0)]
        + [go(side, 0, part_b, 0, to) for side in sides for to in sides],
        "1c": [go(0, 1, (128, 64), 0, -1), go(0, -1, (192, 64), 0, 1)],
        "1s": sib(near),
        "2a": [go(0, 2, part_a, 1, 0), go(0, 2, part_a, -1, 0), go(-1, 1, part_a, 1, 0), go(1, -1, part_a, -1, 0)],
        "2b": [go(2, 0, part_b, 0, 1), go(2, 0, part_b, 0, -1), go(1, -1, part_b, 0, 1), go(-1, 1, part_b, 0, -1)],
        "2s": sib([(2, 0), (-1, -1), (-1, 1), (1, -1), (1, 1)]),
        "3a": [go(-1, 2, (0, 64), 1, 0), go(1, 2, (64, 64), -1, 0)],
        "3b": [go(2, -1, (128, 64), 0, 1), go(2, 1, (192, 64), 0, -1)],
        "3s": sib([(-1, 2), (1, 2), (2, -1), (2, 1)]),
        "4s": sib([(0, 2), (2, 2)]),
    }
    return {
        name: (i, sum(entry[3] for entry in entries), entries) for i, (name, entries) in enumerate(lists.items())
    }


W_GROUPS = plane_copies()
NEAR = [(0, 0), (0, 3), (0, 1), (3, 0), (1, 0), (2, 0), (3, 3), (3, 1), (1, 3), (1, 1)]
FAR = [(3, 2), (1, 2), (2, 3), (2, 1), (0, 2), (2, 2)]
LANES = (256, 384)


def bdot(a, b):
    return jnp.dot(a, b, preferred_element_type=F32)


def bdot_nt(a, b):
    return lax.dot_general(a, b, (((1,), (1,)), ((), ())), preferred_element_type=F32)


def normalize(values):
    mean_val = jnp.mean(values, axis=-1, keepdims=True)
    centered = values - mean_val
    variance = jnp.mean(centered * centered, axis=-1, keepdims=True)
    return centered * lax.rsqrt(variance + EPSILON)


def iota(shape, axis):
    return lax.broadcasted_iota(jnp.int32, shape, axis)


def one_hot(mask):
    return mask.astype(F32).astype(BF16)


def kernel(
    slot_ref, tenant_ref, len_ref, counts, sessions, vit_qkv, vit_out,
    patches_hbm, mw, w, down_hbm, up, text_hbm, perm_hbm, select_hbm, cosine_hbm, sine_hbm,
    out,
    patches, down, text, perm, select, cosine, sine, w_in, up_in,
    g0, g1, wf, wall, pp, ln, qkv, o_all, ctx_all, enc, mwb, vis, xs, ys, tok_l, tok_e, dl, w_near, w_far, x_near, x_far, up_all, acc, squares, res,
    load_sem, gs_sem, gr_sem, fs_sem, fr_sem, ws_sem, wr_sem,
    os_sem, or_sem, ofs_sem, ofr_sem, cs_sem, cr_sem, es_sem, er_sem, ls_sem, lr_sem,
    as_sem, ar_sem, ds_sem, dr_sem,
):
    s = lax.axis_index("seq")
    t = lax.axis_index("tp")
    core = lax.rem(s, 2)
    chip = s // 2
    cx = lax.rem(chip, 4)
    cy = chip // 4
    sibling = s + 1 - 2 * core

    def chip_at(dy, dx):
        return lax.rem(cy + (dy + 4), 4) * 4 + lax.rem(cx + (dx + 4), 4)

    def rows(ref, start, size, step=16):
        return ref.at[pl.ds(pl.multiple_of(start, step), size)]

    def arrived(ref, sem):
        pltpu.make_async_copy(ref, ref, sem).wait()

    barrier = pltpu.get_barrier_semaphore()

    def greet_seq(i, carry):
        pl.semaphore_signal(barrier, inc=1, device_id=(lax.rem(s + i, N_SEQ), t), device_id_type=MESH)
        return carry

    def greet_tp(i, carry):
        pl.semaphore_signal(barrier, inc=1, device_id=(s, lax.rem(t + i, N_TP)), device_id_type=MESH)
        return carry

    lax.fori_loop(1, N_SEQ, greet_seq, 0)
    lax.fori_loop(1, N_TP, greet_tp, 0)

    loads = [
        pltpu.make_async_copy(source, to, load_sem.at[i])
        for i, (source, to) in enumerate(
            (
                (perm_hbm, perm), (patches_hbm, patches), (text_hbm, text), (select_hbm, select), (down_hbm, down),
                (cosine_hbm, cosine), (sine_hbm, sine), (w, w_in), (up, up_in), (mw, mwb),
            )
        )
    ]
    for load in loads:
        load.start()
    g_of = (g0, g1)

    def g_ref(c, at, blocks, phase):
        return rows(g_of[phase], (c * 16 + at) * 48, 48 * blocks)

    def g_start(phase):
        for dx, dy in ((2, 2), (1, 2), (2, 1), (3, 2), (2, 3), (1, 1), (3, 3), (1, 3), (3, 1), (2, 0), (0, 2), (1, 0), (0, 1), (3, 0), (0, 3)):
            piece = g_ref(core, chip, 1, phase)
            pltpu.make_async_remote_copy(
                src_ref=piece, dst_ref=piece, send_sem=gs_sem.at[phase], recv_sem=gr_sem.at[4 * phase + (4 - dy) % 4],
                device_id=(chip_at(dy, dx) * 2 + core, t), device_id_type=MESH,
            ).start()

    def g_row_of_chips(c, d, phase):
        return g_ref(c, lax.rem(cy + d, 4) * 4, 4, phase)

    def g_share(phase, groups):
        for d in groups:
            group = g_row_of_chips(core, d, phase)
            arrived(g_of[phase].at[pl.ds(0, 192 if d > 0 else 144)], gr_sem.at[4 * phase + d])
            pltpu.make_async_remote_copy(
                src_ref=group, dst_ref=group, send_sem=fs_sem.at[phase], recv_sem=fr_sem.at[phase],
                device_id=(sibling, t), device_id_type=MESH,
            ).start()

    def g_shared(phase, sems):
        arrived(g_of[phase].at[pl.ds(0, 768)], sems.at[phase])

    def g_sent():
        for phase in range(2):
            arrived(g_of[phase].at[pl.ds(0, 720)], gs_sem.at[phase])
            g_shared(phase, fs_sem)

    def w_ref(c, by, bx, first, size):
        place = (by % 4, bx % 4)
        buf, order = (w_near, NEAR) if place in NEAR else (w_far, FAR)
        return rows(buf, order.index(place) * 512 + c * 256 + first, size)

    def w_start(name):
        group, total, entries = W_GROUPS[name]
        for by, bx, first, size, ty, tx, sib in entries:
            pltpu.make_async_remote_copy(
                src_ref=w_ref(core, by, bx, first, size), dst_ref=w_ref(core, by - ty, bx - tx, first, size),
                send_sem=ws_sem.at[group], recv_sem=wr_sem.at[group],
                device_id=(sibling if sib else chip_at(ty, tx) * 2 + core, t), device_id_type=MESH,
            ).start()

    def w_wait(name):
        group, total, entries = W_GROUPS[name]
        arrived(w_near.at[pl.ds(0, total)], wr_sem.at[group])

    def w_sent():
        for group, total, entries in W_GROUPS.values():
            arrived(w_near.at[pl.ds(0, total)], ws_sem.at[group])

    right = (s, lax.rem(t + 1, N_TP))
    left = (s, lax.rem(t + N_TP - 1, N_TP))

    def ring(buf, base, size, cut, send, recv, crossed):
        def piece(origin, j):
            first = base(lax.rem(origin + 2 * N_TP, N_TP))
            return rows(buf, first + cut * j, cut if j == 0 else size - cut)

        def ways(k, j):
            both = [(0, j), (1, 1 - j if crossed else j)]
            return both if k < 3 else [(way, part) for way, part in both if part == way]

        def start(k, j):
            for way, part in ways(k, j):
                block = piece(t - k if way == 0 else t + k, part)
                pltpu.make_async_remote_copy(
                    src_ref=block, dst_ref=block, send_sem=send.at[0], recv_sem=recv.at[k * 2 + j],
                    device_id=(right, left)[way], device_id_type=MESH,
                ).start()

        def wait(k, j):
            total = sum((cut, size - cut)[part] for way, part in ways(k, j))
            if total > 0:
                arrived(buf.at[pl.ds(0, total)], recv.at[k * 2 + j])

        def on(k, j):
            wait(k - 1, j)
            start(k, j)

        def sent():
            arrived(buf.at[pl.ds(0, 7 * size)], send.at[0])

        return start, wait, on, sent

    e_start, e_wait, e_on, e_sent = ring(tok_e, lambda z: z * 128, 128, 64, es_sem, er_sem, True)
    l_start, l_wait, l_on, l_sent = ring(tok_l, lambda z: z * 128, 128, 64, ls_sem, lr_sem, True)
    o_start, o_wait, o_on, o_sent = ring(o_all, lambda z: z * 160 + 80 * core, 80, 48, os_sem, or_sem, True)
    c_start, c_wait, c_on, c_sent = ring(ctx_all, lambda z: z * 160, 160, 80, cs_sem, cr_sem, True)

    def o_share(k):
        for origin in (t - 1 - k, t + 1 + k) if k < 3 else (t + 4,):
            piece = rows(o_all, lax.rem(origin + 2 * N_TP, N_TP) * 160 + 80 * core, 80)
            pltpu.make_async_remote_copy(
                src_ref=piece, dst_ref=piece, send_sem=ofs_sem.at[0], recv_sem=ofr_sem.at[k],
                device_id=(sibling, t), device_id_type=MESH,
            ).start()

    def o_shared(k):
        arrived(o_all.at[pl.ds(0, 160 if k < 3 else 80)], ofr_sem.at[k])

    r_640, c_640 = iota((160, 640), 0), iota((160, 640), 1)
    mine = bdot(vit_out[...], one_hot(c_640 == r_640))
    for j in range(3):
        mine += bdot(vit_qkv[j], one_hot(c_640 == r_640 + 160 * (j + 1)))
    own_g = pl.ds(pl.multiple_of((core * 16 + chip) * 48, 16), 48)
    mine = jnp.concatenate([mine, jnp.zeros((8, 640), F32)], axis=0).astype(BF16)
    g0[own_g, :] = mine[:, :256]
    g1[own_g, :] = mine[:, 256:]

    def look_up(k, carry):
        slots, len0, len1, tenant0, tenant1 = carry
        slot = slot_ref[k]
        slots = jnp.where(sessions[...] == k, slot, slots)
        at0, at1 = slot == 2 * s, slot == 2 * s + 1
        return (
            slots, jnp.where(at0, len_ref[k], len0), jnp.where(at1, len_ref[k], len1),
            jnp.where(at0, tenant_ref[k], tenant0), jnp.where(at1, tenant_ref[k], tenant1),
        )

    zero = jnp.int32(0)
    slots, len0, len1, tenant0, tenant1 = lax.fori_loop(
        0, 64, look_up, (jnp.zeros((8, 128), jnp.int32), zero, zero, zero, zero)
    )
    length = (len0, len1)

    loads[7].wait()
    own_w = pl.ds(pl.multiple_of(core * 256, 256), 256)
    for j in range(10):
        w_near[own_w, 128 * j:128 * j + 128] = w_in[j]
    loads[8].wait()
    for j in range(10):
        up_all[:, 128 * j:128 * j + 128] = up_in[j]

    pl.semaphore_wait(barrier, N_SEQ + N_TP - 2)
    g_start(0)

    own_tok = pl.multiple_of(t * 128, 128)
    loads[2].wait()
    for l in range(2):
        tok_e[pl.ds(own_tok + 64 * l, 64), :] = jnp.where(
            iota((64, 1024), 0) + 64 < length[l], text[128 * l + 64:128 * l + 128, :], jnp.zeros((64, 1024), BF16)
        )
    e_start(0, 0)
    e_start(0, 1)

    loads[0].wait()
    loads[1].wait()
    for n in range(5):
        lanes = slice(256 * n, 256 * n + 256)
        pp[:, lanes] = bdot(perm[...], patches[:, lanes]).astype(BF16)
    for r in range(4):
        part = slice(128 * r, 128 * r + 128)
        ln[part, :] = normalize(pp[part, :].astype(F32)).astype(BF16)

    here = (slots >> 1) == s
    folded = jnp.concatenate(
        [jnp.where(here, counts[...], 0).astype(F32), jnp.where(here, slots & 1, 0).astype(F32)], axis=0
    ).astype(BF16)
    spread = bdot(folded, one_hot((iota((128, 512), 0) >> 5) == ((iota((128, 512), 1) >> 4) & 3)))
    n_8 = iota((8, 512), 1)
    own_row = iota((8, 512), 0) == (n_8 >> 6)
    count_n = jnp.sum(jnp.where(own_row, spread[:8, :], 0.0), axis=0, keepdims=True)
    place_n = jnp.sum(jnp.where(own_row, spread[8:, :], 0.0), axis=0, keepdims=True)
    by_place = jnp.where(iota((8, 512), 0) == place_n.astype(jnp.int32), count_n, 0.0)
    n_from, n_to = iota((512, 512), 0), iota((512, 512), 1)
    before = bdot(by_place.astype(BF16), one_hot(((n_from & 15) == 0) & ((n_from >> 4) < (n_to >> 4))))
    offset_n = jnp.where(place_n > 0.5, before[1:2, :], before[0:1, :])
    visual_rows = jnp.sum(by_place, axis=1, keepdims=True) * (1.0 / 16.0)
    n_1 = n_8[0:1, :]
    row_n = jnp.where(
        (n_1 & 3).astype(F32) < count_n, place_n * 64.0 + offset_n + (n_1 & 3).astype(F32), -1.0
    ).astype(jnp.int32)

    lane_8 = iota((128, 128), 1)
    encoded_here = bdot(
        jnp.concatenate([slots.astype(F32), counts[...].astype(F32)], axis=0).astype(BF16),
        one_hot(iota((128, 128), 0) == lax.rem(s, 4) * 32 + (lane_8 >> 2)),
    )
    own_row = iota((8, 128), 0) == s // 4
    slot_c = jnp.sum(jnp.where(own_row, encoded_here[:8, :], 0.0), axis=0, keepdims=True).astype(jnp.int32)
    count_c = jnp.sum(jnp.where(own_row, encoded_here[8:, :], 0.0), axis=0, keepdims=True).astype(jnp.int32)
    target_c = (slot_c >> 1) * 16 + (lane_8[0:1, :] & 3)
    key_8 = iota((128, 128), 0)
    bias = jnp.where(((key_8 >> 2) == (lane_8 >> 2)) & ((key_8 & 3) < count_c), 0.0, -1e30)
    tenant_mask = (
        (iota((128, 256), 0) >> 4) == jnp.where((iota((128, 256), 1) & 64) == 0, tenant0, tenant1)
    ).astype(F32)

    g_share(0, (2, 3, 1, 0))
    g_start(1)
    g_shared(0, fr_sem)

    def unpack(phase):
        lanes = slice(256 * phase, 256 * phase + LANES[phase])
        for c in range(4):
            for b in range(8):
                first = ((b % 2) * 16 + 4 * c + b // 2) * 48
                wf[40 * b:40 * b + 40, lanes] = g_of[phase][first:first + 48, :].astype(F32)[:40, :]
            wall[320 * c:320 * c + 320, lanes] = wf[:, lanes].astype(BF16)

    unpack(0)
    own_o = pl.multiple_of(t * 160, 32)
    pick = one_hot(iota((160, 256), 0) == iota((160, 256), 1))
    for r in range(5):
        part = slice(256 * r, 256 * r + 256)
        o_all[pl.ds(own_o, 160), part] = bdot_nt(pick, wall[part, 0:256]).astype(BF16)
    o_start(0, 0)
    o_start(0, 1)

    g_share(1, (2, 3))
    o_on(1, 0)
    w_start("0a")
    w_start("0b")
    w_start("0s")
    g_share(1, (1, 0))
    o_on(1, 1)
    o_share(0)
    g_shared(1, fr_sem)
    unpack(1)
    for n in range(2):
        lanes = slice(256 * n, 256 * n + 256)
        qkv[:, lanes] = bdot(ln[...], wall[:, 128 + 256 * n:384 + 256 * n]).astype(BF16)
    loads[3].wait()
    scale = 1.0 / math.sqrt(HEAD)
    for h in range(2):
        q_h = bdot(qkv[...], select[:, 128 * h:128 * h + 128]).astype(BF16)
        k_h = bdot(qkv[...], select[:, 256 + 128 * h:384 + 128 * h]).astype(BF16)
        v_h = bdot(qkv[...], select[:, 512 + 128 * h:640 + 128 * h])
        v_t = jnp.transpose(v_h).astype(BF16)
        for q in range(4):
            scores = bdot_nt(k_h, q_h[128 * q:128 * q + 128, :]) * scale
            scores = scores.reshape(4, 128, 128) + bias[None]
            largest = jnp.max(jnp.max(scores, axis=0), axis=0, keepdims=True)
            exponent = jnp.exp(scores - largest[None])
            total = jnp.sum(jnp.sum(exponent, axis=0), axis=0, keepdims=True)
            probs = (exponent / total[None]).astype(BF16).reshape(512, 128)
            ctx_t = bdot(v_t, probs).astype(BF16)
            ctx_all[pl.ds(own_o + 80 * h, 80), 128 * q:128 * q + 128] = ctx_t[:80, :]
        if h == 0:
            o_on(2, 0)

    c_start(0, 0)
    c_start(0, 1)

    def project_out(z, first=False):
        at = pl.ds(pl.multiple_of(lax.rem(z + 2 * N_TP, N_TP) * 160, 32), 160)
        for n in range(5):
            lanes = slice(256 * n, 256 * n + 256)
            term = lax.dot_general(
                ctx_all[at, :], o_all[at, lanes], (((0,), (0,)), ((), ())), preferred_element_type=F32
            )
            enc[:, lanes] = (pp[:, lanes].astype(F32) if first else enc[:, lanes]) + term

    o_on(2, 1)
    o_share(1)
    project_out(t, True)
    w_wait("0a")
    w_start("1a")
    c_on(1, 0)
    c_on(1, 1)
    o_shared(0)
    project_out(t - 1)
    project_out(t + 1)
    o_on(3, 0)
    o_on(3, 1)
    o_share(2)
    w_wait("0b")
    w_start("1b")
    c_on(2, 0)
    c_on(2, 1)
    o_shared(1)
    project_out(t - 2)
    project_out(t + 2)
    o_wait(3, 0)
    o_share(3)
    c_on(3, 0)
    c_on(3, 1)
    w_start("1s")
    o_shared(2)
    e_on(1, 0)
    e_on(1, 1)
    project_out(t - 3)
    project_out(t + 3)
    o_shared(3)
    loads[9].wait()
    c_wait(3, 0)
    project_out(t + 4)

    for j in range(4):
        x_near[0:128, 1280 * j:1280 * j + 1280] = normalize(enc[128 * j:128 * j + 128, :]).astype(BF16)
    for n in range(4):
        lanes = slice(256 * n, 256 * n + 256)
        vis[:, lanes] = bdot(x_near[0:128, :], mwb[:, lanes]).astype(BF16)
    e_on(2, 0)

    row_512 = iota((512, 128), 0)
    outgoing = jnp.zeros((512, 256), F32)
    for q in range(4):
        outgoing += bdot(one_hot(row_512 == target_c + 4 * q), vis[:, 256 * q:256 * q + 256])
    xs[...] = outgoing.astype(BF16)

    def send_rows(i, carry):
        to = lax.rem(s + i, N_SEQ)
        pltpu.make_async_remote_copy(
            src_ref=rows(xs, to * 16, 16), dst_ref=rows(ys, s * 16, 16),
            send_sem=as_sem.at[0], recv_sem=ar_sem.at[0], device_id=(to, t), device_id_type=MESH,
        ).start()
        return carry

    lax.fori_loop(1, N_SEQ, send_rows, 0)
    own_y = pl.ds(pl.multiple_of(s * 16, 16), 16)
    ys[own_y, :] = xs[own_y, :]
    e_on(2, 1)
    e_on(3, 0)
    arrived(ys.at[pl.ds(0, 496)], ar_sem.at[0])

    row_128 = iota((128, 512), 0)
    position = iota((64, 256), 0)
    for q in range(4):
        lanes = slice(256 * q, 256 * q + 256)
        picked = bdot(one_hot((row_128 == row_n) & (((n_1 >> 2) & 3) == q)), ys[...]).astype(BF16)
        for l in range(2):
            is_text = (position.astype(F32) >= visual_rows[l:l + 1, :]) & (position < length[l])
            tok_l[pl.ds(own_tok + 64 * l, 64), lanes] = jnp.where(
                is_text, text[128 * l:128 * l + 64, lanes], picked[64 * l:64 * l + 64, :]
            )
    l_start(0, 0)
    l_start(0, 1)
    w_wait("1a")
    w_start("2a")
    w_wait("1b")
    w_start("2b")
    w_start("1c")
    w_start("2s")

    loads[4].wait()
    own_rows = jnp.concatenate([tok_l[pl.ds(own_tok, 128), :], tok_e[pl.ds(own_tok, 128), :]], axis=0)
    down_sums = jnp.transpose(bdot(own_rows, down[...])) * tenant_mask
    dl[pl.ds(pl.multiple_of(t * 16, 16), 16), :] = jnp.sum(down_sums.reshape(8, 16, 256), axis=0)

    def send_down(i, carry):
        piece = rows(dl, t * 16, 16)
        pltpu.make_async_remote_copy(
            src_ref=piece, dst_ref=piece, send_sem=ds_sem.at[0], recv_sem=dr_sem.at[0],
            device_id=(s, lax.rem(t + i, N_TP)), device_id_type=MESH,
        ).start()
        return carry

    lax.fori_loop(1, N_TP, send_down, 0)

    def collect(tok, top):
        for to, order in ((x_near, NEAR), (x_far, FAR)):
            for n, (by, bx) in enumerate(order):
                at = chip_at(by, bx)
                of_z = pl.ds(pl.multiple_of(at // 2 * 128, 128), 128)
                half = pl.ds(pl.multiple_of(lax.rem(at, 2) * 512, 512), 512)
                to[top:top + 128, 512 * n:512 * n + 512] = tok[of_z, half]

    def project(x, weight, top, size, first, last):
        for n in range(5):
            lanes = slice(256 * n, 256 * n + 256)
            acc[top:top + size, lanes] += bdot(x[top:top + size, first:last], weight[first:last, lanes])

    def add_squares(aheads, tok, top):
        for ahead in aheads:
            of_z = pl.ds(pl.multiple_of(lax.rem(t + ahead + N_TP, N_TP) * 128, 128), 128)
            total = squares[top:top + 128, :]
            for n in range(8):
                part = tok[of_z, 128 * n:128 * n + 128].astype(F32)
                total += part * part
            squares[top:top + 128, :] = total

    acc[...] = jnp.zeros_like(acc)
    squares[...] = jnp.zeros_like(squares)
    l_on(1, 0)
    e_wait(2, 1)
    e_wait(3, 0)
    add_squares(range(8), tok_e, 128)
    collect(tok_e, 128)
    l_on(1, 1)
    add_squares((0, 1, -1), tok_l, 0)
    for name in ("0s", "1s"):
        w_wait(name)
    project(x_near, w_near, 128, 128, 0, 2560)
    l_on(2, 0)
    w_wait("2s")
    project(x_near, w_near, 128, 128, 2560, 5120)
    l_on(2, 1)
    w_wait("2a")
    w_start("3a")
    add_squares((2, -2), tok_l, 0)
    l_on(3, 0)
    w_wait("2b")
    w_start("3b")
    w_start("3s")
    l_on(3, 1)
    add_squares((3, -3), tok_l, 0)
    for name in ("1c", "3a", "3b"):
        w_wait(name)
    w_start("4s")
    arrived(dl.at[pl.ds(0, 112)], dr_sem.at[0])
    down_t = jnp.sum(dl[...].reshape(8, 16, 256), axis=0)
    lora = jnp.transpose(jnp.concatenate([down_t] * 8, axis=0) * tenant_mask).astype(BF16)
    acc[...] += bdot(lora, up_all[...])
    l_wait(3, 0)
    add_squares((4,), tok_l, 0)
    collect(tok_l, 0)
    project(x_near, w_near, 0, 128, 0, 5120)
    w_wait("3s")
    w_wait("4s")
    project(x_far, w_far, 0, 256, 0, 3072)
    inverse = lax.rsqrt(jnp.sum(squares[...], axis=1, keepdims=True) * (1.0 / DECODER_WIDTH) + EPSILON)

    loads[5].wait()
    loads[6].wait()

    causal = (iota((1024, 128), 0) & 127) >= iota((1024, 128), 1)
    ones = jnp.ones((128, 128), BF16)
    stores = []
    for l in range(2):
        low, high = slice(64 * l, 64 * l + 64), slice(128 + 64 * l, 192 + 64 * l)
        factor = jnp.concatenate([inverse[low, :], inverse[high, :]], axis=0)

        def column(index):
            lanes = slice(128 * index, 128 * index + 128)
            return jnp.concatenate([acc[low, lanes], acc[high, lanes]], axis=0) * factor

        def rotate(values):
            return values * cosine[...] + pltpu.roll(values, 64, 1) * sine[...]

        key_rows = rotate(column(8)).astype(BF16)
        value_rows = jnp.concatenate([column(9).astype(BF16), ones], axis=1)
        kept = iota((128, 128), 0) < length[l]
        queries = jnp.concatenate([rotate(column(j)).astype(BF16) for j in range(QUERY_PER_KEY)], axis=0)
        scores = bdot_nt(queries, key_rows) * (1.0 / math.sqrt(DECODER_HEAD_DIM))
        scores = jnp.where(causal, scores, -1e30)
        exponent = jnp.exp(scores - jnp.max(scores, axis=1, keepdims=True)).astype(BF16)
        summed = bdot(exponent, value_rows)
        ratio = summed[:, :128] / summed[:, 128:]
        for j in range(QUERY_PER_KEY):
            res[128 * l:128 * l + 128, 128 * j:128 * j + 128] = jnp.where(
                kept, ratio[128 * j:128 * j + 128, :], 0.0
            ).astype(BF16)
        stores.append(pltpu.make_async_copy(
            res.at[pl.ds(128 * l, 128)], out.at[pl.ds(128 * l, 128)], load_sem.at[10 + l]
        ))
        stores[l].start()

    for store in stores:
        store.wait()
    g_sent()
    w_sent()
    e_sent()
    l_sent()
    o_sent()
    c_sent()
    arrived(o_all.at[pl.ds(0, 560)], ofs_sem.at[0])
    arrived(xs.at[pl.ds(0, 496)], as_sem.at[0])
    arrived(dl.at[pl.ds(0, 112)], ds_sem.at[0])


def on_device(
    patches, vit_qkv, vit_out, merge_weight, query_key_value_weight, adapter_down, adapter_up_weight,
    text_embed, vis_count, image_session, session_slot, session_tenant, session_len,
):
    operands = (
        session_slot, session_tenant, session_len, vis_count.reshape(8, 128), image_session.reshape(8, 128),
        vit_qkv, vit_out.T, patches.reshape(512, DV), merge_weight,
        jnp.transpose(query_key_value_weight.reshape(256, 10, 128), (1, 0, 2)), adapter_down,
        jnp.transpose(adapter_up_weight.reshape(128, 10, 128), (1, 0, 2)), text_embed,
    ) + tables()
    vmem = pl.BlockSpec(memory_space=pltpu.VMEM)
    smem = pl.BlockSpec(memory_space=pltpu.SMEM)
    hbm = pl.BlockSpec(memory_space=pl.ANY)
    dma = pltpu.SemaphoreType.DMA
    return pl.pallas_call(
        kernel,
        out_shape=jax.ShapeDtypeStruct((256, 1024), BF16),
        in_specs=[smem if i < 3 else vmem if i < 7 else hbm for i in range(len(operands))],
        out_specs=hbm,
        scratch_shapes=[
            pltpu.VMEM((512, 1280), BF16),
            pltpu.VMEM((1024, 128), BF16),
            pltpu.VMEM((256, 1024), BF16),
            pltpu.VMEM((512, 512), BF16),
            pltpu.VMEM((512, 768), BF16),
            pltpu.VMEM((128, 128), F32),
            pltpu.VMEM((128, 128), F32),
            pltpu.VMEM((10, 256, 128), BF16),
            pltpu.VMEM((10, 128, 128), BF16),
            pltpu.VMEM((1536, LANES[0]), BF16),
            pltpu.VMEM((1536, LANES[1]), BF16),
            pltpu.VMEM((320, 640), F32),
            pltpu.VMEM((1280, 640), BF16),
            pltpu.VMEM((512, 1280), BF16),
            pltpu.VMEM((512, 1280), BF16),
            pltpu.VMEM((512, 512), BF16),
            pltpu.VMEM((1280, 1280), BF16),
            pltpu.VMEM((1280, 512), BF16),
            pltpu.VMEM((512, 1280), F32),
            pltpu.VMEM((5120, 1024), BF16),
            pltpu.VMEM((128, 1024), BF16),
            pltpu.VMEM((512, 256), BF16),
            pltpu.VMEM((512, 256), BF16),
            pltpu.VMEM((1024, 1024), BF16),
            pltpu.VMEM((1024, 1024), BF16),
            pltpu.VMEM((128, 256), F32),
            pltpu.VMEM((5120, 1280), BF16),
            pltpu.VMEM((3072, 1280), BF16),
            pltpu.VMEM((256, 5120), BF16),
            pltpu.VMEM((256, 3072), BF16),
            pltpu.VMEM((128, 1280), BF16),
            pltpu.VMEM((256, 1280), F32),
            pltpu.VMEM((256, 128), F32),
            pltpu.VMEM((256, 1024), BF16),
            dma((12,)), dma((2,)), dma((8,)), dma((2,)), dma((2,)), dma((len(W_GROUPS),)), dma((len(W_GROUPS),)),
            dma((1,)), dma((8,)), dma((1,)), dma((4,)),
            dma((1,)), dma((8,)), dma((1,)), dma((8,)), dma((1,)), dma((8,)),
            dma((1,)), dma((1,)), dma((1,)), dma((1,)),
        ],
        compiler_params=pltpu.CompilerParams(
            collective_id=0, has_side_effects=True, vmem_limit_bytes=64 * 1024 * 1024
        ),
    )(*operands).astype(F32)


def solution(mesh):
    placed = (
        P("seq", None, None),
        P(None, "seq", "tp"),
        P("tp", "seq"),
        P(None, "tp"),
        P("seq", "tp", None, None),
        P("tp", None),
        P(None, "tp", None, None),
        P("seq", "tp"),
        P(),
        P(),
        P(),
        P(),
        P(),
    )
    return jax.shard_map(
        on_device, mesh=mesh, in_specs=placed, out_specs=P("seq", "tp"), check_vma=False
    )
```

```python
import functools
import math

import jax
import jax.numpy as jnp
import numpy as np
from jax import lax
from jax.experimental import pallas as pl
from jax.experimental.pallas import tpu as pltpu
from jax.sharding import PartitionSpec as P

DV = 1280
HV = 16
HEAD = 80
DECODER_WIDTH = 8192
DECODER_HEAD_DIM = 128
ADAPTER_RANK = 16
IMG_DEV = 32
VMAX = 4
SLOT = 128
QUERY_PER_KEY = 8
N_SEQ = 32
N_TP = 8
COLS = 1280
EPSILON = 1e-06
ROPE_BASE = 1000000.0
MESH = pl.DeviceIdType.MESH
F32 = jnp.float32
BF16 = jnp.bfloat16


def tables():
    perm = np.zeros((512, 512), np.float32)
    for j in range(4):
        for i in range(32):
            for m in range(4):
                perm[j * 128 + i * 4 + m, i * 16 + m * 4 + j] = 1
    select = np.zeros((512, 768), np.float32)
    for group in range(6):
        for lane in range(HEAD):
            select[32 + group * HEAD + lane, group * 128 + lane] = 1
    half = DECODER_HEAD_DIM // 2
    inverse_freq = np.power(
        np.float32(ROPE_BASE), -(np.arange(half, dtype=np.float32) * 2.0 / DECODER_HEAD_DIM)
    ).astype(np.float32)
    angles = np.arange(SLOT, dtype=np.float32)[:, None] * inverse_freq[None, :]
    cosine = np.cos(angles).astype(np.float32)
    sine = np.sin(angles).astype(np.float32)
    return (
        jnp.asarray(perm, BF16),
        jnp.asarray(select, BF16),
        jnp.asarray(np.concatenate([cosine, cosine], 1)),
        jnp.asarray(np.concatenate([-sine, sine], 1)),
    )


def plane_copies():
    part_a, part_b = (0, 128), (128, 128)

    def sib(blocks):
        return [(by, bx, 0, 256, 0, 0, True) for by, bx in blocks]

    def go(by, bx, part, ty, tx):
        return (by, bx, part[0], part[1], ty, tx, False)

    sides = (-1, 1)
    near = [(0, -1), (0, 1), (-1, 0), (1, 0)]
    lists = {
        "0a": [go(0, 0, part_a, ty, tx) for ty, tx in near],
        "0b": [go(0, 0, part_b, ty, tx) for ty, tx in near],
        "0s": sib([(0, 0)]),
        "1a": [go(0, -1, (0, 64), 0, 1), go(0, 1, (64, 64), 0, -1)]
        + [go(0, side, part_a, to, 0) for side in sides for to in sides],
        "1b": [go(-1, 0, (128, 64), 1, 0), go(1, 0, (192, 64), -1, 0)]
        + [go(side, 0, part_b, 0, to) for side in sides for to in sides],
        "1c": [
            go(0, 1, (128, 64), 0, -1), go(0, -1, (192, 64), 0, 1), go(-1, 0, (0, 64), 1, 0), go(1, 0, (64, 64), -1, 0),
        ],
        "1s": sib(near),
        "2a": [go(0, 2, part_a, 1, 0), go(0, 2, part_a, -1, 0), go(-1, 1, part_a, 1, 0), go(1, -1, part_a, -1, 0)],
        "2b": [go(2, 0, part_b, 0, 1), go(2, 0, part_b, 0, -1), go(1, -1, part_b, 0, 1), go(-1, 1, part_b, 0, -1)],
        "2s": sib([(-1, -1), (-1, 1), (1, -1), (1, 1)]),
        "3a": [go(-1, 2, (0, 64), 1, 0), go(1, 2, (64, 64), -1, 0)],
        "3b": [go(2, -1, (128, 64), 0, 1), go(2, 1, (192, 64), 0, -1)],
        "3s": sib([(-1, 2), (1, 2), (2, -1), (2, 1)]),
        "4s": sib([(0, 2), (2, 0)]),
        "5s": sib([(2, 2)]),
    }
    return {
        name: (i, sum(entry[3] for entry in entries), entries) for i, (name, entries) in enumerate(lists.items())
    }


W_GROUPS = plane_copies()
NEAR = [(0, 0), (0, 3), (0, 1), (3, 0), (1, 0), (3, 3), (3, 1), (1, 3), (1, 1)]
FAR = [(3, 2), (1, 2), (2, 3), (2, 1), (0, 2), (2, 0), (2, 2)]
LANES = (256, 384)


def bdot(a, b):
    return jnp.dot(a, b, preferred_element_type=F32)


def bdot_nt(a, b):
    return lax.dot_general(a, b, (((1,), (1,)), ((), ())), preferred_element_type=F32)


def normalize(values):
    mean_val = jnp.mean(values, axis=-1, keepdims=True)
    centered = values - mean_val
    variance = jnp.mean(centered * centered, axis=-1, keepdims=True)
    return centered * lax.rsqrt(variance + EPSILON)


def iota(shape, axis):
    return lax.broadcasted_iota(jnp.int32, shape, axis)


def one_hot(mask):
    return mask.astype(F32).astype(BF16)


def kernel(
    slot_ref, tenant_ref, len_ref, counts, sessions, vit_qkv, vit_out,
    patches_hbm, mw, w, down_hbm, up, text_hbm, perm_hbm, select_hbm, cosine_hbm, sine_hbm,
    out,
    patches, down, text, perm, select, cosine, sine, w_in, up_in,
    g0, g1, wf, wall, pp, ln, qkv, o_all, ctx_all, enc, mwb, vis, xs, ys, tok_l, tok_e, dl, w_near, w_far, x_near, x_far, up_all, acc, squares, res,
    load_sem, gs_sem, gr_sem, fs_sem, fr_sem, ws_sem, wr_sem,
    os_sem, or_sem, ofs_sem, ofr_sem, cs_sem, cr_sem, es_sem, er_sem, ls_sem, lr_sem,
    as_sem, ar_sem, ds_sem, dr_sem,
):
    s = lax.axis_index("seq")
    t = lax.axis_index("tp")
    core = lax.rem(s, 2)
    chip = s // 2
    cx = lax.rem(chip, 4)
    cy = chip // 4
    sibling = s + 1 - 2 * core

    def chip_at(dy, dx):
        return lax.rem(cy + (dy + 4), 4) * 4 + lax.rem(cx + (dx + 4), 4)

    def rows(ref, start, size, step=16):
        return ref.at[pl.ds(pl.multiple_of(start, step), size)]

    def arrived(ref, sem):
        pltpu.make_async_copy(ref, ref, sem).wait()

    barrier = pltpu.get_barrier_semaphore()

    def greet_seq(i, carry):
        pl.semaphore_signal(barrier, inc=1, device_id=(lax.rem(s + i, N_SEQ), t), device_id_type=MESH)
        return carry

    def greet_tp(i, carry):
        pl.semaphore_signal(barrier, inc=1, device_id=(s, lax.rem(t + i, N_TP)), device_id_type=MESH)
        return carry

    lax.fori_loop(1, N_SEQ, greet_seq, 0)
    lax.fori_loop(1, N_TP, greet_tp, 0)

    loads = [
        pltpu.make_async_copy(source, to, load_sem.at[i])
        for i, (source, to) in enumerate(
            (
                (perm_hbm, perm), (patches_hbm, patches), (text_hbm, text), (select_hbm, select), (down_hbm, down),
                (cosine_hbm, cosine), (sine_hbm, sine), (w, w_in), (up, up_in), (mw, mwb),
            )
        )
    ]
    for load in loads:
        load.start()
    g_of = (g0, g1)

    def g_ref(c, at, blocks, phase):
        return rows(g_of[phase], (c * 16 + at) * 48, 48 * blocks)

    def g_start(phase):
        for dx, dy in ((2, 2), (1, 2), (2, 1), (3, 2), (2, 3), (1, 1), (3, 3), (1, 3), (3, 1), (2, 0), (0, 2), (1, 0), (0, 1), (3, 0), (0, 3)):
            piece = g_ref(core, chip, 1, phase)
            pltpu.make_async_remote_copy(
                src_ref=piece, dst_ref=piece, send_sem=gs_sem.at[phase], recv_sem=gr_sem.at[4 * phase + (4 - dy) % 4],
                device_id=(chip_at(dy, dx) * 2 + core, t), device_id_type=MESH,
            ).start()

    def g_row_of_chips(c, d, phase):
        return g_ref(c, lax.rem(cy + d, 4) * 4, 4, phase)

    def g_share(phase, groups):
        for d in groups:
            group = g_row_of_chips(core, d, phase)
            arrived(g_of[phase].at[pl.ds(0, 192 if d > 0 else 144)], gr_sem.at[4 * phase + d])
            pltpu.make_async_remote_copy(
                src_ref=group, dst_ref=group, send_sem=fs_sem.at[phase], recv_sem=fr_sem.at[phase],
                device_id=(sibling, t), device_id_type=MESH,
            ).start()

    def g_shared(phase, sems):
        arrived(g_of[phase].at[pl.ds(0, 768)], sems.at[phase])

    def g_sent():
        for phase in range(2):
            arrived(g_of[phase].at[pl.ds(0, 720)], gs_sem.at[phase])
            g_shared(phase, fs_sem)

    def w_ref(c, by, bx, first, size):
        place = (by % 4, bx % 4)
        buf, order = (w_near, NEAR) if place in NEAR else (w_far, FAR)
        return rows(buf, order.index(place) * 512 + c * 256 + first, size)

    def w_start(name):
        group, total, entries = W_GROUPS[name]
        for by, bx, first, size, ty, tx, sib in entries:
            pltpu.make_async_remote_copy(
                src_ref=w_ref(core, by, bx, first, size), dst_ref=w_ref(core, by - ty, bx - tx, first, size),
                send_sem=ws_sem.at[group], recv_sem=wr_sem.at[group],
                device_id=(sibling if sib else chip_at(ty, tx) * 2 + core, t), device_id_type=MESH,
            ).start()

    def w_wait(name):
        group, total, entries = W_GROUPS[name]
        arrived(w_near.at[pl.ds(0, total)], wr_sem.at[group])

    def w_sent():
        for group, total, entries in W_GROUPS.values():
            arrived(w_near.at[pl.ds(0, total)], ws_sem.at[group])

    right = (s, lax.rem(t + 1, N_TP))
    left = (s, lax.rem(t + N_TP - 1, N_TP))

    def ring(buf, base, size, cut, send, recv, crossed):
        def piece(origin, j):
            first = base(lax.rem(origin + 2 * N_TP, N_TP))
            return rows(buf, first + cut * j, cut if j == 0 else size - cut)

        def ways(k, j):
            both = [(0, j), (1, 1 - j if crossed else j)]
            return both if k < 3 else [(way, part) for way, part in both if part == way]

        def start(k, j):
            for way, part in ways(k, j):
                block = piece(t - k if way == 0 else t + k, part)
                pltpu.make_async_remote_copy(
                    src_ref=block, dst_ref=block, send_sem=send.at[0], recv_sem=recv.at[k * 2 + j],
                    device_id=(right, left)[way], device_id_type=MESH,
                ).start()

        def wait(k, j):
            total = sum((cut, size - cut)[part] for way, part in ways(k, j))
            if total > 0:
                arrived(buf.at[pl.ds(0, total)], recv.at[k * 2 + j])

        def on(k, j):
            wait(k - 1, j)
            start(k, j)

        def sent():
            arrived(buf.at[pl.ds(0, 7 * size)], send.at[0])

        return start, wait, on, sent

    e_start, e_wait, e_on, e_sent = ring(tok_e, lambda z: z * 128, 128, 64, es_sem, er_sem, True)
    l_start, l_wait, l_on, l_sent = ring(tok_l, lambda z: z * 128, 128, 64, ls_sem, lr_sem, True)
    o_start, o_wait, o_on, o_sent = ring(o_all, lambda z: z * 160 + 80 * core, 80, 48, os_sem, or_sem, True)
    c_start, c_wait, c_on, c_sent = ring(ctx_all, lambda z: z * 160, 160, 80, cs_sem, cr_sem, True)

    def o_share(k):
        for origin in (t - 1 - k, t + 1 + k) if k < 3 else (t + 4,):
            piece = rows(o_all, lax.rem(origin + 2 * N_TP, N_TP) * 160 + 80 * core, 80)
            pltpu.make_async_remote_copy(
                src_ref=piece, dst_ref=piece, send_sem=ofs_sem.at[0], recv_sem=ofr_sem.at[k],
                device_id=(sibling, t), device_id_type=MESH,
            ).start()

    def o_shared(k):
        arrived(o_all.at[pl.ds(0, 160 if k < 3 else 80)], ofr_sem.at[k])

    r_640, c_640 = iota((160, 640), 0), iota((160, 640), 1)
    mine = bdot(vit_out[...], one_hot(c_640 == r_640))
    for j in range(3):
        mine += bdot(vit_qkv[j], one_hot(c_640 == r_640 + 160 * (j + 1)))
    own_g = pl.ds(pl.multiple_of((core * 16 + chip) * 48, 16), 48)
    mine = jnp.concatenate([mine, jnp.zeros((8, 640), F32)], axis=0).astype(BF16)
    g0[own_g, :] = mine[:, :256]
    g1[own_g, :] = mine[:, 256:]

    def look_up(k, carry):
        slots, len0, len1, tenant0, tenant1 = carry
        slot = slot_ref[k]
        slots = jnp.where(sessions[...] == k, slot, slots)
        at0, at1 = slot == 2 * s, slot == 2 * s + 1
        return (
            slots, jnp.where(at0, len_ref[k], len0), jnp.where(at1, len_ref[k], len1),
            jnp.where(at0, tenant_ref[k], tenant0), jnp.where(at1, tenant_ref[k], tenant1),
        )

    zero = jnp.int32(0)
    slots, len0, len1, tenant0, tenant1 = lax.fori_loop(
        0, 64, look_up, (jnp.zeros((8, 128), jnp.int32), zero, zero, zero, zero)
    )
    length = (len0, len1)

    loads[7].wait()
    own_w = pl.ds(pl.multiple_of(core * 256, 256), 256)
    for j in range(10):
        w_near[own_w, 128 * j:128 * j + 128] = w_in[j]
    loads[8].wait()
    for j in range(10):
        up_all[:, 128 * j:128 * j + 128] = up_in[j]

    pl.semaphore_wait(barrier, N_SEQ + N_TP - 2)
    g_start(0)

    own_tok = pl.multiple_of(t * 128, 128)
    loads[2].wait()
    for l in range(2):
        tok_e[pl.ds(own_tok + 64 * l, 64), :] = jnp.where(
            iota((64, 1024), 0) + 64 < length[l], text[128 * l + 64:128 * l + 128, :], jnp.zeros((64, 1024), BF16)
        )
    e_start(0, 0)
    e_start(0, 1)

    loads[0].wait()
    loads[1].wait()
    for n in range(5):
        lanes = slice(256 * n, 256 * n + 256)
        pp[:, lanes] = bdot(perm[...], patches[:, lanes]).astype(BF16)
    for r in range(4):
        part = slice(128 * r, 128 * r + 128)
        ln[part, :] = normalize(pp[part, :].astype(F32)).astype(BF16)

    here = (slots >> 1) == s
    folded = jnp.concatenate(
        [jnp.where(here, counts[...], 0).astype(F32), jnp.where(here, slots & 1, 0).astype(F32)], axis=0
    ).astype(BF16)
    spread = bdot(folded, one_hot((iota((128, 512), 0) >> 5) == ((iota((128, 512), 1) >> 4) & 3)))
    n_8 = iota((8, 512), 1)
    own_row = iota((8, 512), 0) == (n_8 >> 6)
    count_n = jnp.sum(jnp.where(own_row, spread[:8, :], 0.0), axis=0, keepdims=True)
    place_n = jnp.sum(jnp.where(own_row, spread[8:, :], 0.0), axis=0, keepdims=True)
    by_place = jnp.where(iota((8, 512), 0) == place_n.astype(jnp.int32), count_n, 0.0)
    n_from, n_to = iota((512, 512), 0), iota((512, 512), 1)
    before = bdot(by_place.astype(BF16), one_hot(((n_from & 15) == 0) & ((n_from >> 4) < (n_to >> 4))))
    offset_n = jnp.where(place_n > 0.5, before[1:2, :], before[0:1, :])
    visual_rows = jnp.sum(by_place, axis=1, keepdims=True) * (1.0 / 16.0)
    n_1 = n_8[0:1, :]
    row_n = jnp.where(
        (n_1 & 3).astype(F32) < count_n, place_n * 64.0 + offset_n + (n_1 & 3).astype(F32), -1.0
    ).astype(jnp.int32)

    lane_8 = iota((128, 128), 1)
    encoded_here = bdot(
        jnp.concatenate([slots.astype(F32), counts[...].astype(F32)], axis=0).astype(BF16),
        one_hot(iota((128, 128), 0) == lax.rem(s, 4) * 32 + (lane_8 >> 2)),
    )
    own_row = iota((8, 128), 0) == s // 4
    slot_c = jnp.sum(jnp.where(own_row, encoded_here[:8, :], 0.0), axis=0, keepdims=True).astype(jnp.int32)
    count_c = jnp.sum(jnp.where(own_row, encoded_here[8:, :], 0.0), axis=0, keepdims=True).astype(jnp.int32)
    target_c = (slot_c >> 1) * 16 + (lane_8[0:1, :] & 3)
    key_8 = iota((128, 128), 0)
    bias = jnp.where(((key_8 >> 2) == (lane_8 >> 2)) & ((key_8 & 3) < count_c), 0.0, -1e30)
    tenant_mask = (
        (iota((128, 256), 0) >> 4) == jnp.where((iota((128, 256), 1) & 64) == 0, tenant0, tenant1)
    ).astype(F32)

    g_share(0, (2, 3, 1, 0))
    g_start(1)
    e_on(1, 0)
    g_shared(0, fr_sem)

    def unpack(phase):
        lanes = slice(256 * phase, 256 * phase + LANES[phase])
        for c in range(4):
            for b in range(8):
                first = ((b % 2) * 16 + 4 * c + b // 2) * 48
                wf[40 * b:40 * b + 40, lanes] = g_of[phase][first:first + 48, :].astype(F32)[:40, :]
            wall[320 * c:320 * c + 320, lanes] = wf[:, lanes].astype(BF16)

    unpack(0)
    own_o = pl.multiple_of(t * 160, 32)
    pick = one_hot(iota((160, 256), 0) == iota((160, 256), 1))
    for r in range(5):
        part = slice(256 * r, 256 * r + 256)
        o_all[pl.ds(own_o, 160), part] = bdot_nt(pick, wall[part, 0:256]).astype(BF16)
    o_start(0, 0)
    o_start(0, 1)

    g_share(1, (2, 3))
    o_on(1, 0)
    w_start("0a")
    w_start("0b")
    w_start("0s")
    g_share(1, (1, 0))
    o_on(1, 1)
    o_share(0)
    g_shared(1, fr_sem)
    unpack(1)
    for n in range(2):
        lanes = slice(256 * n, 256 * n + 256)
        qkv[:, lanes] = bdot(ln[...], wall[:, 128 + 256 * n:384 + 256 * n]).astype(BF16)
    loads[3].wait()
    scale = 1.0 / math.sqrt(HEAD)
    for h in range(2):
        q_h = bdot(qkv[...], select[:, 128 * h:128 * h + 128]).astype(BF16)
        k_h = bdot(qkv[...], select[:, 256 + 128 * h:384 + 128 * h]).astype(BF16)
        v_h = bdot(qkv[...], select[:, 512 + 128 * h:640 + 128 * h])
        v_t = jnp.transpose(v_h).astype(BF16)
        for q in range(4):
            scores = bdot_nt(k_h, q_h[128 * q:128 * q + 128, :]) * scale
            scores = scores.reshape(4, 128, 128) + bias[None]
            largest = jnp.max(jnp.max(scores, axis=0), axis=0, keepdims=True)
            exponent = jnp.exp(scores - largest[None])
            total = jnp.sum(jnp.sum(exponent, axis=0), axis=0, keepdims=True)
            probs = (exponent / total[None]).astype(BF16).reshape(512, 128)
            ctx_t = bdot(v_t, probs).astype(BF16)
            ctx_all[pl.ds(own_o + 80 * h, 80), 128 * q:128 * q + 128] = ctx_t[:80, :]
        if h == 0:
            o_on(2, 0)

    c_start(0, 0)
    c_start(0, 1)

    def project_out(z, first=False):
        at = pl.ds(pl.multiple_of(lax.rem(z + 2 * N_TP, N_TP) * 160, 32), 160)
        for n in range(5):
            lanes = slice(256 * n, 256 * n + 256)
            term = lax.dot_general(
                ctx_all[at, :], o_all[at, lanes], (((0,), (0,)), ((), ())), preferred_element_type=F32
            )
            enc[:, lanes] = (pp[:, lanes].astype(F32) if first else enc[:, lanes]) + term

    o_on(2, 1)
    o_share(1)
    project_out(t, True)
    w_wait("0a")
    w_start("1a")
    c_on(1, 0)
    c_on(1, 1)
    o_shared(0)
    project_out(t - 1)
    project_out(t + 1)
    o_on(3, 0)
    o_on(3, 1)
    o_share(2)
    w_wait("0b")
    w_start("1b")
    c_on(2, 0)
    c_on(2, 1)
    o_shared(1)
    project_out(t - 2)
    project_out(t + 2)
    o_wait(3, 0)
    o_share(3)
    c_on(3, 0)
    c_on(3, 1)
    w_start("1s")
    o_shared(2)
    e_on(1, 1)
    e_on(2, 0)
    project_out(t - 3)
    project_out(t + 3)
    o_shared(3)
    loads[9].wait()
    c_wait(3, 0)
    project_out(t + 4)

    for j in range(4):
        x_near[0:128, 1280 * j:1280 * j + 1280] = normalize(enc[128 * j:128 * j + 128, :]).astype(BF16)
    for n in range(4):
        lanes = slice(256 * n, 256 * n + 256)
        vis[:, lanes] = bdot(x_near[0:128, :], mwb[:, lanes]).astype(BF16)
    e_on(2, 1)

    row_512 = iota((512, 128), 0)
    outgoing = jnp.zeros((512, 256), F32)
    for q in range(4):
        outgoing += bdot(one_hot(row_512 == target_c + 4 * q), vis[:, 256 * q:256 * q + 256])
    xs[...] = outgoing.astype(BF16)

    def send_rows(i, carry):
        to = lax.rem(s + i, N_SEQ)
        pltpu.make_async_remote_copy(
            src_ref=rows(xs, to * 16, 16), dst_ref=rows(ys, s * 16, 16),
            send_sem=as_sem.at[0], recv_sem=ar_sem.at[0], device_id=(to, t), device_id_type=MESH,
        ).start()
        return carry

    lax.fori_loop(1, N_SEQ, send_rows, 0)
    own_y = pl.ds(pl.multiple_of(s * 16, 16), 16)
    ys[own_y, :] = xs[own_y, :]
    e_on(3, 0)
    w_wait("1a")
    w_wait("1b")
    arrived(ys.at[pl.ds(0, 496)], ar_sem.at[0])
    w_start("2a")
    w_start("2b")
    w_start("1c")
    w_start("2s")

    row_128 = iota((128, 512), 0)
    position = iota((64, 256), 0)
    for q in range(4):
        lanes = slice(256 * q, 256 * q + 256)
        picked = bdot(one_hot((row_128 == row_n) & (((n_1 >> 2) & 3) == q)), ys[...]).astype(BF16)
        for l in range(2):
            is_text = (position.astype(F32) >= visual_rows[l:l + 1, :]) & (position < length[l])
            tok_l[pl.ds(own_tok + 64 * l, 64), lanes] = jnp.where(
                is_text, text[128 * l:128 * l + 64, lanes], picked[64 * l:64 * l + 64, :]
            )
    l_start(0, 0)
    l_start(0, 1)

    loads[4].wait()
    own_rows = jnp.concatenate([tok_l[pl.ds(own_tok, 128), :], tok_e[pl.ds(own_tok, 128), :]], axis=0)
    down_sums = jnp.transpose(bdot(own_rows, down[...])) * tenant_mask
    dl[pl.ds(pl.multiple_of(t * 16, 16), 16), :] = jnp.sum(down_sums.reshape(8, 16, 256), axis=0)

    def send_down(i, carry):
        piece = rows(dl, t * 16, 16)
        pltpu.make_async_remote_copy(
            src_ref=piece, dst_ref=piece, send_sem=ds_sem.at[0], recv_sem=dr_sem.at[0],
            device_id=(s, lax.rem(t + i, N_TP)), device_id_type=MESH,
        ).start()
        return carry

    lax.fori_loop(1, N_TP, send_down, 0)

    def collect(tok, top):
        for to, order in ((x_near, NEAR), (x_far, FAR)):
            for n, (by, bx) in enumerate(order):
                at = chip_at(by, bx)
                of_z = pl.ds(pl.multiple_of(at // 2 * 128, 128), 128)
                half = pl.ds(pl.multiple_of(lax.rem(at, 2) * 512, 512), 512)
                to[top:top + 128, 512 * n:512 * n + 512] = tok[of_z, half]

    def project(x, weight, top, size, first, last):
        for n in range(5):
            lanes = slice(256 * n, 256 * n + 256)
            acc[top:top + size, lanes] += bdot(x[top:top + size, first:last], weight[first:last, lanes])

    def add_squares(aheads, tok, top):
        for ahead in aheads:
            of_z = pl.ds(pl.multiple_of(lax.rem(t + ahead + N_TP, N_TP) * 128, 128), 128)
            total = squares[top:top + 128, :]
            for n in range(8):
                part = tok[of_z, 128 * n:128 * n + 128].astype(F32)
                total += part * part
            squares[top:top + 128, :] = total

    acc[...] = jnp.zeros_like(acc)
    squares[...] = jnp.zeros_like(squares)
    l_on(1, 0)
    e_wait(2, 1)
    e_wait(3, 0)
    add_squares(range(8), tok_e, 128)
    collect(tok_e, 128)
    l_on(1, 1)
    add_squares((0, 1, -1), tok_l, 0)
    for name in ("0s", "1s"):
        w_wait(name)
    project(x_near, w_near, 128, 128, 0, 2560)
    l_on(2, 0)
    w_wait("2s")
    project(x_near, w_near, 128, 128, 2560, 4608)
    l_on(2, 1)
    w_wait("2a")
    w_start("3a")
    w_wait("2b")
    w_start("3b")
    w_start("3s")
    add_squares((2, -2), tok_l, 0)
    l_on(3, 0)
    l_on(3, 1)
    add_squares((3, -3), tok_l, 0)
    w_wait("1c")
    w_start("4s")
    w_wait("3a")
    w_wait("3b")
    w_start("5s")
    arrived(dl.at[pl.ds(0, 112)], dr_sem.at[0])
    down_t = jnp.sum(dl[...].reshape(8, 16, 256), axis=0)
    lora = jnp.transpose(jnp.concatenate([down_t] * 8, axis=0) * tenant_mask).astype(BF16)
    acc[...] += bdot(lora, up_all[...])
    l_wait(3, 0)
    add_squares((4,), tok_l, 0)
    collect(tok_l, 0)
    project(x_near, w_near, 0, 128, 0, 4608)
    w_wait("3s")
    w_wait("4s")
    w_wait("5s")
    project(x_far, w_far, 0, 256, 0, 3584)
    inverse = lax.rsqrt(jnp.sum(squares[...], axis=1, keepdims=True) * (1.0 / DECODER_WIDTH) + EPSILON)

    loads[5].wait()
    loads[6].wait()

    causal = (iota((1024, 128), 0) & 127) >= iota((1024, 128), 1)
    ones = jnp.ones((128, 128), BF16)
    stores = []
    for l in range(2):
        low, high = slice(64 * l, 64 * l + 64), slice(128 + 64 * l, 192 + 64 * l)
        factor = jnp.concatenate([inverse[low, :], inverse[high, :]], axis=0)

        def column(index):
            lanes = slice(128 * index, 128 * index + 128)
            return jnp.concatenate([acc[low, lanes], acc[high, lanes]], axis=0) * factor

        def rotate(values):
            return values * cosine[...] + pltpu.roll(values, 64, 1) * sine[...]

        key_rows = rotate(column(8)).astype(BF16)
        value_rows = jnp.concatenate([column(9).astype(BF16), ones], axis=1)
        kept = iota((128, 128), 0) < length[l]
        queries = jnp.concatenate([rotate(column(j)).astype(BF16) for j in range(QUERY_PER_KEY)], axis=0)
        scores = bdot_nt(queries, key_rows) * (1.0 / math.sqrt(DECODER_HEAD_DIM))
        scores = jnp.where(causal, scores, -1e30)
        exponent = jnp.exp(scores - jnp.max(scores, axis=1, keepdims=True)).astype(BF16)
        summed = bdot(exponent, value_rows)
        ratio = summed[:, :128] / summed[:, 128:]
        for j in range(QUERY_PER_KEY):
            res[128 * l:128 * l + 128, 128 * j:128 * j + 128] = jnp.where(
                kept, ratio[128 * j:128 * j + 128, :], 0.0
            ).astype(BF16)
        stores.append(pltpu.make_async_copy(
            res.at[pl.ds(128 * l, 128)], out.at[pl.ds(128 * l, 128)], load_sem.at[10 + l]
        ))
        stores[l].start()

    for store in stores:
        store.wait()
    g_sent()
    w_sent()
    e_sent()
    l_sent()
    o_sent()
    c_sent()
    arrived(o_all.at[pl.ds(0, 560)], ofs_sem.at[0])
    arrived(xs.at[pl.ds(0, 496)], as_sem.at[0])
    arrived(dl.at[pl.ds(0, 112)], ds_sem.at[0])


def on_device(
    patches, vit_qkv, vit_out, merge_weight, query_key_value_weight, adapter_down, adapter_up_weight,
    text_embed, vis_count, image_session, session_slot, session_tenant, session_len,
):
    operands = (
        session_slot, session_tenant, session_len, vis_count.reshape(8, 128), image_session.reshape(8, 128),
        vit_qkv, vit_out.T, patches.reshape(512, DV), merge_weight,
        jnp.transpose(query_key_value_weight.reshape(256, 10, 128), (1, 0, 2)), adapter_down,
        jnp.transpose(adapter_up_weight.reshape(128, 10, 128), (1, 0, 2)), text_embed,
    ) + tables()
    vmem = pl.BlockSpec(memory_space=pltpu.VMEM)
    smem = pl.BlockSpec(memory_space=pltpu.SMEM)
    hbm = pl.BlockSpec(memory_space=pl.ANY)
    dma = pltpu.SemaphoreType.DMA
    return pl.pallas_call(
        kernel,
        out_shape=jax.ShapeDtypeStruct((256, 1024), BF16),
        in_specs=[smem if i < 3 else vmem if i < 7 else hbm for i in range(len(operands))],
        out_specs=hbm,
        scratch_shapes=[
            pltpu.VMEM((512, 1280), BF16),
            pltpu.VMEM((1024, 128), BF16),
            pltpu.VMEM((256, 1024), BF16),
            pltpu.VMEM((512, 512), BF16),
            pltpu.VMEM((512, 768), BF16),
            pltpu.VMEM((128, 128), F32),
            pltpu.VMEM((128, 128), F32),
            pltpu.VMEM((10, 256, 128), BF16),
            pltpu.VMEM((10, 128, 128), BF16),
            pltpu.VMEM((1536, LANES[0]), BF16),
            pltpu.VMEM((1536, LANES[1]), BF16),
            pltpu.VMEM((320, 640), F32),
            pltpu.VMEM((1280, 640), BF16),
            pltpu.VMEM((512, 1280), BF16),
            pltpu.VMEM((512, 1280), BF16),
            pltpu.VMEM((512, 512), BF16),
            pltpu.VMEM((1280, 1280), BF16),
            pltpu.VMEM((1280, 512), BF16),
            pltpu.VMEM((512, 1280), F32),
            pltpu.VMEM((5120, 1024), BF16),
            pltpu.VMEM((128, 1024), BF16),
            pltpu.VMEM((512, 256), BF16),
            pltpu.VMEM((512, 256), BF16),
            pltpu.VMEM((1024, 1024), BF16),
            pltpu.VMEM((1024, 1024), BF16),
            pltpu.VMEM((128, 256), F32),
            pltpu.VMEM((4608, 1280), BF16),
            pltpu.VMEM((3584, 1280), BF16),
            pltpu.VMEM((256, 5120), BF16),
            pltpu.VMEM((256, 3584), BF16),
            pltpu.VMEM((128, 1280), BF16),
            pltpu.VMEM((256, 1280), F32),
            pltpu.VMEM((256, 128), F32),
            pltpu.VMEM((256, 1024), BF16),
            dma((12,)), dma((2,)), dma((8,)), dma((2,)), dma((2,)), dma((len(W_GROUPS),)), dma((len(W_GROUPS),)),
            dma((1,)), dma((8,)), dma((1,)), dma((4,)),
            dma((1,)), dma((8,)), dma((1,)), dma((8,)), dma((1,)), dma((8,)),
            dma((1,)), dma((1,)), dma((1,)), dma((1,)),
        ],
        compiler_params=pltpu.CompilerParams(
            collective_id=0, has_side_effects=True, vmem_limit_bytes=64 * 1024 * 1024
        ),
    )(*operands).astype(F32)


def solution(mesh):
    placed = (
        P("seq", None, None),
        P(None, "seq", "tp"),
        P("tp", "seq"),
        P(None, "tp"),
        P("seq", "tp", None, None),
        P("tp", None),
        P(None, "tp", None, None),
        P("seq", "tp"),
        P(),
        P(),
        P(),
        P(),
        P(),
    )
    return jax.shard_map(
        on_device, mesh=mesh, in_specs=placed, out_specs=P("seq", "tp"), check_vma=False
    )
```

```python
import functools
import math

import jax
import jax.numpy as jnp
import numpy as np
from jax import lax
from jax.experimental import pallas as pl
from jax.experimental.pallas import tpu as pltpu
from jax.sharding import PartitionSpec as P

DV = 1280
HV = 16
HEAD = 80
DECODER_WIDTH = 8192
DECODER_HEAD_DIM = 128
ADAPTER_RANK = 16
IMG_DEV = 32
VMAX = 4
SLOT = 128
QUERY_PER_KEY = 8
N_SEQ = 32
N_TP = 8
COLS = 1280
EPSILON = 1e-06
ROPE_BASE = 1000000.0
MESH = pl.DeviceIdType.MESH
F32 = jnp.float32
BF16 = jnp.bfloat16


def tables():
    perm = np.zeros((512, 512), np.float32)
    for j in range(4):
        for i in range(32):
            for m in range(4):
                perm[j * 128 + i * 4 + m, i * 16 + m * 4 + j] = 1
    select = np.zeros((512, 768), np.float32)
    for group in range(6):
        for lane in range(HEAD):
            select[32 + group * HEAD + lane, group * 128 + lane] = 1
    half = DECODER_HEAD_DIM // 2
    inverse_freq = np.power(
        np.float32(ROPE_BASE), -(np.arange(half, dtype=np.float32) * 2.0 / DECODER_HEAD_DIM)
    ).astype(np.float32)
    angles = np.arange(SLOT, dtype=np.float32)[:, None] * inverse_freq[None, :]
    cosine = np.cos(angles).astype(np.float32)
    sine = np.sin(angles).astype(np.float32)
    return (
        jnp.asarray(perm, BF16),
        jnp.asarray(select, BF16),
        jnp.asarray(np.concatenate([cosine, cosine], 1)),
        jnp.asarray(np.concatenate([-sine, sine], 1)),
    )


def plane_copies():
    part_a, part_b = (0, 128), (128, 128)

    def sib(blocks):
        return [(by, bx, 0, 256, 0, 0, True) for by, bx in blocks]

    def go(by, bx, part, ty, tx):
        return (by, bx, part[0], part[1], ty, tx, False)

    sides = (-1, 1)
    near = [(0, -1), (0, 1), (-1, 0), (1, 0)]
    lists = {
        "0a": [go(0, 0, part_a, ty, tx) for ty, tx in near],
        "0b": [go(0, 0, part_b, ty, tx) for ty, tx in near],
        "0s": sib([(0, 0)]),
        "1a": [go(0, -1, (0, 64), 0, 1), go(0, 1, (64, 64), 0, -1)]
        + [go(0, side, part_a, to, 0) for side in sides for to in sides],
        "1b": [go(-1, 0, (128, 64), 1, 0), go(1, 0, (192, 64), -1, 0)]
        + [go(side, 0, part_b, 0, to) for side in sides for to in sides],
        "1c": [
            go(0, 1, (128, 64), 0, -1), go(0, -1, (192, 64), 0, 1), go(-1, 0, (0, 64), 1, 0), go(1, 0, (64, 64), -1, 0),
        ],
        "1s": sib(near),
        "2a": [go(0, 2, part_a, 1, 0), go(0, 2, part_a, -1, 0), go(-1, 1, part_a, 1, 0), go(1, -1, part_a, -1, 0)],
        "2b": [go(2, 0, part_b, 0, 1), go(2, 0, part_b, 0, -1), go(1, -1, part_b, 0, 1), go(-1, 1, part_b, 0, -1)],
        "2s": sib([(-1, -1), (-1, 1), (1, -1), (1, 1)]),
        "3a": [go(-1, 2, (0, 64), 1, 0), go(1, 2, (64, 64), -1, 0)],
        "3b": [go(2, -1, (128, 64), 0, 1), go(2, 1, (192, 64), 0, -1)],
        "3s": sib([(-1, 2), (1, 2), (2, -1), (2, 1)]),
        "4s": sib([(0, 2), (2, 0)]),
        "5s": sib([(2, 2)]),
    }
    return {
        name: (i, sum(entry[3] for entry in entries), entries) for i, (name, entries) in enumerate(lists.items())
    }


W_GROUPS = plane_copies()
NEAR = [(0, 0), (0, 3), (0, 1), (3, 0), (1, 0), (3, 3), (3, 1), (1, 3), (1, 1)]
FAR = [(3, 2), (1, 2), (2, 3), (2, 1), (0, 2), (2, 0), (2, 2)]
LANES = (256, 384)


def bdot(a, b):
    return jnp.dot(a, b, preferred_element_type=F32)


def bdot_nt(a, b):
    return lax.dot_general(a, b, (((1,), (1,)), ((), ())), preferred_element_type=F32)


def normalize(values):
    mean_val = jnp.mean(values, axis=-1, keepdims=True)
    centered = values - mean_val
    variance = jnp.mean(centered * centered, axis=-1, keepdims=True)
    return centered * lax.rsqrt(variance + EPSILON)


def iota(shape, axis):
    return lax.broadcasted_iota(jnp.int32, shape, axis)


def one_hot(mask):
    return mask.astype(F32).astype(BF16)


def kernel(
    slot_ref, tenant_ref, len_ref, counts, sessions, vit_qkv, vit_out,
    patches_hbm, mw, w, down_hbm, up, text_hbm, perm_hbm, select_hbm, cosine_hbm, sine_hbm,
    out,
    patches, down, text, perm, select, cosine, sine, w_in, up_in,
    g0, g1, wf, wall, pp, ln, qkv, o_all, ctx_all, enc, mwb, vis, xs, ys, tok_l, tok_e, dl, w_near, w_far, x_near, x_far, up_all, acc, squares, res,
    load_sem, gs_sem, gr_sem, fs_sem, fr_sem, ws_sem, wr_sem,
    os_sem, or_sem, ofs_sem, ofr_sem, cs_sem, cr_sem, es_sem, er_sem, ls_sem, lr_sem,
    as_sem, ar_sem, ds_sem, dr_sem,
):
    s = lax.axis_index("seq")
    t = lax.axis_index("tp")
    core = lax.rem(s, 2)
    chip = s // 2
    cx = lax.rem(chip, 4)
    cy = chip // 4
    sibling = s + 1 - 2 * core

    def chip_at(dy, dx):
        return lax.rem(cy + (dy + 4), 4) * 4 + lax.rem(cx + (dx + 4), 4)

    def rows(ref, start, size, step=16):
        return ref.at[pl.ds(pl.multiple_of(start, step), size)]

    def arrived(ref, sem):
        pltpu.make_async_copy(ref, ref, sem).wait()

    barrier = pltpu.get_barrier_semaphore()

    def greet_seq(i, carry):
        pl.semaphore_signal(barrier, inc=1, device_id=(lax.rem(s + i, N_SEQ), t), device_id_type=MESH)
        return carry

    def greet_tp(i, carry):
        pl.semaphore_signal(barrier, inc=1, device_id=(s, lax.rem(t + i, N_TP)), device_id_type=MESH)
        return carry

    lax.fori_loop(1, N_SEQ, greet_seq, 0)
    lax.fori_loop(1, N_TP, greet_tp, 0)

    loads = [
        pltpu.make_async_copy(source, to, load_sem.at[i])
        for i, (source, to) in enumerate(
            (
                (perm_hbm, perm), (patches_hbm, patches), (text_hbm, text), (select_hbm, select), (down_hbm, down),
                (cosine_hbm, cosine), (sine_hbm, sine), (w, w_in), (up, up_in), (mw, mwb),
            )
        )
    ]
    for load in loads:
        load.start()
    g_of = (g0, g1)

    def g_ref(c, at, blocks, phase):
        return rows(g_of[phase], (c * 16 + at) * 48, 48 * blocks)

    def g_start(phase):
        for dx, dy in ((2, 2), (1, 2), (2, 1), (3, 2), (2, 3), (1, 1), (3, 3), (1, 3), (3, 1), (2, 0), (0, 2), (1, 0), (0, 1), (3, 0), (0, 3)):
            piece = g_ref(core, chip, 1, phase)
            pltpu.make_async_remote_copy(
                src_ref=piece, dst_ref=piece, send_sem=gs_sem.at[phase], recv_sem=gr_sem.at[4 * phase + (4 - dy) % 4],
                device_id=(chip_at(dy, dx) * 2 + core, t), device_id_type=MESH,
            ).start()

    def g_row_of_chips(c, d, phase):
        return g_ref(c, lax.rem(cy + d, 4) * 4, 4, phase)

    def g_share(phase, groups):
        for d in groups:
            group = g_row_of_chips(core, d, phase)
            arrived(g_of[phase].at[pl.ds(0, 192 if d > 0 else 144)], gr_sem.at[4 * phase + d])
            pltpu.make_async_remote_copy(
                src_ref=group, dst_ref=group, send_sem=fs_sem.at[phase], recv_sem=fr_sem.at[phase],
                device_id=(sibling, t), device_id_type=MESH,
            ).start()

    def g_shared(phase, sems):
        arrived(g_of[phase].at[pl.ds(0, 768)], sems.at[phase])

    def g_sent():
        for phase in range(2):
            arrived(g_of[phase].at[pl.ds(0, 720)], gs_sem.at[phase])
            g_shared(phase, fs_sem)

    def w_ref(c, by, bx, first, size):
        place = (by % 4, bx % 4)
        buf, order = (w_near, NEAR) if place in NEAR else (w_far, FAR)
        return rows(buf, order.index(place) * 512 + c * 256 + first, size)

    def w_start(name):
        group, total, entries = W_GROUPS[name]
        for by, bx, first, size, ty, tx, sib in entries:
            pltpu.make_async_remote_copy(
                src_ref=w_ref(core, by, bx, first, size), dst_ref=w_ref(core, by - ty, bx - tx, first, size),
                send_sem=ws_sem.at[group], recv_sem=wr_sem.at[group],
                device_id=(sibling if sib else chip_at(ty, tx) * 2 + core, t), device_id_type=MESH,
            ).start()

    def w_wait(name):
        group, total, entries = W_GROUPS[name]
        arrived(w_near.at[pl.ds(0, total)], wr_sem.at[group])

    def w_sent():
        for group, total, entries in W_GROUPS.values():
            arrived(w_near.at[pl.ds(0, total)], ws_sem.at[group])

    right = (s, lax.rem(t + 1, N_TP))
    left = (s, lax.rem(t + N_TP - 1, N_TP))

    def ring(buf, base, size, cut, send, recv, crossed):
        def piece(origin, j):
            first = base(lax.rem(origin + 2 * N_TP, N_TP))
            return rows(buf, first + cut * j, cut if j == 0 else size - cut)

        def ways(k, j):
            both = [(0, j), (1, 1 - j if crossed else j)]
            return both if k < 3 else [(way, part) for way, part in both if part == way]

        def start(k, j):
            for way, part in ways(k, j):
                block = piece(t - k if way == 0 else t + k, part)
                pltpu.make_async_remote_copy(
                    src_ref=block, dst_ref=block, send_sem=send.at[0], recv_sem=recv.at[k * 2 + j],
                    device_id=(right, left)[way], device_id_type=MESH,
                ).start()

        def wait(k, j):
            total = sum((cut, size - cut)[part] for way, part in ways(k, j))
            if total > 0:
                arrived(buf.at[pl.ds(0, total)], recv.at[k * 2 + j])

        def on(k, j):
            wait(k - 1, j)
            start(k, j)

        def sent():
            arrived(buf.at[pl.ds(0, 7 * size)], send.at[0])

        return start, wait, on, sent

    e_start, e_wait, e_on, e_sent = ring(tok_e, lambda z: z * 128, 128, 64, es_sem, er_sem, True)
    l_start, l_wait, l_on, l_sent = ring(tok_l, lambda z: z * 128, 128, 64, ls_sem, lr_sem, True)
    o_start, o_wait, o_on, o_sent = ring(o_all, lambda z: z * 160 + 80 * core, 80, 48, os_sem, or_sem, True)
    c_start, c_wait, c_on, c_sent = ring(ctx_all, lambda z: z * 160, 160, 80, cs_sem, cr_sem, True)

    def o_share(k):
        for origin in (t - 1 - k, t + 1 + k) if k < 3 else (t + 4,):
            piece = rows(o_all, lax.rem(origin + 2 * N_TP, N_TP) * 160 + 80 * core, 80)
            pltpu.make_async_remote_copy(
                src_ref=piece, dst_ref=piece, send_sem=ofs_sem.at[0], recv_sem=ofr_sem.at[k],
                device_id=(sibling, t), device_id_type=MESH,
            ).start()

    def o_shared(k):
        arrived(o_all.at[pl.ds(0, 160 if k < 3 else 80)], ofr_sem.at[k])

    r_640, c_640 = iota((160, 640), 0), iota((160, 640), 1)
    mine = bdot(vit_out[...], one_hot(c_640 == r_640))
    for j in range(3):
        mine += bdot(vit_qkv[j], one_hot(c_640 == r_640 + 160 * (j + 1)))
    own_g = pl.ds(pl.multiple_of((core * 16 + chip) * 48, 16), 48)
    mine = jnp.concatenate([mine, jnp.zeros((8, 640), F32)], axis=0).astype(BF16)
    g0[own_g, :] = mine[:, :256]
    g1[own_g, :] = mine[:, 256:]

    def look_up(k, carry):
        slots, len0, len1, tenant0, tenant1 = carry
        slot = slot_ref[k]
        slots = jnp.where(sessions[...] == k, slot, slots)
        at0, at1 = slot == 2 * s, slot == 2 * s + 1
        return (
            slots, jnp.where(at0, len_ref[k], len0), jnp.where(at1, len_ref[k], len1),
            jnp.where(at0, tenant_ref[k], tenant0), jnp.where(at1, tenant_ref[k], tenant1),
        )

    zero = jnp.int32(0)
    slots, len0, len1, tenant0, tenant1 = lax.fori_loop(
        0, 64, look_up, (jnp.zeros((8, 128), jnp.int32), zero, zero, zero, zero)
    )
    length = (len0, len1)

    loads[7].wait()
    own_w = pl.ds(pl.multiple_of(core * 256, 256), 256)
    for j in range(10):
        w_near[own_w, 128 * j:128 * j + 128] = w_in[j]
    loads[8].wait()
    for j in range(10):
        up_all[:, 128 * j:128 * j + 128] = up_in[j]

    pl.semaphore_wait(barrier, N_SEQ + N_TP - 2)
    g_start(0)

    own_tok = pl.multiple_of(t * 128, 128)
    loads[2].wait()
    for l in range(2):
        tok_e[pl.ds(own_tok + 64 * l, 64), :] = jnp.where(
            iota((64, 1024), 0) + 64 < length[l], text[128 * l + 64:128 * l + 128, :], jnp.zeros((64, 1024), BF16)
        )
    e_start(0, 0)
    e_start(0, 1)

    loads[0].wait()
    loads[1].wait()
    for n in range(5):
        lanes = slice(256 * n, 256 * n + 256)
        pp[:, lanes] = bdot(perm[...], patches[:, lanes]).astype(BF16)
    for r in range(4):
        part = slice(128 * r, 128 * r + 128)
        ln[part, :] = normalize(pp[part, :].astype(F32)).astype(BF16)

    here = (slots >> 1) == s
    folded = jnp.concatenate(
        [jnp.where(here, counts[...], 0).astype(F32), jnp.where(here, slots & 1, 0).astype(F32)], axis=0
    ).astype(BF16)
    spread = bdot(folded, one_hot((iota((128, 512), 0) >> 5) == ((iota((128, 512), 1) >> 4) & 3)))
    n_8 = iota((8, 512), 1)
    own_row = iota((8, 512), 0) == (n_8 >> 6)
    count_n = jnp.sum(jnp.where(own_row, spread[:8, :], 0.0), axis=0, keepdims=True)
    place_n = jnp.sum(jnp.where(own_row, spread[8:, :], 0.0), axis=0, keepdims=True)
    by_place = jnp.where(iota((8, 512), 0) == place_n.astype(jnp.int32), count_n, 0.0)
    n_from, n_to = iota((512, 512), 0), iota((512, 512), 1)
    before = bdot(by_place.astype(BF16), one_hot(((n_from & 15) == 0) & ((n_from >> 4) < (n_to >> 4))))
    offset_n = jnp.where(place_n > 0.5, before[1:2, :], before[0:1, :])
    visual_rows = jnp.sum(by_place, axis=1, keepdims=True) * (1.0 / 16.0)
    n_1 = n_8[0:1, :]
    row_n = jnp.where(
        (n_1 & 3).astype(F32) < count_n, place_n * 64.0 + offset_n + (n_1 & 3).astype(F32), -1.0
    ).astype(jnp.int32)

    lane_8 = iota((128, 128), 1)
    encoded_here = bdot(
        jnp.concatenate([slots.astype(F32), counts[...].astype(F32)], axis=0).astype(BF16),
        one_hot(iota((128, 128), 0) == lax.rem(s, 4) * 32 + (lane_8 >> 2)),
    )
    own_row = iota((8, 128), 0) == s // 4
    slot_c = jnp.sum(jnp.where(own_row, encoded_here[:8, :], 0.0), axis=0, keepdims=True).astype(jnp.int32)
    count_c = jnp.sum(jnp.where(own_row, encoded_here[8:, :], 0.0), axis=0, keepdims=True).astype(jnp.int32)
    target_c = (slot_c >> 1) * 16 + (lane_8[0:1, :] & 3)
    key_8 = iota((128, 128), 0)
    bias = jnp.where(((key_8 >> 2) == (lane_8 >> 2)) & ((key_8 & 3) < count_c), 0.0, -1e30)
    tenant_mask = (
        (iota((128, 256), 0) >> 4) == jnp.where((iota((128, 256), 1) & 64) == 0, tenant0, tenant1)
    ).astype(F32)

    g_share(0, (2, 3, 1, 0))
    g_start(1)
    e_on(1, 0)
    g_shared(0, fr_sem)

    def unpack(phase):
        lanes = slice(256 * phase, 256 * phase + LANES[phase])
        for c in range(4):
            for b in range(8):
                first = ((b % 2) * 16 + 4 * c + b // 2) * 48
                wf[40 * b:40 * b + 40, lanes] = g_of[phase][first:first + 48, :].astype(F32)[:40, :]
            wall[320 * c:320 * c + 320, lanes] = wf[:, lanes].astype(BF16)

    unpack(0)
    own_o = pl.multiple_of(t * 160, 32)
    pick = one_hot(iota((160, 256), 0) == iota((160, 256), 1))
    for r in range(5):
        part = slice(256 * r, 256 * r + 256)
        o_all[pl.ds(own_o, 160), part] = bdot_nt(pick, wall[part, 0:256]).astype(BF16)
    o_start(0, 0)
    o_start(0, 1)

    g_share(1, (2, 3))
    o_on(1, 0)
    w_start("0a")
    w_start("0b")
    w_start("0s")
    g_share(1, (1, 0))
    o_on(1, 1)
    o_share(0)
    g_shared(1, fr_sem)
    unpack(1)
    for n in range(2):
        lanes = slice(256 * n, 256 * n + 256)
        qkv[:, lanes] = bdot(ln[...], wall[:, 128 + 256 * n:384 + 256 * n]).astype(BF16)
    loads[3].wait()
    scale = 1.0 / math.sqrt(HEAD)
    for h in range(2):
        q_h = bdot(qkv[...], select[:, 128 * h:128 * h + 128]).astype(BF16)
        k_h = bdot(qkv[...], select[:, 256 + 128 * h:384 + 128 * h]).astype(BF16)
        v_h = bdot(qkv[...], select[:, 512 + 128 * h:640 + 128 * h])
        v_t = jnp.transpose(v_h).astype(BF16)
        for q in range(4):
            scores = bdot_nt(k_h, q_h[128 * q:128 * q + 128, :]) * scale
            scores = scores.reshape(4, 128, 128) + bias[None]
            largest = jnp.max(jnp.max(scores, axis=0), axis=0, keepdims=True)
            exponent = jnp.exp(scores - largest[None])
            total = jnp.sum(jnp.sum(exponent, axis=0), axis=0, keepdims=True)
            probs = (exponent / total[None]).astype(BF16).reshape(512, 128)
            ctx_t = bdot(v_t, probs).astype(BF16)
            ctx_all[pl.ds(own_o + 80 * h, 80), 128 * q:128 * q + 128] = ctx_t[:80, :]
        if h == 0:
            o_on(2, 0)

    c_start(0, 0)
    c_start(0, 1)

    def project_out(z, first=False):
        at = pl.ds(pl.multiple_of(lax.rem(z + 2 * N_TP, N_TP) * 160, 32), 160)
        for n in range(5):
            lanes = slice(256 * n, 256 * n + 256)
            term = lax.dot_general(
                ctx_all[at, :], o_all[at, lanes], (((0,), (0,)), ((), ())), preferred_element_type=F32
            )
            enc[:, lanes] = (pp[:, lanes].astype(F32) if first else enc[:, lanes]) + term

    o_on(2, 1)
    o_share(1)
    project_out(t, True)
    w_wait("0a")
    w_start("1a")
    c_on(1, 0)
    c_on(1, 1)
    o_shared(0)
    project_out(t - 1)
    project_out(t + 1)
    o_on(3, 0)
    o_on(3, 1)
    o_share(2)
    w_wait("0b")
    w_start("1b")
    c_on(2, 0)
    c_on(2, 1)
    o_shared(1)
    project_out(t - 2)
    project_out(t + 2)
    o_wait(3, 0)
    o_share(3)
    c_on(3, 0)
    c_on(3, 1)
    w_start("1s")
    o_shared(2)
    e_on(1, 1)
    e_on(2, 0)
    project_out(t - 3)
    project_out(t + 3)
    o_shared(3)
    loads[9].wait()
    c_wait(3, 0)
    project_out(t + 4)

    for j in range(4):
        x_near[0:128, 1280 * j:1280 * j + 1280] = normalize(enc[128 * j:128 * j + 128, :]).astype(BF16)
    for n in range(4):
        lanes = slice(256 * n, 256 * n + 256)
        vis[:, lanes] = bdot(x_near[0:128, :], mwb[:, lanes]).astype(BF16)
    e_on(2, 1)

    row_512 = iota((512, 128), 0)
    outgoing = jnp.zeros((512, 256), F32)
    for q in range(4):
        outgoing += bdot(one_hot(row_512 == target_c + 4 * q), vis[:, 256 * q:256 * q + 256])
    xs[...] = outgoing.astype(BF16)

    def send_rows(i, carry):
        to = lax.rem(s + i, N_SEQ)
        pltpu.make_async_remote_copy(
            src_ref=rows(xs, to * 16, 16), dst_ref=rows(ys, s * 16, 16),
            send_sem=as_sem.at[0], recv_sem=ar_sem.at[0], device_id=(to, t), device_id_type=MESH,
        ).start()
        return carry

    lax.fori_loop(1, N_SEQ, send_rows, 0)
    own_y = pl.ds(pl.multiple_of(s * 16, 16), 16)
    ys[own_y, :] = xs[own_y, :]
    e_on(3, 0)
    w_wait("1a")
    w_wait("1b")
    arrived(ys.at[pl.ds(0, 496)], ar_sem.at[0])
    w_start("2a")
    w_start("2b")
    w_start("1c")
    w_start("2s")

    row_128 = iota((128, 512), 0)
    position = iota((64, 256), 0)
    for q in range(4):
        lanes = slice(256 * q, 256 * q + 256)
        picked = bdot(one_hot((row_128 == row_n) & (((n_1 >> 2) & 3) == q)), ys[...]).astype(BF16)
        for l in range(2):
            is_text = (position.astype(F32) >= visual_rows[l:l + 1, :]) & (position < length[l])
            tok_l[pl.ds(own_tok + 64 * l, 64), lanes] = jnp.where(
                is_text, text[128 * l:128 * l + 64, lanes], picked[64 * l:64 * l + 64, :]
            )
    l_start(0, 0)
    l_start(0, 1)

    loads[4].wait()
    own_rows = jnp.concatenate([tok_l[pl.ds(own_tok, 128), :], tok_e[pl.ds(own_tok, 128), :]], axis=0)
    down_sums = jnp.transpose(bdot(own_rows, down[...])) * tenant_mask
    dl[pl.ds(pl.multiple_of(t * 16, 16), 16), :] = jnp.sum(down_sums.reshape(8, 16, 256), axis=0)

    def send_down(i, carry):
        piece = rows(dl, t * 16, 16)
        pltpu.make_async_remote_copy(
            src_ref=piece, dst_ref=piece, send_sem=ds_sem.at[0], recv_sem=dr_sem.at[0],
            device_id=(s, lax.rem(t + i, N_TP)), device_id_type=MESH,
        ).start()
        return carry


    def collect(tok, top):
        for to, order in ((x_near, NEAR), (x_far, FAR)):
            for n, (by, bx) in enumerate(order):
                at = chip_at(by, bx)
                of_z = pl.ds(pl.multiple_of(at // 2 * 128, 128), 128)
                half = pl.ds(pl.multiple_of(lax.rem(at, 2) * 512, 512), 512)
                to[top:top + 128, 512 * n:512 * n + 512] = tok[of_z, half]

    def project(x, weight, top, size, first, last):
        for n in range(5):
            lanes = slice(256 * n, 256 * n + 256)
            acc[top:top + size, lanes] += bdot(x[top:top + size, first:last], weight[first:last, lanes])

    def add_squares(aheads, tok, top):
        for ahead in aheads:
            of_z = pl.ds(pl.multiple_of(lax.rem(t + ahead + N_TP, N_TP) * 128, 128), 128)
            total = squares[top:top + 128, :]
            for n in range(8):
                part = tok[of_z, 128 * n:128 * n + 128].astype(F32)
                total += part * part
            squares[top:top + 128, :] = total

    acc[...] = jnp.zeros_like(acc)
    squares[...] = jnp.zeros_like(squares)
    l_on(1, 0)
    e_wait(2, 1)
    e_wait(3, 0)
    add_squares(range(8), tok_e, 128)
    collect(tok_e, 128)
    l_on(1, 1)
    add_squares((0, 1, -1), tok_l, 0)
    for name in ("0s", "1s"):
        w_wait(name)
    project(x_near, w_near, 128, 128, 0, 2560)
    l_on(2, 0)
    w_wait("2s")
    project(x_near, w_near, 128, 128, 2560, 4608)
    l_on(2, 1)
    w_wait("2a")
    w_start("3a")
    w_wait("2b")
    w_start("3b")
    w_start("3s")
    add_squares((2, -2), tok_l, 0)
    l_on(3, 0)
    lax.fori_loop(1, N_TP, send_down, 0)
    l_on(3, 1)
    add_squares((3, -3), tok_l, 0)
    w_wait("1c")
    w_start("4s")
    w_wait("3a")
    w_wait("3b")
    w_start("5s")
    l_wait(3, 0)
    add_squares((4,), tok_l, 0)
    collect(tok_l, 0)
    project(x_near, w_near, 0, 128, 0, 4608)
    w_wait("3s")
    w_wait("4s")
    w_wait("5s")
    project(x_far, w_far, 0, 256, 0, 3584)
    arrived(dl.at[pl.ds(0, 112)], dr_sem.at[0])
    down_t = jnp.sum(dl[...].reshape(8, 16, 256), axis=0)
    lora = jnp.transpose(jnp.concatenate([down_t] * 8, axis=0) * tenant_mask).astype(BF16)
    acc[...] += bdot(lora, up_all[...])
    inverse = lax.rsqrt(jnp.sum(squares[...], axis=1, keepdims=True) * (1.0 / DECODER_WIDTH) + EPSILON)

    loads[5].wait()
    loads[6].wait()

    causal = (iota((1024, 128), 0) & 127) >= iota((1024, 128), 1)
    ones = jnp.ones((128, 128), BF16)
    stores = []
    for l in range(2):
        low, high = slice(64 * l, 64 * l + 64), slice(128 + 64 * l, 192 + 64 * l)
        factor = jnp.concatenate([inverse[low, :], inverse[high, :]], axis=0)

        def column(index):
            lanes = slice(128 * index, 128 * index + 128)
            return jnp.concatenate([acc[low, lanes], acc[high, lanes]], axis=0) * factor

        def rotate(values):
            return values * cosine[...] + pltpu.roll(values, 64, 1) * sine[...]

        key_rows = rotate(column(8)).astype(BF16)
        value_rows = jnp.concatenate([column(9).astype(BF16), ones], axis=1)
        kept = iota((128, 128), 0) < length[l]
        queries = jnp.concatenate([rotate(column(j)).astype(BF16) for j in range(QUERY_PER_KEY)], axis=0)
        scores = bdot_nt(queries, key_rows) * (1.0 / math.sqrt(DECODER_HEAD_DIM))
        scores = jnp.where(causal, scores, -1e30)
        exponent = jnp.exp(scores - jnp.max(scores, axis=1, keepdims=True)).astype(BF16)
        summed = bdot(exponent, value_rows)
        ratio = summed[:, :128] / summed[:, 128:]
        for j in range(QUERY_PER_KEY):
            res[128 * l:128 * l + 128, 128 * j:128 * j + 128] = jnp.where(
                kept, ratio[128 * j:128 * j + 128, :], 0.0
            ).astype(BF16)
        stores.append(pltpu.make_async_copy(
            res.at[pl.ds(128 * l, 128)], out.at[pl.ds(128 * l, 128)], load_sem.at[10 + l]
        ))
        stores[l].start()

    for store in stores:
        store.wait()
    g_sent()
    w_sent()
    e_sent()
    l_sent()
    o_sent()
    c_sent()
    arrived(o_all.at[pl.ds(0, 560)], ofs_sem.at[0])
    arrived(xs.at[pl.ds(0, 496)], as_sem.at[0])
    arrived(dl.at[pl.ds(0, 112)], ds_sem.at[0])


def on_device(
    patches, vit_qkv, vit_out, merge_weight, query_key_value_weight, adapter_down, adapter_up_weight,
    text_embed, vis_count, image_session, session_slot, session_tenant, session_len,
):
    operands = (
        session_slot, session_tenant, session_len, vis_count.reshape(8, 128), image_session.reshape(8, 128),
        vit_qkv, vit_out.T, patches.reshape(512, DV), merge_weight,
        jnp.transpose(query_key_value_weight.reshape(256, 10, 128), (1, 0, 2)), adapter_down,
        jnp.transpose(adapter_up_weight.reshape(128, 10, 128), (1, 0, 2)), text_embed,
    ) + tables()
    vmem = pl.BlockSpec(memory_space=pltpu.VMEM)
    smem = pl.BlockSpec(memory_space=pltpu.SMEM)
    hbm = pl.BlockSpec(memory_space=pl.ANY)
    dma = pltpu.SemaphoreType.DMA
    return pl.pallas_call(
        kernel,
        out_shape=jax.ShapeDtypeStruct((256, 1024), BF16),
        in_specs=[smem if i < 3 else vmem if i < 7 else hbm for i in range(len(operands))],
        out_specs=hbm,
        scratch_shapes=[
            pltpu.VMEM((512, 1280), BF16),
            pltpu.VMEM((1024, 128), BF16),
            pltpu.VMEM((256, 1024), BF16),
            pltpu.VMEM((512, 512), BF16),
            pltpu.VMEM((512, 768), BF16),
            pltpu.VMEM((128, 128), F32),
            pltpu.VMEM((128, 128), F32),
            pltpu.VMEM((10, 256, 128), BF16),
            pltpu.VMEM((10, 128, 128), BF16),
            pltpu.VMEM((1536, LANES[0]), BF16),
            pltpu.VMEM((1536, LANES[1]), BF16),
            pltpu.VMEM((320, 640), F32),
            pltpu.VMEM((1280, 640), BF16),
            pltpu.VMEM((512, 1280), BF16),
            pltpu.VMEM((512, 1280), BF16),
            pltpu.VMEM((512, 512), BF16),
            pltpu.VMEM((1280, 1280), BF16),
            pltpu.VMEM((1280, 512), BF16),
            pltpu.VMEM((512, 1280), F32),
            pltpu.VMEM((5120, 1024), BF16),
            pltpu.VMEM((128, 1024), BF16),
            pltpu.VMEM((512, 256), BF16),
            pltpu.VMEM((512, 256), BF16),
            pltpu.VMEM((1024, 1024), BF16),
            pltpu.VMEM((1024, 1024), BF16),
            pltpu.VMEM((128, 256), F32),
            pltpu.VMEM((4608, 1280), BF16),
            pltpu.VMEM((3584, 1280), BF16),
            pltpu.VMEM((256, 5120), BF16),
            pltpu.VMEM((256, 3584), BF16),
            pltpu.VMEM((128, 1280), BF16),
            pltpu.VMEM((256, 1280), F32),
            pltpu.VMEM((256, 128), F32),
            pltpu.VMEM((256, 1024), BF16),
            dma((12,)), dma((2,)), dma((8,)), dma((2,)), dma((2,)), dma((len(W_GROUPS),)), dma((len(W_GROUPS),)),
            dma((1,)), dma((8,)), dma((1,)), dma((4,)),
            dma((1,)), dma((8,)), dma((1,)), dma((8,)), dma((1,)), dma((8,)),
            dma((1,)), dma((1,)), dma((1,)), dma((1,)),
        ],
        compiler_params=pltpu.CompilerParams(
            collective_id=0, has_side_effects=True, vmem_limit_bytes=64 * 1024 * 1024
        ),
    )(*operands).astype(F32)


def solution(mesh):
    placed = (
        P("seq", None, None),
        P(None, "seq", "tp"),
        P("tp", "seq"),
        P(None, "tp"),
        P("seq", "tp", None, None),
        P("tp", None),
        P(None, "tp", None, None),
        P("seq", "tp"),
        P(),
        P(),
        P(),
        P(),
        P(),
    )
    return jax.shard_map(
        on_device, mesh=mesh, in_specs=placed, out_specs=P("seq", "tp"), check_vma=False
    )
```
